256 devices in a mesh: context: 32 (over x, y, z_lo), tensor: 8 (over z_hi, core).
Axes of the slice: x: 4, y: 4, z: 8 (z_hi: 4, z_lo: 2; z = z_hi * 2 + z_lo), core: 2. Of those that a mesh axis runs over, the one named last changes fastest.
Arguments:
- query_proj: bfloat16 [16384, 4096], P('context', 'tensor'), may hold values from -6 to 6
- key_proj: bfloat16 [16384, 4096], P('context', 'tensor'), may hold values from -6 to 6
- value_proj: bfloat16 [16384, 4096], P('context', 'tensor'), may hold values from -6 to 6
- filter_gains: float32 [4096, 16], P('tensor'), may hold values from -3 to 3
- log_rates: float32 [4096, 16], P('tensor'), may hold values from -12 to -0.5
- out_weight: bfloat16 [4096, 4096], P('tensor', 'context'), may hold values from -0.09375 to 0.09375
- grad_out: bfloat16 [16384, 4096], P('context', 'tensor'), may hold values from -6 to 6
Outputs:
- grad_query: bfloat16 [16384, 4096], P('context', 'tensor')
- grad_key: bfloat16 [16384, 4096], P('context', 'tensor')
- grad_value: bfloat16 [16384, 4096], P('context', 'tensor')
- grad_gains: float32 [4096, 16], P('tensor')
- grad_log_rates: float32 [4096, 16], P('tensor')
- grad_out_weight: float32 [4096, 4096], P('tensor', 'context')
The draws below stay inside these ranges and needn't reach their ends.
All inputs are finite; a program needn't handle non-finite values.
Results may differ from the reference program's by a relative error of at most 0.03.
Values may be sent and summed in bfloat16 or wider, within the bound.
A program may use at most 128 MiB of HBM per device.

```python
import math
import jax
import jax.numpy as jnp
from jax import lax

ROWS = 512
CHANNELS = 4096
OUT_WIDTH = 4096
MODES = 16
FFT_BLOCK = 1024
LENGTH = 16384
FFT_LEN = 32768
FFT_INNER = 32
N_CONTEXT = 32


def draw_log_rates(key, part):
    key = jax.random.fold_in(key, 11)
    pick_key, slow_key, fast_key = jax.random.split(key, 3)
    slow_share = 0.5
    slow_rates = jax.random.uniform(slow_key, (CHANNELS, MODES), jnp.float32, -12.0, -9.0)
    fast_rates = jax.random.uniform(fast_key, (CHANNELS, MODES), jnp.float32, -9.0, -0.5)
    chooser = jax.random.uniform(pick_key, (CHANNELS, MODES), jnp.float32) < slow_share
    return jnp.where(chooser, slow_rates, fast_rates)


def strengthened(drawn, own_key, source, target, blocks, factor):
    owner, partner = [(jnp.arange(drawn.shape[position]) // (drawn.shape[position] // blocks)).reshape([-1 if axis == position else 1 for axis in range(drawn.ndim)]) for position in (source, target)]
    chosen = jax.random.permutation(own_key, blocks)[partner]
    strong = (owner == chosen) | (owner == (partner + blocks // 2) % blocks)
    return jnp.where(strong, factor * drawn, drawn)


def levels(key, extent, cuts, least, high):
    factor_of, own = 1.0, jax.random.fold_in(key, 6)
    for position, parts in cuts:
        steps = jnp.exp(jax.random.uniform(jax.random.fold_in(own, position), (parts,), jnp.float32, least / len(cuts), high / len(cuts)))
        factor_of = factor_of * jnp.repeat(steps, extent[position] // parts).reshape([-1 if axis == position else 1 for axis in range(len(extent))])
    return factor_of


def noise(stream_key, extent, deviation, bound, pieces=(), kind=jnp.bfloat16):
    level = levels(stream_key, extent, pieces, -0.22, 0.18) if pieces else 1.0
    drawn = jax.random.normal(stream_key, extent, jnp.float32) * deviation * level
    return jnp.minimum(jnp.maximum(drawn, -bound), bound).astype(kind)


def bell_draw_with(own_key, shape, deviation, most, cuts, heavy, kind=jnp.bfloat16):
    entries = deviation * jax.random.normal(own_key, shape, jnp.float32)
    if cuts:
        entries = entries * levels(own_key, shape, cuts, -0.22, 0.18)
    return jnp.clip(strengthened(entries, jax.random.fold_in(own_key, 3), *heavy), -most, most).astype(kind)


def setup_inputs(seed: int = 0) -> dict:
    splits = jax.random.split(jax.random.key(seed), 8)
    return {
        "query_proj": noise(splits[0], (LENGTH, CHANNELS), 1.0, 6.0, ((0, 32), (1, 8))),
        "key_proj": noise(splits[1], (LENGTH, CHANNELS), 1.0, 6.0, ((0, 32), (1, 8))),
        "value_proj": noise(splits[2], (LENGTH, CHANNELS), 1.0, 6.0, ((0, 32), (1, 8))),
        "filter_gains": noise(splits[3], (CHANNELS, MODES), 0.5, 3.0, ((0, 8),), jnp.float32),
        "log_rates": draw_log_rates(jax.random.fold_in(splits[7], 71), 0),
        "out_weight": noise(splits[5], (CHANNELS, OUT_WIDTH), OUT_WIDTH ** -0.5, 0.09375, ((0, 8), (1, 32))),
        "grad_out": bell_draw_with(splits[6], (LENGTH, OUT_WIDTH), 1.0, 6.0, ((0, 32), (1, 8)), (0, 1, 32, 2.75)),
    }


TWO_PI = 2.0 * math.pi

def index_range(length):
    return jnp.arange(length, dtype=jnp.int32)

def angle_grid(first_vals, second_vals, period):
    product = first_vals[:, None] * second_vals[None, :] % period
    return product.astype(jnp.float32) * (TWO_PI / period)

def complex_times(left_spec, right_spec):
    left_re = left_spec[0].astype(jnp.float32)
    left_im = left_spec[1].astype(jnp.float32)
    right_re = right_spec[0].astype(jnp.float32)
    right_im = right_spec[1].astype(jnp.float32)
    real_part = left_re * right_re - left_im * right_im
    imag_part = left_re * right_im + left_im * right_re
    return jnp.stack([real_part, imag_part]).astype(jnp.bfloat16)

def conj_times(left_spec, right_spec):
    left_re = left_spec[0].astype(jnp.float32)
    left_im = left_spec[1].astype(jnp.float32)
    right_re = right_spec[0].astype(jnp.float32)
    right_im = right_spec[1].astype(jnp.float32)
    real_part = left_re * right_re + left_im * right_im
    imag_part = left_re * right_im - left_im * right_re
    return jnp.stack([real_part, imag_part]).astype(jnp.bfloat16)

def forward_signal(signal, front_rows, inner_fwd, turn_cos, turn_sin):
    chan_count = signal.shape[1]
    flat_grid = signal.reshape(FFT_BLOCK // 2, FFT_INNER * chan_count)
    mixed_rows = jnp.dot(front_rows, flat_grid, preferred_element_type=jnp.float32)
    mixed_rows = mixed_rows.reshape(2, FFT_BLOCK, FFT_INNER, chan_count)
    real_part = mixed_rows[0] * turn_cos[:, :, None] + mixed_rows[1] * turn_sin[:, :, None]
    imag_part = mixed_rows[1] * turn_cos[:, :, None] - mixed_rows[0] * turn_sin[:, :, None]
    turned = jnp.stack([real_part, imag_part]).astype(jnp.bfloat16)
    spectrum = jnp.einsum('xykn,yanc->xakc', inner_fwd.astype(jnp.float32), turned.astype(jnp.float32), precision=lax.Precision.HIGHEST)
    return spectrum.astype(jnp.bfloat16)

def inverse_signal(spectrum, inner_back, end_rows, turn_cos, turn_sin):
    chan_count = spectrum.shape[-1]
    summed = jnp.einsum('xynk,yakc->xanc', inner_back.astype(jnp.float32), spectrum.astype(jnp.float32), precision=lax.Precision.HIGHEST)
    real_part = summed[0] * turn_cos[:, :, None] - summed[1] * turn_sin[:, :, None]
    imag_part = summed[1] * turn_cos[:, :, None] + summed[0] * turn_sin[:, :, None]
    turned = jnp.stack([real_part, imag_part]).astype(jnp.bfloat16)
    flat_grid = turned.reshape(2 * FFT_BLOCK, FFT_INNER * chan_count)
    values = jnp.dot(end_rows, flat_grid, preferred_element_type=jnp.float32) * (1.0 / FFT_LEN)
    return values.reshape(LENGTH, chan_count).astype(jnp.bfloat16)

def filter_spectrum(gains_block, rates_block):
    chan_count = gains_block.shape[0]
    time_vals = index_range(LENGTH).astype(jnp.float32)
    decay_rates = jnp.exp(rates_block)
    mode_amps = gains_block * jnp.sqrt(2.0 * decay_rates)
    filter_vals = lax.optimization_barrier(jnp.sum(mode_amps[None] * jnp.exp(-decay_rates[None] * time_vals[:, None, None]), axis=2))
    padded = jnp.concatenate([filter_vals, jnp.zeros((LENGTH, chan_count), jnp.float32)], axis=0)
    spectrum = jnp.fft.fft(padded, axis=0)
    spectrum = jnp.transpose(spectrum.reshape(FFT_INNER, FFT_BLOCK, chan_count), (1, 0, 2))
    return jnp.stack([jnp.real(spectrum), jnp.imag(spectrum)]).astype(jnp.float32)

def reference(query_proj, key_proj, value_proj, filter_gains, log_rates, out_weight, grad_out):
    chan_total = query_proj.shape[1]
    block_width = min(128, chan_total)
    block_total = chan_total // block_width
    front_angles = angle_grid(index_range(FFT_BLOCK), index_range(FFT_BLOCK // 2), FFT_BLOCK)
    front_rows = jnp.concatenate([jnp.cos(front_angles), -jnp.sin(front_angles)], axis=0).astype(jnp.bfloat16)
    inner_angles = angle_grid(index_range(FFT_INNER), index_range(FFT_INNER), FFT_INNER)
    inner_cos = jnp.cos(inner_angles)
    inner_sin = jnp.sin(inner_angles)
    inner_fwd = jnp.stack([jnp.stack([inner_cos, inner_sin]), jnp.stack([-inner_sin, inner_cos])]).astype(jnp.bfloat16)
    inner_back = jnp.stack([jnp.stack([inner_cos, -inner_sin]), jnp.stack([inner_sin, inner_cos])]).astype(jnp.bfloat16)
    end_angles = angle_grid(index_range(FFT_BLOCK // 2), index_range(FFT_BLOCK), FFT_BLOCK)
    end_rows = jnp.concatenate([jnp.cos(end_angles), -jnp.sin(end_angles)], axis=1).astype(jnp.bfloat16)
    turn_angles = angle_grid(index_range(FFT_BLOCK), index_range(FFT_INNER), FFT_LEN)
    turn_cos = jnp.cos(turn_angles)
    turn_sin = jnp.sin(turn_angles)
    norm_scale = 1.0 / math.sqrt(LENGTH)
    time_vals = index_range(LENGTH).astype(jnp.float32)
    out_parts = grad_out.reshape(N_CONTEXT, ROWS, OUT_WIDTH).astype(jnp.float32)

    def split_channels(full_array):
        return jnp.transpose(full_array.reshape(LENGTH, block_total, block_width), (1, 0, 2))

    def split_rows(full_array):
        return full_array.reshape(block_total, block_width, full_array.shape[1])

    def one_block(inputs):
        query_blk, key_blk, value_blk, gains_blk, rates_blk, weight_blk = inputs
        filter_spec = filter_spectrum(gains_blk, rates_blk)
        signal = (key_blk.astype(jnp.float32) * value_blk.astype(jnp.float32)).astype(jnp.bfloat16)
        signal_spec = forward_signal(signal, front_rows, inner_fwd, turn_cos, turn_sin)
        conv_out = inverse_signal(complex_times(filter_spec, signal_spec), inner_back, end_rows, turn_cos, turn_sin)
        gate_grad = jnp.dot(grad_out, weight_blk.T, preferred_element_type=jnp.float32)
        gated_out = (query_blk.astype(jnp.float32) * conv_out.astype(jnp.float32)).astype(jnp.bfloat16)
        grad_query = (gate_grad * conv_out.astype(jnp.float32)).astype(jnp.bfloat16)
        conv_grad = (gate_grad * query_blk.astype(jnp.float32)).astype(jnp.bfloat16)
        gated_parts = gated_out.reshape(N_CONTEXT, ROWS, block_width).astype(jnp.float32)
        partial_value = jnp.einsum('prc,prd->pcd', gated_parts, out_parts, precision=lax.Precision.HIGHEST)
        partial_value = lax.optimization_barrier(partial_value.astype(jnp.bfloat16)).astype(jnp.float32)
        grad_weight = lax.optimization_barrier(jnp.sum(partial_value, axis=0)) * norm_scale
        conv_grad_spec = forward_signal(conv_grad, front_rows, inner_fwd, turn_cos, turn_sin)
        input_grad = inverse_signal(conj_times(filter_spec, conv_grad_spec), inner_back, end_rows, turn_cos, turn_sin)
        filter_grad = inverse_signal(conj_times(signal_spec, conv_grad_spec), inner_back, end_rows, turn_cos, turn_sin)
        grad_key = (input_grad.astype(jnp.float32) * value_blk.astype(jnp.float32)).astype(jnp.bfloat16)
        grad_value = (input_grad.astype(jnp.float32) * key_blk.astype(jnp.float32)).astype(jnp.bfloat16)
        decay_rates = jnp.exp(rates_blk)
        mode_basis = jnp.sqrt(2.0 * decay_rates)[None] * jnp.exp(-decay_rates[None] * time_vals[:, None, None])
        weighted = filter_grad.astype(jnp.float32)[:, :, None] * mode_basis
        grad_gains = lax.optimization_barrier(jnp.sum(weighted, axis=0)) * norm_scale
        rate_terms = weighted * (0.5 - decay_rates[None] * time_vals[:, None, None])
        grad_rates = lax.optimization_barrier(jnp.sum(rate_terms, axis=0)) * gains_blk * norm_scale
        return (grad_query, grad_key, grad_value, grad_gains, grad_rates, grad_weight)
    results = lax.map(one_block, (split_channels(query_proj), split_channels(key_proj), split_channels(value_proj), split_rows(filter_gains), split_rows(log_rates), split_rows(out_weight)))

    def join_channels(stacked):
        return jnp.transpose(stacked, (1, 0, 2)).reshape(LENGTH, chan_total)

    def join_rows(stacked):
        return stacked.reshape(chan_total, stacked.shape[2])
    return (join_channels(results[0]), join_channels(results[1]), join_channels(results[2]), join_rows(results[3]), join_rows(results[4]), join_rows(results[5]))
```

```python
import math

import jax
import jax.numpy as jnp
from jax import lax
from jax.experimental import pallas as pl
from jax.experimental.pallas import tpu as pltpu
from jax.sharding import PartitionSpec as P

BF16 = jnp.bfloat16
F32 = jnp.float32
MESH = pl.DeviceIdType.MESH

NCTX = 32
ROWS = 512
CH = 512
MODES = 16
SUB = 8
STEPS = ROWS // SUB
LANES = 128
GROUPS = CH // LANES
SEQ = ROWS * NCTX
NORM = 1.0 / math.sqrt(SEQ)

N_A = 11
N_W = 17
N_O = 25
OFF_W = N_A
OFF_O = OFF_W + N_W
N_RING = OFF_O + N_O


def shift_sub(val, step):
    rolled = pltpu.roll(val, step % SUB, 1)
    ids = lax.broadcasted_iota(jnp.int32, val.shape, 1)
    keep = ids >= step if step > 0 else ids < SUB + step
    return jnp.where(keep, rolled, 0.0)


def kernel(
    q_ref, k_ref, v_ref, gain2, rate2, gain3, rate3, w_ref, go_ref,
    gq_out, gk_out, gv_out, yz_out, ow_out,
    ag, wg, op, xs, gs, ys, perm, perm_t, a8, amp8, ebuf, eall, qbuf, qall, hd3, st2,
    scr8, hfwd, hbwd, tend, gate, cv, gt, yz, yz_in, yz_all,
    opp_y0, fin_y0, opp_x0, fin_x0, opp_x1, fin_x1, opp_y1, fin_y1,
    v0, v1, rsum, rsend, zin,
    ring_s, ring_r, e_s, e_r, q_s, q_r, y_s, y_r, o_s, o_r, loc,
):
    c = lax.axis_index("context")
    t = lax.axis_index("tensor")
    x = c // 8
    y = (c // 2) % 4
    zl = c % 2
    zh = t // 2
    core = t % 2

    def ctx_of(xx, yy, zz):
        return xx * 8 + yy * 2 + zz

    x_right = ctx_of((x + 1) % 4, y, zl)
    x_left = ctx_of((x + 3) % 4, y, zl)
    y_right = ctx_of(x, (y + 1) % 4, zl)
    y_left = ctx_of(x, (y + 3) % 4, zl)
    z_peer = ctx_of(x, y, 1 - zl)
    partner = zh * 2 + (1 - core)
    t_right = ((zh + 1) % 4) * 2 + core
    t_left = ((zh + 3) % 4) * 2 + core
    t_opp = ((zh + 2) % 4) * 2 + core

    pending = []

    def remote(index, src, dst, ctx, ten):
        copy = pltpu.make_async_remote_copy(
            src_ref=src, dst_ref=dst, send_sem=ring_s.at[index], recv_sem=ring_r.at[index],
            device_id=(ctx, ten), device_id_type=MESH,
        )
        copy.start()
        pending.append(copy)
        return copy

    barrier = pltpu.get_barrier_semaphore()

    def greet(d, _):
        pl.semaphore_signal(barrier, inc=1, device_id=((c + d) % NCTX, t), device_id_type=MESH)
        return 0

    lax.fori_loop(1, NCTX, greet, 0)
    for ten in (partner, t_right, t_left):
        pl.semaphore_signal(barrier, inc=1, device_id=(c, ten), device_id_type=MESH)
    pl.semaphore_wait(barrier, NCTX - 1 + 3)

    lo, hi = pl.ds(0, 256), pl.ds(256, 256)
    wz = remote(
        OFF_W, w_ref, wg.at[x, y, :, pl.ds(pl.multiple_of(zl * 128, 128), 128)], z_peer, t
    )
    a_r0 = remote(0, go_ref.at[lo], ag.at[t, lo], c, t_right)
    a_l1 = remote(1, go_ref.at[hi], ag.at[t, hi], c, t_left)
    a_r1 = remote(2, go_ref.at[hi], ag.at[t, hi], c, t_right)
    a_l0 = remote(3, go_ref.at[lo], ag.at[t, lo], c, t_left)
    a_p = remote(4, go_ref, ag.at[t], c, partner)
    own_a = pltpu.make_async_copy(go_ref, ag.at[t], loc.at[0])
    own_w = pltpu.make_async_copy(
        w_ref, wg.at[x, y, :, pl.ds(pl.multiple_of(zl * 128, 128), 128)], loc.at[1]
    )
    own_a.start()
    own_w.start()

    rate_wide = jnp.exp(rate3[...])
    a8[...] = jnp.broadcast_to(jnp.exp(-rate_wide), a8.shape)
    amp8[...] = jnp.broadcast_to(gain3[...] * jnp.sqrt(2.0 * rate_wide), amp8.shape)
    row_id = lax.broadcasted_iota(jnp.int32, (ROWS, ROWS), 0)
    col_id = lax.broadcasted_iota(jnp.int32, (ROWS, ROWS), 1)
    perm[...] = jnp.where(col_id == STEPS * (row_id % SUB) + row_id // SUB, 1.0, 0.0).astype(BF16)
    perm_t[...] = jnp.where(row_id == STEPS * (col_id % SUB) + col_id // SUB, 1.0, 0.0).astype(BF16)

    def spread(dst, natural):
        mixed = jnp.dot(perm[...], natural, preferred_element_type=F32)
        for grp in range(GROUPS):
            dst[grp] = mixed[:, grp * LANES:(grp + 1) * LANES]

    def gather_back():
        mixed = jnp.concatenate([ys[grp] for grp in range(GROUPS)], axis=1).astype(BF16)
        return jnp.dot(perm_t[...], mixed, preferred_element_type=F32)

    signal = (k_ref[...].astype(F32) * v_ref[...].astype(F32)).astype(BF16)
    spread(xs, signal)

    def lane_at(grp):
        return pl.ds(pl.multiple_of(grp * LANES, LANES), LANES)

    def step_rows(j):
        return pl.ds(pl.multiple_of(j * SUB, SUB), SUB)

    def rates_at(grp):
        return jnp.exp(rate3[:, :, lane_at(grp)])

    UNROLL = 4

    def end_states(src, backward, hsub):
        def group(grp, _):
            decay = a8[:, :, lane_at(grp)]

            def step(i, state):
                for u in range(UNROLL):
                    j = i * UNROLL + u
                    j = STEPS - 1 - j if backward else j
                    state = decay * state + src[grp, step_rows(j)][None]
                return state

            state = lax.fori_loop(
                0, STEPS // UNROLL, step, jnp.zeros((MODES, SUB, LANES), F32)
            )
            rates = rates_at(grp)
            sign = -1 if backward else 1
            for power in (1, 2, 4):
                factor = jnp.exp(-rates * float(STEPS * power))
                state = state + factor * shift_sub(state, sign * power)
            hsub[:, :, lane_at(grp)] = shift_sub(state, sign)
            scr8[grp, 0:MODES] = state
            return 0

        lax.fori_loop(0, GROUPS, group, 0)
        edge = 0 if backward else SUB - 1
        for grp in range(GROUPS):
            for m in range(MODES):
                st2[m:m + 1, grp * LANES:(grp + 1) * LANES] = scr8[grp, m, edge:edge + 1, :]

    def add_incoming(state, backward, hsub):
        for m in range(MODES):
            hd3[m] = state[m:m + 1, :]

        def group(grp, _):
            ids = lax.broadcasted_iota(jnp.int32, (MODES, SUB, LANES), 1).astype(F32)
            ids = (SUB - 1.0) - ids if backward else ids
            weight = jnp.exp(-rates_at(grp) * (ids * float(STEPS)))
            hsub[:, :, lane_at(grp)] += weight * hd3[:, :, lane_at(grp)]
            return 0

        lax.fori_loop(0, GROUPS, group, 0)

    end_states(xs, False, hfwd)
    ebuf[...] = st2[...].astype(BF16)

    def e_copy(d, index):
        other = (c + d) % NCTX
        return pltpu.make_async_remote_copy(
            src_ref=ebuf, dst_ref=eall.at[index], send_sem=e_s.at[other], recv_sem=e_r.at[index],
            device_id=(other, t), device_id_type=MESH,
        )

    def q_copy(d, index):
        other = (c + d) % NCTX
        return pltpu.make_async_remote_copy(
            src_ref=qbuf, dst_ref=qall.at[index], send_sem=q_s.at[other], recv_sem=q_r.at[index],
            device_id=(other, t), device_id_type=MESH,
        )

    def run(first, last, fun):
        def body(i, carry):
            fun(i)
            return carry

        lax.fori_loop(first, last, body, 0)

    run(1, NCTX - c, lambda d: e_copy(d, c).start())

    own_w.wait()
    wz.wait_recv()
    w0, w1 = pl.ds(0, 256), pl.ds(256, 256)
    w0a, w0b, w1a, w1b = pl.ds(0, 128), pl.ds(128, 128), pl.ds(256, 128), pl.ds(384, 128)
    i = OFF_W + 1
    s_xr = remote(i + 0, wg.at[x, y, w0], wg.at[x, y, w0], x_right, t)
    s_xl = remote(i + 1, wg.at[x, y, w0], wg.at[x, y, w0], x_left, t)
    s_yr = remote(i + 2, wg.at[x, y, w1], wg.at[x, y, w1], y_right, t)
    s_yl = remote(i + 3, wg.at[x, y, w1], wg.at[x, y, w1], y_left, t)
    xm, xp, ym, yp = (x + 3) % 4, (x + 1) % 4, (y + 3) % 4, (y + 1) % 4
    s_xr.wait_recv()
    f_xr = remote(i + 4, wg.at[xm, y, w0a], wg.at[xm, y, w0a], x_right, t)
    s_yr.wait_recv()
    f_yr = remote(i + 6, wg.at[x, ym, w1a], wg.at[x, ym, w1a], y_right, t)
    s_xl.wait_recv()
    f_xl = remote(i + 5, wg.at[xp, y, w0b], wg.at[xp, y, w0b], x_left, t)
    s_yl.wait_recv()
    f_yl = remote(i + 7, wg.at[x, yp, w1b], wg.at[x, yp, w1b], y_left, t)
    f_xr.wait_recv()
    f_xl.wait_recv()
    g_yr = remote(i + 8, wg.at[:, y, w0], wg.at[:, y, w0], y_right, t)
    g_yl = remote(i + 9, wg.at[:, y, w0], wg.at[:, y, w0], y_left, t)
    f_yr.wait_recv()
    f_yl.wait_recv()
    g_xr = remote(i + 10, wg.at[x, :, w1], wg.at[x, :, w1], x_right, t)
    g_xl = remote(i + 11, wg.at[x, :, w1], wg.at[x, :, w1], x_left, t)

    run(0, c, lambda j: e_copy(j - c + NCTX, j).wait_recv())
    chunk_decay = jnp.exp(-jnp.exp(rate2[...]) * float(ROWS))
    head = lax.fori_loop(
        0, c, lambda j, h: chunk_decay * h + eall[j].astype(F32), jnp.zeros((MODES, CH), F32)
    )
    add_incoming(head, False, hfwd)

    def scan_out(src, backward, hsub):
        def group(grp, _):
            decay = a8[:, :, lane_at(grp)]
            amp = amp8[:, :, lane_at(grp)]

            def step(i, state):
                for u in range(UNROLL):
                    j = i * UNROLL + u
                    j = STEPS - 1 - j if backward else j
                    state = decay * state + src[grp, step_rows(j)][None]
                    ys[grp, step_rows(j)] = jnp.sum(amp * state, axis=0)
                return state

            lax.fori_loop(0, STEPS // UNROLL, step, hsub[:, :, lane_at(grp)])
            return 0

        lax.fori_loop(0, GROUPS, group, 0)

    scan_out(xs, False, hfwd)
    cv[...] = gather_back().astype(BF16)
    gated = (q_ref[...].astype(F32) * cv[...].astype(F32)).astype(BF16).astype(F32)
    gt[...] = jnp.transpose(gated).astype(BF16)

    tl, tr, to = t_left, t_right, t_opp
    a_r0.wait_recv()
    f_r = remote(5, ag.at[tl, lo], ag.at[tl, lo], c, t_right)
    a_l1.wait_recv()
    f_l = remote(6, ag.at[tr, hi], ag.at[tr, hi], c, t_left)
    a_r1.wait_recv()
    p_l = remote(7, ag.at[tl], ag.at[tl], c, partner)
    a_l0.wait_recv()
    p_r = remote(8, ag.at[tr], ag.at[tr], c, partner)

    g_yr.wait_recv()
    h_yr = remote(i + 12, wg.at[:, ym, w0a], wg.at[:, ym, w0a], y_right, t)
    g_xr.wait_recv()
    h_xr = remote(i + 14, wg.at[xm, :, w1a], wg.at[xm, :, w1a], x_right, t)
    g_yl.wait_recv()
    h_yl = remote(i + 13, wg.at[:, yp, w0b], wg.at[:, yp, w0b], y_left, t)
    g_xl.wait_recv()
    h_xl = remote(i + 15, wg.at[xp, :, w1b], wg.at[xp, :, w1b], x_left, t)

    f_r.wait_recv()
    p_a = remote(9, ag.at[to, lo], ag.at[to, lo], c, partner)
    f_l.wait_recv()
    p_b = remote(10, ag.at[to, hi], ag.at[to, hi], c, partner)
    own_a.wait()
    a_p.wait_recv()
    p_l.wait_recv()
    p_r.wait_recv()
    p_a.wait_recv()
    p_b.wait_recv()

    def out_block(j):
        half = pl.ds(pl.multiple_of((j % 2) * 256, 256), 256)
        op[j // 4, j % 4] = jnp.dot(
            gt[...], ag[j // 2, :, half], preferred_element_type=F32
        ).astype(BF16)

    run(0, 16, out_block)

    def send_ring(base, unit, opp, fin, pos, right, left):
        far, nxt, prv = (pos + 2) % 4, (pos + 1) % 4, (pos + 3) % 4
        o_r_ = remote(base + 0, unit(far, 0), opp.at[0], right, t)
        o_l_ = remote(base + 1, unit(far, 1), opp.at[1], left, t)
        d_r = remote(base + 2, unit(nxt, 1), fin.at[0, 1], right, t)
        d_l = remote(base + 3, unit(prv, 0), fin.at[1, 0], left, t)
        return (base, unit, opp, fin, nxt, prv, right, left, o_r_, o_l_, d_r, d_l)

    def add_ring(ring):
        base, unit, opp, fin, nxt, prv, right, left, o_r_, o_l_, d_r, d_l = ring
        o_r_.wait_recv()
        ref = unit(nxt, 0)
        ref[...] = (ref[...].astype(F32) + opp[0].astype(F32)).astype(BF16)
        e_r_ = remote(base + 4, ref, fin.at[0, 0], right, t)
        o_l_.wait_recv()
        ref = unit(prv, 1)
        ref[...] = (ref[...].astype(F32) + opp[1].astype(F32)).astype(BF16)
        e_l_ = remote(base + 5, ref, fin.at[1, 1], left, t)
        return (d_r, d_l, e_r_, e_l_)

    def ring_sum(unit, fin, pos, waits, part):
        return (
            unit(pos, part)[...].astype(F32) + fin[0, part].astype(F32) + fin[1, part].astype(F32)
        )

    def unit_y0(target, part):
        return op.at[:, target, pl.ds(part * 128, 128)]

    def unit_x1(target, part):
        return op.at[target, :, pl.ds(256 + part * 128, 128)]

    def unit_x0(target, part):
        return v0.at[target, pl.ds(part * 128, 128)]

    def unit_y1(target, part):
        return v1.at[target, pl.ds(part * 128, 128)]

    ring_a = send_ring(OFF_O, unit_y0, opp_y0, fin_y0, y, y_right, y_left)
    ring_b = send_ring(OFF_O + 6, unit_x1, opp_x1, fin_x1, x, x_right, x_left)

    h_yr.wait_recv()
    h_yl.wait_recv()
    h_xr.wait_recv()
    h_xl.wait_recv()
    gate[...] = jnp.zeros_like(gate)
    dims = (((1,), (1,)), ((), ()))

    def gate_block(j):
        rows = ag.at[j]
        gate[...] += lax.dot_general(
            rows[:, 0:256], wg[j // 2, (j % 2) * 2], dims, preferred_element_type=F32
        ) + lax.dot_general(
            rows[:, 256:512], wg[j // 2, (j % 2) * 2 + 1], dims, preferred_element_type=F32
        )

    run(0, 8, gate_block)
    gq_out[...] = (gate[...] * cv[...].astype(F32)).astype(BF16)
    conv_grad = (gate[...] * q_ref[...].astype(F32)).astype(BF16)
    spread(gs, conv_grad)

    def gain_scan(grp, _):
        for part in range(2):
            mode = pl.ds(part * 8, 8)
            decay = a8[mode, :, lane_at(grp)]

            def step(i, carry):
                state, timed, gain_sum, rate_sum = carry
                for u in range(UNROLL):
                    rows = step_rows(i * UNROLL + u)
                    grad = gs[grp, rows][None]
                    decayed = decay * state
                    timed = decay * timed + decayed
                    state = decayed + xs[grp, rows][None]
                    gain_sum = gain_sum + grad * state
                    rate_sum = rate_sum + grad * timed
                return (state, timed, gain_sum, rate_sum)

            zero = jnp.zeros((8, SUB, LANES), F32)
            _, timed, gain_sum, rate_sum = lax.fori_loop(
                0, STEPS // UNROLL, step, (hfwd[mode, :, lane_at(grp)], zero, zero, zero)
            )
            tend[mode, :, lane_at(grp)] = timed
            scr8[grp, mode] = gain_sum
            scr8[grp, pl.ds(MODES + part * 8, 8)] = rate_sum
        return 0

    end_states(gs, True, hbwd)
    qbuf[...] = st2[...].astype(BF16)
    run(NCTX - c, NCTX, lambda d: q_copy(d, c).start())

    waits_a = add_ring(ring_a)
    waits_b = add_ring(ring_b)
    lax.fori_loop(0, GROUPS, gain_scan, 0)
    for grp in range(GROUPS):
        yz[0:MODES, grp] = jnp.sum(scr8[grp, 0:MODES], axis=1)
        yz[MODES:2 * MODES, grp] = jnp.sum(scr8[grp, MODES:2 * MODES], axis=1)

    for copy in waits_a:
        copy.wait_recv()
    for part in range(2):
        total = ring_sum(unit_y0, fin_y0, y, None, part)
        v0[:, part * 128:(part + 1) * 128] = total.astype(BF16)
    ring_c = send_ring(OFF_O + 12, unit_x0, opp_x0, fin_x0, x, x_right, x_left)
    for copy in waits_b:
        copy.wait_recv()
    for part in range(2):
        total = ring_sum(unit_x1, fin_x1, x, None, part)
        v1[:, part * 128:(part + 1) * 128] = total.astype(BF16)
    ring_d = send_ring(OFF_O + 18, unit_y1, opp_y1, fin_y1, y, y_right, y_left)

    run(c + 1, NCTX, lambda j: q_copy(j - c, j).wait_recv())
    tail = lax.fori_loop(
        0, NCTX - 1 - c,
        lambda j, h: chunk_decay * h + qall[NCTX - 1 - j].astype(F32),
        jnp.zeros((MODES, CH), F32),
    )
    add_incoming(tail, True, hbwd)
    for grp in range(GROUPS):
        lanes = slice(grp * LANES, (grp + 1) * LANES)
        cross = jnp.sum(tend[:, :, lanes] * a8[:, :, lanes] * hbwd[:, :, lanes], axis=1)
        yz[MODES:2 * MODES, grp] += cross

    def y_copy(d, index):
        other = (c + d) % NCTX
        return pltpu.make_async_remote_copy(
            src_ref=yz.at[other], dst_ref=yz_in.at[index], send_sem=y_s.at[other],
            recv_sem=y_r.at[index], device_id=(other, t), device_id_type=MESH,
        )

    run(1, NCTX, lambda d: y_copy(d, c).start())

    waits_c = add_ring(ring_c)
    waits_d = add_ring(ring_d)

    scan_out(gs, True, hbwd)
    input_grad = gather_back().astype(BF16).astype(F32)
    gk_out[...] = (input_grad * v_ref[...].astype(F32)).astype(BF16)
    gv_out[...] = (input_grad * k_ref[...].astype(F32)).astype(BF16)

    for copy in waits_c:
        copy.wait_recv()
    for part in range(2):
        rsum[part * 128:(part + 1) * 128] = ring_sum(unit_x0, fin_x0, x, None, part)
    for copy in waits_d:
        copy.wait_recv()
    for part in range(2):
        rsum[256 + part * 128:256 + (part + 1) * 128] = ring_sum(unit_y1, fin_y1, y, None, part)
    rsend[...] = rsum[:, pl.ds(pl.multiple_of((1 - zl) * 128, 128), 128)].astype(BF16)
    z_copy = remote(OFF_O + 24, rsend, zin, z_peer, t)

    run(1, NCTX, lambda d: y_copy(d, (c + d) % NCTX).wait_recv())
    yz_in[c] = yz[c]
    yz_all[c] = jnp.sum(yz_in[...], axis=0)

    def o_copy(d, index):
        other = (c + d) % NCTX
        return pltpu.make_async_remote_copy(
            src_ref=yz_all.at[c], dst_ref=yz_all.at[index], send_sem=o_s.at[other],
            recv_sem=o_r.at[index], device_id=(other, t), device_id_type=MESH,
        )

    run(1, NCTX, lambda d: o_copy(d, c).start())

    z_copy.wait_recv()
    ow_out[...] = (
        rsum[:, pl.ds(pl.multiple_of(zl * 128, 128), 128)] + zin[...].astype(F32)
    ) * NORM

    run(1, NCTX, lambda d: o_copy(d, (c + d) % NCTX).wait_recv())
    yz_out[...] = yz_all[...]
    run(1, NCTX - c, lambda d: e_copy(d, c).wait_send())
    run(NCTX - c, NCTX, lambda d: q_copy(d, c).wait_send())
    run(1, NCTX, lambda d: y_copy(d, c).wait_send())
    run(1, NCTX, lambda d: o_copy(d, c).wait_send())
    for copy in pending:
        copy.wait_send()


def on_device(query_proj, key_proj, value_proj, filter_gains, log_rates, out_weight, grad_out):
    gain2 = filter_gains.T
    rate2 = log_rates.T
    vmem = pl.BlockSpec(memory_space=pltpu.VMEM)
    shape = jax.ShapeDtypeStruct
    dma = pltpu.SemaphoreType.DMA
    wide = (MODES, SUB, CH)
    grad_query, grad_key, grad_value, sums, grad_weight = pl.pallas_call(
        kernel,
        out_shape=(
            shape((ROWS, CH), BF16),
            shape((ROWS, CH), BF16),
            shape((ROWS, CH), BF16),
            shape((2 * MODES, GROUPS, LANES), F32),
            shape((CH, 128), F32),
        ),
        in_specs=[vmem] * 9,
        out_specs=[vmem] * 5,
        scratch_shapes=[
            pltpu.VMEM((8, ROWS, 512), BF16),
            pltpu.VMEM((4, 4, CH, 256), BF16),
            pltpu.VMEM((4, 4, CH, 256), BF16),
            pltpu.VMEM((GROUPS, ROWS, LANES), F32),
            pltpu.VMEM((GROUPS, ROWS, LANES), F32),
            pltpu.VMEM((GROUPS, ROWS, LANES), F32),
            pltpu.VMEM((ROWS, ROWS), BF16),
            pltpu.VMEM((ROWS, ROWS), BF16),
            pltpu.VMEM(wide, F32),
            pltpu.VMEM(wide, F32),
            pltpu.VMEM((MODES, CH), BF16),
            pltpu.VMEM((NCTX, MODES, CH), BF16),
            pltpu.VMEM((MODES, CH), BF16),
            pltpu.VMEM((NCTX, MODES, CH), BF16),
            pltpu.VMEM((MODES, 1, CH), F32),
            pltpu.VMEM((MODES, CH), F32),
            pltpu.VMEM((GROUPS, 2 * MODES, SUB, LANES), F32),
            pltpu.VMEM(wide, F32),
            pltpu.VMEM(wide, F32),
            pltpu.VMEM(wide, F32),
            pltpu.VMEM((ROWS, CH), F32),
            pltpu.VMEM((ROWS, CH), BF16),
            pltpu.VMEM((CH, ROWS), BF16),
            pltpu.VMEM((2 * MODES, GROUPS, LANES), F32),
            pltpu.VMEM((NCTX, GROUPS, LANES), F32),
            pltpu.VMEM((NCTX, GROUPS, LANES), F32),
            pltpu.VMEM((2, 4, 128, 256), BF16),
            pltpu.VMEM((2, 2, 4, 128, 256), BF16),
            pltpu.VMEM((2, 128, 256), BF16),
            pltpu.VMEM((2, 2, 128, 256), BF16),
            pltpu.VMEM((2, 4, 128, 256), BF16),
            pltpu.VMEM((2, 2, 4, 128, 256), BF16),
            pltpu.VMEM((2, 128, 256), BF16),
            pltpu.VMEM((2, 2, 128, 256), BF16),
            pltpu.VMEM((4, 256, 256), BF16),
            pltpu.VMEM((4, 256, 256), BF16),
            pltpu.VMEM((CH, 256), F32),
            pltpu.VMEM((CH, 128), BF16),
            pltpu.VMEM((CH, 128), BF16),
            dma((N_RING,)),
            dma((N_RING,)),
            dma((NCTX,)),
            dma((NCTX,)),
            dma((NCTX,)),
            dma((NCTX,)),
            dma((NCTX,)),
            dma((NCTX,)),
            dma((NCTX,)),
            dma((NCTX,)),
            dma((2,)),
        ],
        compiler_params=pltpu.CompilerParams(
            collective_id=0, has_side_effects=True, vmem_limit_bytes=56 * 1024 * 1024
        ),
        cost_estimate=pl.CostEstimate(
            flops=5_000_000_000, bytes_accessed=5_000_000, transcendentals=0
        ),
    )(
        query_proj, key_proj, value_proj, gain2, rate2,
        gain2[:, None, :], rate2[:, None, :], out_weight, grad_out,
    )
    flat = sums.reshape(2 * MODES, CH).T
    gain_sum, rate_sum = flat[:, :MODES], flat[:, MODES:]
    rates = jnp.exp(log_rates)
    scale = NORM * jnp.sqrt(2.0 * rates)
    grad_gains = scale * gain_sum
    grad_rates = scale * filter_gains * (0.5 * gain_sum - rates * rate_sum)
    return (grad_query, grad_key, grad_value, grad_gains, grad_rates, grad_weight)


def solution(mesh):
    in_specs = (
        P("context", "tensor"),
        P("context", "tensor"),
        P("context", "tensor"),
        P("tensor", None),
        P("tensor", None),
        P("tensor", "context"),
        P("context", "tensor"),
    )
    out_specs = (
        P("context", "tensor"),
        P("context", "tensor"),
        P("context", "tensor"),
        P("tensor", None),
        P("tensor", None),
        P("tensor", "context"),
    )
    return jax.shard_map(
        on_device, mesh=mesh, in_specs=in_specs, out_specs=out_specs, check_vma=False
    )
```

```python
import math

import jax
import jax.numpy as jnp
from jax import lax
from jax.experimental import pallas as pl
from jax.experimental.pallas import tpu as pltpu
from jax.sharding import PartitionSpec as P

BF16 = jnp.bfloat16
F32 = jnp.float32
MESH = pl.DeviceIdType.MESH

NCTX = 32
ROWS = 512
CH = 512
MODES = 16
SUB = 8
STEPS = ROWS // SUB
LANES = 128
GROUPS = CH // LANES
SEQ = ROWS * NCTX
NORM = 1.0 / math.sqrt(SEQ)

N_A = 36
N_W = 29
N_O = 6 * 4 + 6 + 6 + 6 + 1
OFF_W = N_A
OFF_O = OFF_W + N_W
N_RING = OFF_O + N_O
PLANE = 16
W_SPLIT = 256


def shift_sub(val, step):
    rolled = pltpu.roll(val, step % SUB, 1)
    ids = lax.broadcasted_iota(jnp.int32, val.shape, 1)
    keep = ids >= step if step > 0 else ids < SUB + step
    return jnp.where(keep, rolled, 0.0)


def kernel(
    q_ref, k_ref, v_ref, gain2, rate2, w_ref, go_ref,
    gq_out, gk_out, gv_out, gain_out, rate_out, ow_out,
    rate3, ag, wg, op, xs, gs, ys, perm, perm_t, a8, amp8,
    ebuf, epeer, esend, eall, qbuf, qpeer, qsend, qall, hd3, st2,
    scr8, hfs, hft, hbwd, gate, cv, gt, yz, yz_in, yz_all,
    oppx, finx, vsum, oppy, finy, oppb, finb, vcol, oppv, finv, rsum, rsend, zin,
    ring_s, ring_r, e_s, e_r, q_s, q_r, y_s, y_r, o_s, o_r, pair_s, pair_r, loc,
):
    c = lax.axis_index("context")
    t = lax.axis_index("tensor")
    x = c // 8
    y = (c // 2) % 4
    zl = c % 2
    zh = t // 2
    core = t % 2
    plane = c // 2

    def ctx_of(xx, yy, zz):
        return xx * 8 + yy * 2 + zz

    xm, xp, xo = (x + 3) % 4, (x + 1) % 4, (x + 2) % 4
    ym, yp, yo = (y + 3) % 4, (y + 1) % 4, (y + 2) % 4
    zm, zp, zo = (zh + 3) % 4, (zh + 1) % 4, (zh + 2) % 4
    x_right, x_left = ctx_of(xp, y, zl), ctx_of(xm, y, zl)
    y_right, y_left = ctx_of(x, yp, zl), ctx_of(x, ym, zl)
    z_peer = ctx_of(x, y, 1 - zl)
    partner = zh * 2 + (1 - core)
    t_right, t_left = zp * 2 + core, zm * 2 + core

    pending = []

    def remote(index, src, dst, ctx, ten):
        copy = pltpu.make_async_remote_copy(
            src_ref=src, dst_ref=dst, send_sem=ring_s.at[index], recv_sem=ring_r.at[index],
            device_id=(ctx, ten), device_id_type=MESH,
        )
        copy.start()
        pending.append(copy)
        return copy

    def run(first, last, fun):
        def body(i, carry):
            fun(i)
            return carry

        lax.fori_loop(first, last, body, 0)

    barrier = pltpu.get_barrier_semaphore()

    def greet(d):
        pl.semaphore_signal(barrier, inc=1, device_id=((c + d) % NCTX, t), device_id_type=MESH)

    run(1, NCTX, greet)
    for ten in (partner, t_right, t_left):
        pl.semaphore_signal(barrier, inc=1, device_id=(c, ten), device_id_type=MESH)
    pl.semaphore_wait(barrier, NCTX - 1 + 3)

    lane_half = [pl.ds(0, 256), pl.ds(256, 256)]
    mine, theirs = pl.multiple_of(core * 256, 256), pl.multiple_of((1 - core) * 256, 256)
    a_init = []
    for h in range(2):
        a_init.append(remote(
            h, go_ref.at[pl.ds(theirs, 256), lane_half[h]],
            ag.at[zh, core * 2 + h, pl.ds(theirs, 256)], c, partner,
        ))
    own_lanes = pl.ds(pl.multiple_of(zl * 128, 128), 128)
    wz = remote(OFF_W, w_ref, wg.at[x, y, :, own_lanes], z_peer, t)
    local = [
        pltpu.make_async_copy(
            go_ref.at[:, lane_half[h]], ag.at[zh, core * 2 + h], loc.at[h]
        )
        for h in range(2)
    ]
    local.append(pltpu.make_async_copy(w_ref, wg.at[x, y, :, own_lanes], loc.at[2]))
    for copy in local:
        copy.start()
    for h in range(2):
        a_init.append(remote(
            2 + h, go_ref.at[pl.ds(mine, 256), lane_half[h]],
            ag.at[zh, core * 2 + h, pl.ds(mine, 256)], c, partner,
        ))

    rate_rows = jnp.exp(rate2[...])
    decay_rows = jnp.exp(-rate_rows)
    amp_rows = gain2[...] * jnp.sqrt(2.0 * rate_rows)
    for m in range(MODES):
        rate3[m] = rate_rows[m:m + 1, :]
        a8[m] = jnp.broadcast_to(decay_rows[m:m + 1, :], (SUB, CH))
        amp8[m] = jnp.broadcast_to(amp_rows[m:m + 1, :], (SUB, CH))

    order = [yo, yp, ym, y]
    duty = pl.ds(mine, 256)
    duty_lo = pl.ds(mine, 128)
    duty_hi = pl.ds(pl.multiple_of(core * 256 + 128, 128), 128)
    piece_own, piece_fwd, piece_par = {}, {}, {}

    def piece_start(k):
        src = ag.at[zh, order[k], duty]
        base = 4 + 8 * k
        piece_own[k] = (
            remote(base, src, src, c, t_right), remote(base + 1, src, src, c, t_left)
        )

    def piece_forward(k):
        base = 4 + 8 * k
        from_left, from_right = piece_own[k]
        yk = order[k]
        from_left.wait_recv()
        lo = ag.at[zm, yk, duty_lo]
        f_r = remote(base + 2, lo, lo, c, t_right)
        full = ag.at[zm, yk, duty]
        p_l = remote(base + 4, full, full, c, partner)
        from_right.wait_recv()
        hi = ag.at[zp, yk, duty_hi]
        f_l = remote(base + 3, hi, hi, c, t_left)
        full = ag.at[zp, yk, duty]
        p_r = remote(base + 5, full, full, c, partner)
        piece_fwd[k] = (f_r, f_l)
        piece_par[k] = [p_l, p_r]
        if k + 2 < 4:
            piece_start(k + 2)

    def piece_end(k):
        base = 4 + 8 * k
        yk = order[k]
        f_r, f_l = piece_fwd[k]
        f_r.wait_recv()
        lo = ag.at[zo, yk, duty_lo]
        p_a = remote(base + 6, lo, lo, c, partner)
        f_l.wait_recv()
        hi = ag.at[zo, yk, duty_hi]
        p_b = remote(base + 7, hi, hi, c, partner)
        for copy in piece_par[k] + [p_a, p_b]:
            copy.wait_recv()

    for copy in local:
        copy.wait()
    for copy in a_init:
        copy.wait_recv()
    piece_start(0)

    row_id = lax.broadcasted_iota(jnp.int32, (ROWS, ROWS), 0)
    col_id = lax.broadcasted_iota(jnp.int32, (ROWS, ROWS), 1)
    perm[...] = jnp.where(col_id == STEPS * (row_id % SUB) + row_id // SUB, 1.0, 0.0).astype(BF16)
    perm_t[...] = jnp.where(row_id == STEPS * (col_id % SUB) + col_id // SUB, 1.0, 0.0).astype(BF16)

    def spread(dst, natural):
        mixed = jnp.dot(perm[...], natural, preferred_element_type=F32)
        for grp in range(GROUPS):
            dst[grp] = mixed[:, grp * LANES:(grp + 1) * LANES]

    def gather_back():
        mixed = jnp.concatenate([ys[grp] for grp in range(GROUPS)], axis=1).astype(BF16)
        return jnp.dot(perm_t[...], mixed, preferred_element_type=F32)

    signal = (k_ref[...].astype(F32) * v_ref[...].astype(F32)).astype(BF16)
    spread(xs, signal)

    w0, w1 = pl.ds(0, W_SPLIT), pl.ds(W_SPLIT, CH - W_SPLIT)
    half0, half1 = W_SPLIT // 2, (CH - W_SPLIT) // 2
    w0a, w0b = pl.ds(0, half0), pl.ds(half0, half0)
    w1a, w1b = pl.ds(W_SPLIT, half1), pl.ds(W_SPLIT + half1, half1)
    wb = OFF_W + 1
    wc = {}

    def w_send(index, ref, ctx):
        return remote(wb + index, ref, ref, ctx, t)

    def w_row(b, xb):
        wc["yr", b] = w_send(4 + 4 * b, wg.at[xb, y, w0], y_right)
        wc["yl", b] = w_send(5 + 4 * b, wg.at[xb, y, w0], y_left)

    def w_row_forward(b, xb):
        wc["yr", b].wait_recv()
        wc["yfr", b] = w_send(6 + 4 * b, wg.at[xb, ym, w0a], y_right)
        wc["yl", b].wait_recv()
        wc["yfl", b] = w_send(7 + 4 * b, wg.at[xb, yp, w0b], y_left)

    def w_first():
        wz.wait_recv()
        wc["xr"] = w_send(0, wg.at[x, y, w0], x_right)
        wc["xl"] = w_send(1, wg.at[x, y, w0], x_left)
        wc["1r"] = w_send(20, wg.at[x, y, w1], y_right)
        wc["1l"] = w_send(21, wg.at[x, y, w1], y_left)
        w_row(0, x)

    def w_second():
        wc["xr"].wait_recv()
        wc["xfr"] = w_send(2, wg.at[xm, y, w0a], x_right)
        wc["xl"].wait_recv()
        wc["xfl"] = w_send(3, wg.at[xp, y, w0b], x_left)
        wc["1r"].wait_recv()
        wc["1fr"] = w_send(22, wg.at[x, ym, w1a], y_right)
        wc["1l"].wait_recv()
        wc["1fl"] = w_send(23, wg.at[x, yp, w1b], y_left)
        w_row(1, xm)
        w_row(2, xp)

    def w_third():
        wc["1fr"].wait_recv()
        wc["1fl"].wait_recv()
        wc["2r"] = w_send(24, wg.at[x, :, w1], x_right)
        wc["2l"] = w_send(25, wg.at[x, :, w1], x_left)
        w_row_forward(0, x)
        wc["xfr"].wait_recv()
        wc["xfl"].wait_recv()
        w_row(3, xo)

    def w_fourth():
        wc["2r"].wait_recv()
        wc["2fr"] = w_send(26, wg.at[xm, :, w1a], x_right)
        wc["2l"].wait_recv()
        wc["2fl"] = w_send(27, wg.at[xp, :, w1b], x_left)
        w_row_forward(1, xm)
        w_row_forward(2, xp)

    def w_fifth():
        w_row_forward(3, xo)

    def w_end():
        for b in range(4):
            wc["yfr", b].wait_recv()
            wc["yfl", b].wait_recv()
        wc["2fr"].wait_recv()
        wc["2fl"].wait_recv()

    w_first()

    def lane_at(grp):
        return pl.ds(pl.multiple_of(grp * LANES, LANES), LANES)

    def step_rows(j):
        return pl.ds(pl.multiple_of(j * SUB, SUB), SUB)

    def rates_at(grp):
        return rate3[:, :, lane_at(grp)]

    UNROLL = 4

    def forward_group(grp):
        decay = a8[:, :, lane_at(grp)]

        def step(i, carry):
            state, timed = carry
            for u in range(UNROLL):
                decayed = decay * state
                timed = decay * timed + decayed
                state = decayed + xs[grp, step_rows(i * UNROLL + u)][None]
            return (state, timed)

        zero = jnp.zeros((MODES, SUB, LANES), F32)
        state, timed = lax.fori_loop(0, STEPS // UNROLL, step, (zero, zero))
        rates = rates_at(grp)
        for power in (1, 2, 4):
            factor = jnp.exp(-rates * float(STEPS * power))
            before = shift_sub(state, power)
            timed = timed + factor * (shift_sub(timed, power) + float(STEPS * power) * before)
            state = state + factor * before
        hfs[:, :, lane_at(grp)] = shift_sub(state, 1)
        hft[:, :, lane_at(grp)] = shift_sub(timed, 1)
        scr8[grp, 0:MODES] = state
        scr8[grp, MODES:2 * MODES] = timed

    def backward_group(grp):
        decay = a8[:, :, lane_at(grp)]

        def step(i, state):
            for u in range(UNROLL):
                j = STEPS - 1 - (i * UNROLL + u)
                state = decay * state + gs[grp, step_rows(j)][None]
            return state

        state = lax.fori_loop(0, STEPS // UNROLL, step, jnp.zeros((MODES, SUB, LANES), F32))
        rates = rates_at(grp)
        for power in (1, 2, 4):
            factor = jnp.exp(-rates * float(STEPS * power))
            state = state + factor * shift_sub(state, -power)
        hbwd[:, :, lane_at(grp)] = shift_sub(state, -1)
        scr8[grp, 0:MODES] = state

    def edge_rows(count, edge):
        for grp in range(GROUPS):
            for m in range(count):
                st2[m:m + 1, grp * LANES:(grp + 1) * LANES] = scr8[grp, m, edge:edge + 1, :]

    def scan_out(src, backward, start):
        def group(grp):
            decay = a8[:, :, lane_at(grp)]
            amp = amp8[:, :, lane_at(grp)]

            def step(i, state):
                for u in range(UNROLL):
                    j = i * UNROLL + u
                    j = STEPS - 1 - j if backward else j
                    state = decay * state + src[grp, step_rows(j)][None]
                    ys[grp, step_rows(j)] = jnp.sum(amp * state, axis=0)
                return state

            lax.fori_loop(0, STEPS // UNROLL, step, start[:, :, lane_at(grp)])

        run(0, GROUPS, group)

    def exchange(src, dst, send, recv):
        def make(other, index):
            return pltpu.make_async_remote_copy(
                src_ref=src, dst_ref=dst.at[index], send_sem=send.at[other],
                recv_sem=recv.at[index], device_id=(other * 2 + zl, t), device_id_type=MESH,
            )

        return make

    def pair_copy(n, src, dst):
        return pltpu.make_async_remote_copy(
            src_ref=src, dst_ref=dst, send_sem=pair_s.at[n], recv_sem=pair_r.at[n],
            device_id=(z_peer, t), device_id_type=MESH,
        )

    chunk = float(ROWS)
    one_decay = jnp.exp(-rate_rows * chunk)
    two_decay = jnp.exp(-rate_rows * (2.0 * chunk))
    odd = zl == 1

    run(0, GROUPS, forward_group)
    edge_rows(2 * MODES, SUB - 1)
    ebuf[...] = st2[...].astype(BF16)
    e_pair = pair_copy(0, ebuf, epeer)
    e_pair.start()
    piece_start(1)
    piece_forward(0)
    w_second()
    e_pair.wait_recv()
    peer = epeer[...].astype(F32)
    own = st2[...]
    first = jnp.where(odd, peer, own)
    second = jnp.where(odd, own, peer)
    first_s, first_t = first[:MODES], first[MODES:]
    esend[0:MODES] = (second[:MODES] + one_decay * first_s).astype(BF16)
    esend[MODES:] = (second[MODES:] + one_decay * (first_t + chunk * first_s)).astype(BF16)
    e_copy = exchange(esend, eall, e_s, e_r)
    run(plane + 1, PLANE, lambda other: e_copy(other, plane).start())
    w_third()
    piece_forward(1)

    run(0, plane, lambda other: e_copy(other, other).wait_recv())

    def join_forward(j, carry):
        head_s, head_t = carry
        rows = eall[j].astype(F32)
        return (
            two_decay * head_s + rows[:MODES],
            two_decay * (head_t + 2.0 * chunk * head_s) + rows[MODES:],
        )

    zero_rows = jnp.zeros((MODES, CH), F32)
    head_s, head_t = lax.fori_loop(0, plane, join_forward, (zero_rows, zero_rows))
    head_t = jnp.where(odd, peer[MODES:] + one_decay * (head_t + chunk * head_s), head_t)
    head_s = jnp.where(odd, peer[:MODES] + one_decay * head_s, head_s)
    for m in range(MODES):
        hd3[m] = head_s[m:m + 1, :]
        hd3[MODES + m] = head_t[m:m + 1, :]

    def incoming_forward(grp):
        ids = lax.broadcasted_iota(jnp.int32, (MODES, SUB, LANES), 1).astype(F32) * float(STEPS)
        weight = jnp.exp(-rates_at(grp) * ids)
        in_s = hd3[0:MODES, :, lane_at(grp)]
        in_t = hd3[MODES:2 * MODES, :, lane_at(grp)]
        hfs[:, :, lane_at(grp)] += weight * in_s
        hft[:, :, lane_at(grp)] += weight * (in_t + ids * in_s)

    run(0, GROUPS, incoming_forward)
    scan_out(xs, False, hfs)
    cv[...] = gather_back().astype(BF16)
    gated = (q_ref[...].astype(F32) * cv[...].astype(F32)).astype(BF16).astype(F32)
    gt[...] = jnp.transpose(gated).astype(BF16)

    rings = {}

    def add_into(ref, extra):
        ref[...] = (ref[...].astype(F32) + extra.astype(F32)).astype(BF16)
        return ref

    def part_a(part):
        return pl.ds(part * 128, 128)

    def part_b(part):
        return pl.ds(256 + part * 128, 128)

    ybase = OFF_O + 24
    bbase = OFF_O + 30
    vbase = OFF_O + 36
    along = {}

    def out_piece(k):
        yk = order[k]

        def block(j):
            op[j, yk] = jnp.dot(gt[...], ag[j, yk], preferred_element_type=F32).astype(BF16)

        run(0, 4, block)

        def unit(target, part):
            return op.at[target, yk, part_a(part)]

        base = OFF_O + 6 * k
        far_r = remote(base, unit(xo, 0), oppx.at[k, 0], x_right, t)
        far_l = remote(base + 1, unit(xo, 1), oppx.at[k, 1], x_left, t)
        rings[k] = [
            unit, far_r, far_l,
            remote(base + 2, unit(xp, 1), finx.at[k, 0, 1], x_right, t),
            remote(base + 3, unit(xm, 0), finx.at[k, 1, 0], x_left, t),
        ]

        def whole(part):
            return op.at[:, yk, part_b(part)]

        if k == 0:
            along["far_r"] = remote(bbase, whole(0), oppb.at[0], y_right, t)
            along["far_l"] = remote(bbase + 1, whole(1), oppb.at[1], y_left, t)
        elif k == 1:
            along["r1"] = remote(bbase + 2, whole(1), finb.at[0, 1], y_right, t)
        elif k == 2:
            along["l0"] = remote(bbase + 4, whole(0), finb.at[1, 0], y_left, t)

    def along_right():
        along["far_r"].wait_recv()
        ref = add_into(op.at[:, order[1], part_b(0)], oppb[0])
        along["r0"] = remote(bbase + 3, ref, finb.at[0, 0], y_right, t)

    def along_left():
        along["far_l"].wait_recv()
        ref = add_into(op.at[:, order[2], part_b(1)], oppb[1])
        along["l1"] = remote(bbase + 5, ref, finb.at[1, 1], y_left, t)

    def along_own():
        for name in ("r0", "r1", "l0", "l1"):
            along[name].wait_recv()
        for part in range(2):
            rows = slice(part * 128, (part + 1) * 128)
            vcol[:, rows] = (
                op[:, y, part_b(part)].astype(F32) + finb[0, part].astype(F32)
                + finb[1, part].astype(F32)
            ).astype(BF16)

        def unit(target, part):
            return vcol.at[target, part_a(part)]

        along["ring"] = [
            unit,
            remote(vbase, unit(xo, 0), oppv.at[0], x_right, t),
            remote(vbase + 1, unit(xo, 1), oppv.at[1], x_left, t),
            remote(vbase + 2, unit(xp, 1), finv.at[0, 1], x_right, t),
            remote(vbase + 3, unit(xm, 0), finv.at[1, 0], x_left, t),
        ]

    def along_add():
        unit, far_r, far_l = along["ring"][:3]
        far_r.wait_recv()
        ref = add_into(unit(xp, 0), oppv[0])
        along["ring"].append(remote(vbase + 4, ref, finv.at[0, 0], x_right, t))
        far_l.wait_recv()
        ref = add_into(unit(xm, 1), oppv[1])
        along["ring"].append(remote(vbase + 5, ref, finv.at[1, 1], x_left, t))

    def along_last():
        for copy in along["ring"][3:]:
            copy.wait_recv()
        for part in range(2):
            rsum[256 + part * 128:256 + (part + 1) * 128] = (
                vcol[x, part * 128:(part + 1) * 128].astype(F32) + finv[0, part].astype(F32)
                + finv[1, part].astype(F32)
            )

    def out_add(k):
        unit, far_r, far_l = rings[k][:3]
        base = OFF_O + 6 * k
        far_r.wait_recv()
        ref = add_into(unit(xp, 0), oppx[k, 0])
        rings[k].append(remote(base + 4, ref, finx.at[k, 0, 0], x_right, t))
        far_l.wait_recv()
        ref = add_into(unit(xm, 1), oppx[k, 1])
        rings[k].append(remote(base + 5, ref, finx.at[k, 1, 1], x_left, t))

    def out_sum(k):
        unit = rings[k][0]
        for copy in rings[k][3:]:
            copy.wait_recv()
        return [
            unit(x, part)[...].astype(F32) + finx[k, 0, part].astype(F32)
            + finx[k, 1, part].astype(F32)
            for part in range(2)
        ]

    second_ring = {}

    def out_first():
        parts = out_sum(0)
        for part in range(2):
            vsum[0, part] = parts[part].astype(BF16)
        second_ring["far_r"] = remote(ybase, vsum.at[0, 0], oppy.at[0], y_right, t)
        second_ring["far_l"] = remote(ybase + 1, vsum.at[0, 1], oppy.at[1], y_left, t)

    def out_second():
        parts = out_sum(1)
        vsum[1, 1] = parts[1].astype(BF16)
        second_ring["r1"] = remote(ybase + 2, vsum.at[1, 1], finy.at[0, 1], y_right, t)
        second_ring["far_r"].wait_recv()
        vsum[1, 0] = (parts[0] + oppy[0].astype(F32)).astype(BF16)
        second_ring["r0"] = remote(ybase + 3, vsum.at[1, 0], finy.at[0, 0], y_right, t)

    def out_third():
        parts = out_sum(2)
        vsum[2, 0] = parts[0].astype(BF16)
        second_ring["l0"] = remote(ybase + 4, vsum.at[2, 0], finy.at[1, 0], y_left, t)
        second_ring["far_l"].wait_recv()
        vsum[2, 1] = (parts[1] + oppy[1].astype(F32)).astype(BF16)
        second_ring["l1"] = remote(ybase + 5, vsum.at[2, 1], finy.at[1, 1], y_left, t)

    def out_last():
        parts = out_sum(3)
        for name in ("r0", "r1", "l0", "l1"):
            second_ring[name].wait_recv()
        for part in range(2):
            rsum[part * 128:(part + 1) * 128] = (
                parts[part] + finy[0, part].astype(F32) + finy[1, part].astype(F32)
            )

    dims = (((1,), (1,)), ((), ()))

    def gate_piece(k):
        yk = order[k]

        def block(j):
            gate[...] += lax.dot_general(
                ag[j, yk], wg[j, yk], dims, preferred_element_type=F32
            )

        run(0, 4, block)

    w_fourth()
    piece_end(0)
    out_piece(0)
    piece_forward(2)
    w_fifth()
    piece_end(1)
    out_piece(1)
    out_add(0)
    piece_forward(3)
    along_right()
    gate[...] = jnp.zeros_like(gate)
    w_end()
    gate_piece(0)
    gate_piece(1)
    out_first()
    piece_end(2)
    out_piece(2)
    out_add(1)
    gate_piece(2)
    along_left()
    piece_end(3)
    gate_piece(3)

    conv_grad = (gate[...] * q_ref[...].astype(F32)).astype(BF16)
    spread(gs, conv_grad)
    run(0, GROUPS, backward_group)
    edge_rows(MODES, 0)
    qbuf[...] = st2[0:MODES].astype(BF16)
    q_pair = pair_copy(1, qbuf, qpeer)
    q_pair.start()
    q_pair.wait_recv()
    peer_q = qpeer[...].astype(F32)
    own_q = st2[0:MODES]
    first_q = jnp.where(odd, peer_q, own_q)
    second_q = jnp.where(odd, own_q, peer_q)
    qsend[...] = (first_q + one_decay * second_q).astype(BF16)
    q_copy = exchange(qsend, qall, q_s, q_r)
    run(0, plane, lambda other: q_copy(other, plane).start())

    out_piece(3)
    out_add(2)
    along_own()
    gq_out[...] = (gate[...] * cv[...].astype(F32)).astype(BF16)

    def gain_scan(grp):
        for part in range(2):
            mode = pl.ds(part * 8, 8)
            decay = a8[mode, :, lane_at(grp)]

            def step(i, carry):
                state, timed, gain_sum, rate_sum = carry
                for u in range(UNROLL):
                    rows = step_rows(i * UNROLL + u)
                    grad = gs[grp, rows][None]
                    decayed = decay * state
                    timed = decay * timed + decayed
                    state = decayed + xs[grp, rows][None]
                    gain_sum = gain_sum + grad * state
                    rate_sum = rate_sum + grad * timed
                return (state, timed, gain_sum, rate_sum)

            zero = jnp.zeros((8, SUB, LANES), F32)
            _, _, gain_sum, rate_sum = lax.fori_loop(
                0, STEPS // UNROLL, step,
                (hfs[mode, :, lane_at(grp)], hft[mode, :, lane_at(grp)], zero, zero),
            )
            scr8[grp, mode] = gain_sum
            scr8[grp, pl.ds(MODES + part * 8, 8)] = rate_sum

    out_second()
    run(0, GROUPS, gain_scan)
    for grp in range(GROUPS):
        yz[:, grp] = jnp.sum(scr8[grp], axis=1)

    def y_copy(d, index):
        other = (c + d) % NCTX
        return pltpu.make_async_remote_copy(
            src_ref=yz.at[other], dst_ref=yz_in.at[index], send_sem=y_s.at[other],
            recv_sem=y_r.at[index], device_id=(other, t), device_id_type=MESH,
        )

    run(1, NCTX, lambda d: y_copy(d, c).start())
    out_add(3)
    along_add()
    for copy in pending[:OFF_O]:
        copy.wait_send()

    run(plane + 1, PLANE, lambda other: q_copy(other, other).wait_recv())
    tail = lax.fori_loop(
        0, PLANE - 1 - plane,
        lambda j, h: two_decay * h + qall[PLANE - 1 - j].astype(F32),
        zero_rows,
    )
    tail = jnp.where(odd, tail, peer_q + one_decay * tail)
    for m in range(MODES):
        hd3[m] = tail[m:m + 1, :]

    def incoming_backward(grp):
        ids = lax.broadcasted_iota(jnp.int32, (MODES, SUB, LANES), 1).astype(F32)
        weight = jnp.exp(-rates_at(grp) * (((SUB - 1.0) - ids) * float(STEPS)))
        hbwd[:, :, lane_at(grp)] += weight * hd3[0:MODES, :, lane_at(grp)]

    run(0, GROUPS, incoming_backward)
    out_third()
    scan_out(gs, True, hbwd)

    run(1, NCTX, lambda d: y_copy(d, (c + d) % NCTX).wait_recv())
    yz_in[c] = yz[c]
    yz_all[c] = jnp.sum(yz_in[...], axis=0)

    def o_copy(d, index):
        other = (c + d) % NCTX
        return pltpu.make_async_remote_copy(
            src_ref=yz_all.at[c], dst_ref=yz_all.at[index], send_sem=o_s.at[other],
            recv_sem=o_r.at[index], device_id=(other, t), device_id_type=MESH,
        )

    run(1, NCTX, lambda d: o_copy(d, c).start())

    out_last()
    along_last()
    rsend[...] = rsum[:, pl.ds(pl.multiple_of((1 - zl) * 128, 128), 128)].astype(BF16)
    z_copy = remote(OFF_O + 42, rsend, zin, z_peer, t)

    input_grad = gather_back().astype(BF16).astype(F32)
    gk_out[...] = (input_grad * v_ref[...].astype(F32)).astype(BF16)
    gv_out[...] = (input_grad * k_ref[...].astype(F32)).astype(BF16)

    z_copy.wait_recv()
    ow_out[...] = (rsum[:, own_lanes] + zin[...].astype(F32)) * NORM

    run(1, NCTX, lambda d: o_copy(d, (c + d) % NCTX).wait_recv())
    scale = NORM * jnp.sqrt(2.0 * rate_rows)
    gain_sum = jnp.concatenate([yz_all[0:MODES, grp] for grp in range(GROUPS)], axis=1)
    rate_sum = jnp.concatenate([yz_all[MODES:2 * MODES, grp] for grp in range(GROUPS)], axis=1)
    gain_out[...] = scale * gain_sum
    rate_out[...] = scale * gain2[...] * (0.5 * gain_sum - rate_rows * rate_sum)
    e_pair.wait_send()
    q_pair.wait_send()
    run(plane + 1, PLANE, lambda other: e_copy(other, plane).wait_send())
    run(0, plane, lambda other: q_copy(other, plane).wait_send())
    run(1, NCTX, lambda d: y_copy(d, c).wait_send())
    run(1, NCTX, lambda d: o_copy(d, c).wait_send())
    for copy in pending[OFF_O:]:
        copy.wait_send()


def on_device(query_proj, key_proj, value_proj, filter_gains, log_rates, out_weight, grad_out):
    gain2 = filter_gains.T
    rate2 = log_rates.T
    vmem = pl.BlockSpec(memory_space=pltpu.VMEM)
    shape = jax.ShapeDtypeStruct
    dma = pltpu.SemaphoreType.DMA
    wide = (MODES, SUB, CH)
    grad_query, grad_key, grad_value, grad_gains, grad_rates, grad_weight = pl.pallas_call(
        kernel,
        out_shape=(
            shape((ROWS, CH), BF16),
            shape((ROWS, CH), BF16),
            shape((ROWS, CH), BF16),
            shape((MODES, CH), F32),
            shape((MODES, CH), F32),
            shape((CH, 128), F32),
        ),
        in_specs=[vmem] * 7,
        out_specs=[vmem] * 6,
        scratch_shapes=[
            pltpu.VMEM((MODES, 1, CH), F32),
            pltpu.VMEM((4, 4, ROWS, 256), BF16),
            pltpu.VMEM((4, 4, CH, 256), BF16),
            pltpu.VMEM((4, 4, CH, 256), BF16),
            pltpu.VMEM((GROUPS, ROWS, LANES), F32),
            pltpu.VMEM((GROUPS, ROWS, LANES), F32),
            pltpu.VMEM((GROUPS, ROWS, LANES), F32),
            pltpu.VMEM((ROWS, ROWS), BF16),
            pltpu.VMEM((ROWS, ROWS), BF16),
            pltpu.VMEM(wide, F32),
            pltpu.VMEM(wide, F32),
            pltpu.VMEM((2 * MODES, CH), BF16),
            pltpu.VMEM((2 * MODES, CH), BF16),
            pltpu.VMEM((2 * MODES, CH), BF16),
            pltpu.VMEM((PLANE, 2 * MODES, CH), BF16),
            pltpu.VMEM((MODES, CH), BF16),
            pltpu.VMEM((MODES, CH), BF16),
            pltpu.VMEM((MODES, CH), BF16),
            pltpu.VMEM((PLANE, MODES, CH), BF16),
            pltpu.VMEM((2 * MODES, 1, CH), F32),
            pltpu.VMEM((2 * MODES, CH), F32),
            pltpu.VMEM((GROUPS, 2 * MODES, SUB, LANES), F32),
            pltpu.VMEM(wide, F32),
            pltpu.VMEM(wide, F32),
            pltpu.VMEM(wide, F32),
            pltpu.VMEM((ROWS, CH), F32),
            pltpu.VMEM((ROWS, CH), BF16),
            pltpu.VMEM((CH, ROWS), BF16),
            pltpu.VMEM((2 * MODES, GROUPS, LANES), F32),
            pltpu.VMEM((NCTX, GROUPS, LANES), F32),
            pltpu.VMEM((NCTX, GROUPS, LANES), F32),
            pltpu.VMEM((4, 2, 128, 256), BF16),
            pltpu.VMEM((4, 2, 2, 128, 256), BF16),
            pltpu.VMEM((3, 2, 128, 256), BF16),
            pltpu.VMEM((2, 128, 256), BF16),
            pltpu.VMEM((2, 2, 128, 256), BF16),
            pltpu.VMEM((2, 4, 128, 256), BF16),
            pltpu.VMEM((2, 2, 4, 128, 256), BF16),
            pltpu.VMEM((4, 256, 256), BF16),
            pltpu.VMEM((2, 128, 256), BF16),
            pltpu.VMEM((2, 2, 128, 256), BF16),
            pltpu.VMEM((CH, 256), F32),
            pltpu.VMEM((CH, 128), BF16),
            pltpu.VMEM((CH, 128), BF16),
            dma((N_RING,)),
            dma((N_RING,)),
            dma((PLANE,)),
            dma((PLANE,)),
            dma((PLANE,)),
            dma((PLANE,)),
            dma((NCTX,)),
            dma((NCTX,)),
            dma((NCTX,)),
            dma((NCTX,)),
            dma((2,)),
            dma((2,)),
            dma((3,)),
        ],
        compiler_params=pltpu.CompilerParams(
            collective_id=0, has_side_effects=True, vmem_limit_bytes=56 * 1024 * 1024
        ),
        cost_estimate=pl.CostEstimate(
            flops=5_000_000_000, bytes_accessed=5_000_000, transcendentals=0
        ),
    )(
        query_proj, key_proj, value_proj, gain2, rate2, out_weight, grad_out,
    )
    return (grad_query, grad_key, grad_value, grad_gains.T, grad_rates.T, grad_weight)


def solution(mesh):
    in_specs = (
        P("context", "tensor"),
        P("context", "tensor"),
        P("context", "tensor"),
        P("tensor", None),
        P("tensor", None),
        P("tensor", "context"),
        P("context", "tensor"),
    )
    out_specs = (
        P("context", "tensor"),
        P("context", "tensor"),
        P("context", "tensor"),
        P("tensor", None),
        P("tensor", None),
        P("tensor", "context"),
    )
    return jax.shard_map(
        on_device, mesh=mesh, in_specs=in_specs, out_specs=out_specs, check_vma=False
    )
```

```python
import math

import jax
import jax.numpy as jnp
from jax import lax
from jax.experimental import pallas as pl
from jax.experimental.pallas import tpu as pltpu
from jax.sharding import PartitionSpec as P

BF16 = jnp.bfloat16
F32 = jnp.float32
MESH = pl.DeviceIdType.MESH

NCTX = 32
ROWS = 512
CH = 512
MODES = 16
SUB = 8
STEPS = ROWS // SUB
LANES = 128
GROUPS = CH // LANES
SEQ = ROWS * NCTX
NORM = 1.0 / math.sqrt(SEQ)

N_A = 36
N_W = 45
N_O = 6 * 4 + 6 + 6 + 6 + 1
OFF_W = N_A
OFF_O = OFF_W + N_W
N_RING = OFF_O + N_O
SENT_ROWS = (448, 496, 496)
PLANE = 16
W_SPLIT = 256


def shift_sub(val, step):
    rolled = pltpu.roll(val, step % SUB, 1)
    ids = lax.broadcasted_iota(jnp.int32, val.shape, 1)
    keep = ids >= step if step > 0 else ids < SUB + step
    return jnp.where(keep, rolled, 0.0)


def kernel(
    q_in, k_in, v_in, gain2, rate2, w_ref, go_ref,
    gq_out, gk_out, gv_out, gain_out, rate_out, ow_out,
    q_ref, k_ref, v_ref, gq_buf, gk_buf, gv_buf, ow_buf, rate3, ag, wg, op, xs, gs, ys, perm, perm_t, a8, amp8,
    ebuf, epeer, esend, eall, qbuf, qpeer, qsend, qall, hd3, st2,
    scr8, hfs, hft, hbwd, gate, cv, gt, yz, yz_in, yz_all,
    oppx, finx, vsum, oppy, finy, oppb, finb, vcol, oppv, finv, rsum, rsend, zin,
    ring_s, ring_r, e_s, e_r, q_s, q_r, y_s, y_r, o_s, o_r, pair_s, pair_r, loc, io,
):
    c = lax.axis_index("context")
    t = lax.axis_index("tensor")
    x = c // 8
    y = (c // 2) % 4
    zl = c % 2
    zh = t // 2
    core = t % 2
    plane = c // 2

    def ctx_of(xx, yy, zz):
        return xx * 8 + yy * 2 + zz

    xm, xp, xo = (x + 3) % 4, (x + 1) % 4, (x + 2) % 4
    ym, yp, yo = (y + 3) % 4, (y + 1) % 4, (y + 2) % 4
    zm, zp, zo = (zh + 3) % 4, (zh + 1) % 4, (zh + 2) % 4
    x_right, x_left = ctx_of(xp, y, zl), ctx_of(xm, y, zl)
    y_right, y_left = ctx_of(x, yp, zl), ctx_of(x, ym, zl)
    z_peer = ctx_of(x, y, 1 - zl)
    partner = zh * 2 + (1 - core)
    t_right, t_left = zp * 2 + core, zm * 2 + core

    def remote(index, src, dst, ctx, ten):
        copy = pltpu.make_async_remote_copy(
            src_ref=src, dst_ref=dst, send_sem=ring_s.at[(index >= OFF_W) + (index >= OFF_O)],
            recv_sem=ring_r.at[index],
            device_id=(ctx, ten), device_id_type=MESH,
        )
        copy.start()
        return copy

    def wait_bytes(ref, sem):
        pltpu.make_async_copy(ref, ref, sem).wait()

    def run(first, last, fun):
        def body(i, carry):
            fun(i)
            return carry

        lax.fori_loop(first, last, body, 0)

    barrier = pltpu.get_barrier_semaphore()

    def greet(d):
        pl.semaphore_signal(barrier, inc=1, device_id=((c + d) % NCTX, t), device_id_type=MESH)

    run(1, NCTX, greet)
    for ten in (partner, t_right, t_left):
        pl.semaphore_signal(barrier, inc=1, device_id=(c, ten), device_id_type=MESH)
    loads = [
        pltpu.make_async_copy(src, dst, io.at[n])
        for n, (src, dst) in enumerate([(k_in, k_ref), (v_in, v_ref), (q_in, q_ref)])
    ]
    for copy in loads:
        copy.start()

    pl.semaphore_wait(barrier, NCTX - 1 + 3)

    lane_half = [pl.ds(0, 256), pl.ds(256, 256)]
    mine, theirs = pl.multiple_of(core * 256, 256), pl.multiple_of((1 - core) * 256, 256)
    a_init = []
    for h in range(2):
        a_init.append(remote(
            h, go_ref.at[pl.ds(theirs, 256), lane_half[h]],
            ag.at[zh, core * 2 + h, pl.ds(theirs, 256)], c, partner,
        ))
    own_lanes = pl.ds(pl.multiple_of(zl * 128, 128), 128)
    wz = remote(OFF_W, w_ref, wg.at[x, y, :, own_lanes], z_peer, t)
    local = [
        pltpu.make_async_copy(
            go_ref.at[:, lane_half[h]], ag.at[zh, core * 2 + h], loc.at[h]
        )
        for h in range(2)
    ]
    local.append(pltpu.make_async_copy(w_ref, wg.at[x, y, :, own_lanes], loc.at[2]))
    for copy in local:
        copy.start()
    for h in range(2):
        a_init.append(remote(
            2 + h, go_ref.at[pl.ds(mine, 256), lane_half[h]],
            ag.at[zh, core * 2 + h, pl.ds(mine, 256)], c, partner,
        ))

    order = [yo, yp, ym, y]
    duty = pl.ds(mine, 256)
    duty_lo = pl.ds(mine, 128)
    duty_hi = pl.ds(pl.multiple_of(core * 256 + 128, 128), 128)
    piece_own, piece_fwd, piece_par = {}, {}, {}

    def piece_start(k):
        src = ag.at[zh, order[k], duty]
        base = 4 + 8 * k
        piece_own[k] = (
            remote(base, src, src, c, t_right), remote(base + 1, src, src, c, t_left)
        )

    def piece_forward(k):
        base = 4 + 8 * k
        from_left, from_right = piece_own[k]
        yk = order[k]
        from_left.wait_recv()
        lo = ag.at[zm, yk, duty_lo]
        f_r = remote(base + 2, lo, lo, c, t_right)
        full = ag.at[zm, yk, duty]
        p_l = remote(base + 4, full, full, c, partner)
        from_right.wait_recv()
        hi = ag.at[zp, yk, duty_hi]
        f_l = remote(base + 3, hi, hi, c, t_left)
        full = ag.at[zp, yk, duty]
        p_r = remote(base + 5, full, full, c, partner)
        piece_fwd[k] = (f_r, f_l)
        piece_par[k] = [p_l, p_r]
        if k + 2 < 4:
            piece_start(k + 2)

    def piece_pass(k):
        base = 4 + 8 * k
        yk = order[k]
        f_r, f_l = piece_fwd[k]
        f_r.wait_recv()
        lo = ag.at[zo, yk, duty_lo]
        p_a = remote(base + 6, lo, lo, c, partner)
        f_l.wait_recv()
        hi = ag.at[zo, yk, duty_hi]
        p_b = remote(base + 7, hi, hi, c, partner)
        piece_par[k] += [p_a, p_b]

    def piece_wait(k):
        for copy in piece_par[k]:
            copy.wait_recv()

    rate_rows = jnp.exp(rate2[...])
    decay_rows = jnp.exp(-rate_rows)
    amp_rows = gain2[...] * jnp.sqrt(2.0 * rate_rows)
    for m in range(MODES):
        rate3[m] = rate_rows[m:m + 1, :]
        a8[m] = jnp.broadcast_to(decay_rows[m:m + 1, :], (SUB, CH))
        amp8[m] = jnp.broadcast_to(amp_rows[m:m + 1, :], (SUB, CH))

    def spread(dst, natural):
        mixed = jnp.dot(perm[...], natural, preferred_element_type=F32)
        for grp in range(GROUPS):
            dst[grp] = mixed[:, grp * LANES:(grp + 1) * LANES]

    def gather_back():
        mixed = jnp.concatenate([ys[grp] for grp in range(GROUPS)], axis=1).astype(BF16)
        return jnp.dot(perm_t[...], mixed, preferred_element_type=F32)

    w0, w1 = pl.ds(0, W_SPLIT), pl.ds(W_SPLIT, CH - W_SPLIT)
    half0, half1 = W_SPLIT // 2, (CH - W_SPLIT) // 2
    w0a, w0b = pl.ds(0, half0), pl.ds(half0, half0)
    w1a, w1b = pl.ds(W_SPLIT, half1), pl.ds(W_SPLIT + half1, half1)
    wb = OFF_W + 1
    wc = {}

    def w_send(index, ref, ctx):
        return remote(wb + index, ref, ref, ctx, t)

    def w_row(b, xb):
        wc["yr", b] = w_send(4 + 4 * b, wg.at[xb, y, w0], y_right)
        wc["yl", b] = w_send(5 + 4 * b, wg.at[xb, y, w0], y_left)

    def w_row_forward(b, xb):
        wc["yr", b].wait_recv()
        wc["yfr", b] = w_send(6 + 4 * b, wg.at[xb, ym, w0a], y_right)
        wc["yl", b].wait_recv()
        wc["yfl", b] = w_send(7 + 4 * b, wg.at[xb, yp, w0b], y_left)

    def w_col(b, yb):
        wc["xr", b] = w_send(24 + 4 * b, wg.at[x, yb, w1], x_right)
        wc["xl", b] = w_send(25 + 4 * b, wg.at[x, yb, w1], x_left)

    def w_col_forward(b, yb):
        wc["xr", b].wait_recv()
        wc["xfr", b] = w_send(26 + 4 * b, wg.at[xm, yb, w1a], x_right)
        wc["xl", b].wait_recv()
        wc["xfl", b] = w_send(27 + 4 * b, wg.at[xp, yb, w1b], x_left)

    def w_early():
        for n, (rows, ctx) in enumerate(((w0, x_right), (w0, x_left), (w1, y_right), (w1, y_left))):
            wc["early", n] = remote(
                wb + 40 + n, w_ref.at[rows], wg.at[x, y, rows, own_lanes], ctx, t
            )

    def w_first():
        wz.wait_recv()
        peer_lanes = pl.ds(pl.multiple_of((1 - zl) * 128, 128), 128)
        wc["xr"] = w_send(0, wg.at[x, y, w0, peer_lanes], x_right)
        wc["xl"] = w_send(1, wg.at[x, y, w0, peer_lanes], x_left)
        wc["1r"] = w_send(20, wg.at[x, y, w1, peer_lanes], y_right)
        wc["1l"] = w_send(21, wg.at[x, y, w1, peer_lanes], y_left)
        w_row(0, x)
        w_col(0, y)

    def w_second():
        for n in range(4):
            wc["early", n].wait_recv()
        wc["xr"].wait_recv()
        wc["xfr"] = w_send(2, wg.at[xm, y, w0a], x_right)
        wc["xl"].wait_recv()
        wc["xfl"] = w_send(3, wg.at[xp, y, w0b], x_left)
        wc["1r"].wait_recv()
        wc["1fr"] = w_send(22, wg.at[x, ym, w1a], y_right)
        wc["1l"].wait_recv()
        wc["1fl"] = w_send(23, wg.at[x, yp, w1b], y_left)
        w_row(1, xm)
        w_col(1, ym)
        w_row(2, xp)
        w_col(2, yp)

    def w_third():
        wc["1fr"].wait_recv()
        wc["1fl"].wait_recv()
        wc["xfr"].wait_recv()
        wc["xfl"].wait_recv()
        w_row(3, xo)
        w_col(3, yo)
        w_row_forward(0, x)
        w_col_forward(0, y)

    def w_fourth():
        w_row_forward(1, xm)
        w_col_forward(1, ym)
        w_row_forward(2, xp)
        w_col_forward(2, yp)

    def w_fifth():
        w_row_forward(3, xo)
        w_col_forward(3, yo)

    def w_end():
        for b in range(4):
            for name in ("yfr", "yfl", "xfr", "xfl"):
                wc[name, b].wait_recv()

    w_early()

    def lane_at(grp):
        return pl.ds(pl.multiple_of(grp * LANES, LANES), LANES)

    def step_rows(j):
        return pl.ds(pl.multiple_of(j * SUB, SUB), SUB)

    def rates_at(grp):
        return rate3[:, :, lane_at(grp)]

    UNROLL = 4

    def forward_group(grp):
        decay = a8[:, :, lane_at(grp)]

        def step(i, carry):
            state, timed = carry
            for u in range(UNROLL):
                decayed = decay * state
                timed = decay * timed + decayed
                state = decayed + xs[grp, step_rows(i * UNROLL + u)][None]
            return (state, timed)

        zero = jnp.zeros((MODES, SUB, LANES), F32)
        state, timed = lax.fori_loop(0, STEPS // UNROLL, step, (zero, zero))
        rates = rates_at(grp)
        for power in (1, 2, 4):
            factor = jnp.exp(-rates * float(STEPS * power))
            before = shift_sub(state, power)
            timed = timed + factor * (shift_sub(timed, power) + float(STEPS * power) * before)
            state = state + factor * before
        hfs[:, :, lane_at(grp)] = shift_sub(state, 1)
        hft[:, :, lane_at(grp)] = shift_sub(timed, 1)
        scr8[grp, 0:MODES] = state
        scr8[grp, MODES:2 * MODES] = timed

    def backward_group(grp):
        decay = a8[:, :, lane_at(grp)]

        def step(i, state):
            for u in range(UNROLL):
                j = STEPS - 1 - (i * UNROLL + u)
                state = decay * state + gs[grp, step_rows(j)][None]
            return state

        state = lax.fori_loop(0, STEPS // UNROLL, step, jnp.zeros((MODES, SUB, LANES), F32))
        rates = rates_at(grp)
        for power in (1, 2, 4):
            factor = jnp.exp(-rates * float(STEPS * power))
            state = state + factor * shift_sub(state, -power)
        hbwd[:, :, lane_at(grp)] = shift_sub(state, -1)
        scr8[grp, 0:MODES] = state

    def edge_rows(count, edge):
        for grp in range(GROUPS):
            for m in range(count):
                st2[m:m + 1, grp * LANES:(grp + 1) * LANES] = scr8[grp, m, edge:edge + 1, :]

    def scan_out(src, backward, start, group0, group1):
        def group(grp):
            decay = a8[:, :, lane_at(grp)]
            amp = amp8[:, :, lane_at(grp)]

            def step(i, state):
                for u in range(UNROLL):
                    j = i * UNROLL + u
                    j = STEPS - 1 - j if backward else j
                    state = decay * state + src[grp, step_rows(j)][None]
                    ys[grp, step_rows(j)] = jnp.sum(amp * state, axis=0)
                return state

            lax.fori_loop(0, STEPS // UNROLL, step, start[:, :, lane_at(grp)])

        run(group0, group1, group)

    def exchange(src, dst, send, recv):
        def make(other, index):
            return pltpu.make_async_remote_copy(
                src_ref=src, dst_ref=dst.at[index], send_sem=send.at[other],
                recv_sem=recv.at[index], device_id=(other * 2 + zl, t), device_id_type=MESH,
            )

        return make

    def pair_copy(n, src, dst):
        return pltpu.make_async_remote_copy(
            src_ref=src, dst_ref=dst, send_sem=pair_s.at[n], recv_sem=pair_r.at[n],
            device_id=(z_peer, t), device_id_type=MESH,
        )

    chunk = float(ROWS)
    one_decay = jnp.exp(-rate_rows * chunk)
    two_decay = jnp.exp(-rate_rows * (2.0 * chunk))
    odd = zl == 1

    for copy in local:
        copy.wait()
    for copy in a_init:
        copy.wait_recv()
    piece_start(0)
    row_id = lax.broadcasted_iota(jnp.int32, (ROWS, ROWS), 0)
    col_id = lax.broadcasted_iota(jnp.int32, (ROWS, ROWS), 1)
    perm[...] = jnp.where(col_id == STEPS * (row_id % SUB) + row_id // SUB, 1.0, 0.0).astype(BF16)
    perm_t[...] = jnp.where(row_id == STEPS * (col_id % SUB) + col_id // SUB, 1.0, 0.0).astype(BF16)

    loads[0].wait()
    loads[1].wait()
    signal = (k_ref[...].astype(F32) * v_ref[...].astype(F32)).astype(BF16)
    spread(xs, signal)
    run(0, 2, forward_group)
    w_first()
    run(2, GROUPS, forward_group)
    edge_rows(2 * MODES, SUB - 1)
    ebuf[...] = st2[...].astype(BF16)
    e_pair = pair_copy(0, ebuf, epeer)
    e_pair.start()
    piece_start(1)
    w_second()
    e_pair.wait_recv()
    peer = epeer[...].astype(F32)
    own = st2[...]
    first = jnp.where(odd, peer, own)
    second = jnp.where(odd, own, peer)
    first_s, first_t = first[:MODES], first[MODES:]
    esend[0:MODES] = (second[:MODES] + one_decay * first_s).astype(BF16)
    esend[MODES:] = (second[MODES:] + one_decay * (first_t + chunk * first_s)).astype(BF16)
    e_copy = exchange(esend, eall, e_s, e_r)
    run(plane + 1, PLANE, lambda other: e_copy(other, plane).start())
    piece_forward(0)
    w_third()
    piece_forward(1)

    run(0, plane, lambda other: e_copy(other, other).wait_recv())

    def join_forward(j, carry):
        head_s, head_t = carry
        rows = eall[j].astype(F32)
        return (
            two_decay * head_s + rows[:MODES],
            two_decay * (head_t + 2.0 * chunk * head_s) + rows[MODES:],
        )

    zero_rows = jnp.zeros((MODES, CH), F32)
    head_s, head_t = lax.fori_loop(0, plane, join_forward, (zero_rows, zero_rows))
    head_t = jnp.where(odd, peer[MODES:] + one_decay * (head_t + chunk * head_s), head_t)
    head_s = jnp.where(odd, peer[:MODES] + one_decay * head_s, head_s)
    for m in range(MODES):
        hd3[m] = head_s[m:m + 1, :]
        hd3[MODES + m] = head_t[m:m + 1, :]

    def incoming_forward(grp):
        ids = lax.broadcasted_iota(jnp.int32, (MODES, SUB, LANES), 1).astype(F32) * float(STEPS)
        weight = jnp.exp(-rates_at(grp) * ids)
        in_s = hd3[0:MODES, :, lane_at(grp)]
        in_t = hd3[MODES:2 * MODES, :, lane_at(grp)]
        hfs[:, :, lane_at(grp)] += weight * in_s
        hft[:, :, lane_at(grp)] += weight * (in_t + ids * in_s)

    run(0, GROUPS, incoming_forward)
    w_fourth()
    scan_out(xs, False, hfs, 0, 2)
    piece_pass(0)
    scan_out(xs, False, hfs, 2, GROUPS)
    w_fifth()
    piece_forward(2)
    loads[2].wait()
    cv[...] = gather_back().astype(BF16)
    gated = (q_ref[...].astype(F32) * cv[...].astype(F32)).astype(BF16).astype(F32)
    gt[...] = jnp.transpose(gated).astype(BF16)

    rings = {}

    def add_into(ref, extra):
        ref[...] = (ref[...].astype(F32) + extra.astype(F32)).astype(BF16)
        return ref

    def part_a(part):
        return pl.ds(part * 128, 128)

    def part_b(part):
        return pl.ds(256 + part * 128, 128)

    ybase = OFF_O + 24
    bbase = OFF_O + 30
    vbase = OFF_O + 36
    along = {}

    def out_piece(k):
        yk = order[k]

        def block(j):
            op[j, yk] = jnp.dot(gt[...], ag[j, yk], preferred_element_type=F32).astype(BF16)

        run(0, 4, block)

        def unit(target, part):
            return op.at[target, yk, part_a(part)]

        base = OFF_O + 6 * k
        far_r = remote(base, unit(xo, 0), oppx.at[k, 0], x_right, t)
        far_l = remote(base + 1, unit(xo, 1), oppx.at[k, 1], x_left, t)
        rings[k] = [
            unit, far_r, far_l,
            remote(base + 2, unit(xp, 1), finx.at[k, 0, 1], x_right, t),
            remote(base + 3, unit(xm, 0), finx.at[k, 1, 0], x_left, t),
        ]

        def whole(part):
            return op.at[:, yk, part_b(part)]

        if k == 0:
            along["far_r"] = remote(bbase, whole(0), oppb.at[0], y_right, t)
            along["far_l"] = remote(bbase + 1, whole(1), oppb.at[1], y_left, t)
        elif k == 1:
            along["r1"] = remote(bbase + 2, whole(1), finb.at[0, 1], y_right, t)
        elif k == 2:
            along["l0"] = remote(bbase + 4, whole(0), finb.at[1, 0], y_left, t)

    def along_right():
        along["far_r"].wait_recv()
        ref = add_into(op.at[:, order[1], part_b(0)], oppb[0])
        along["r0"] = remote(bbase + 3, ref, finb.at[0, 0], y_right, t)

    def along_left():
        along["far_l"].wait_recv()
        ref = add_into(op.at[:, order[2], part_b(1)], oppb[1])
        along["l1"] = remote(bbase + 5, ref, finb.at[1, 1], y_left, t)

    def along_own():
        for name in ("r0", "r1", "l0", "l1"):
            along[name].wait_recv()
        for part in range(2):
            rows = slice(part * 128, (part + 1) * 128)
            vcol[:, rows] = (
                op[:, y, part_b(part)].astype(F32) + finb[0, part].astype(F32)
                + finb[1, part].astype(F32)
            ).astype(BF16)

        def unit(target, part):
            return vcol.at[target, part_a(part)]

        along["ring"] = [
            unit,
            remote(vbase, unit(xo, 0), oppv.at[0], x_right, t),
            remote(vbase + 1, unit(xo, 1), oppv.at[1], x_left, t),
            remote(vbase + 2, unit(xp, 1), finv.at[0, 1], x_right, t),
            remote(vbase + 3, unit(xm, 0), finv.at[1, 0], x_left, t),
        ]

    def along_add():
        unit, far_r, far_l = along["ring"][:3]
        far_r.wait_recv()
        ref = add_into(unit(xp, 0), oppv[0])
        along["ring"].append(remote(vbase + 4, ref, finv.at[0, 0], x_right, t))
        far_l.wait_recv()
        ref = add_into(unit(xm, 1), oppv[1])
        along["ring"].append(remote(vbase + 5, ref, finv.at[1, 1], x_left, t))

    def along_last():
        for copy in along["ring"][3:]:
            copy.wait_recv()
        for part in range(2):
            rsum[256 + part * 128:256 + (part + 1) * 128] = (
                vcol[x, part * 128:(part + 1) * 128].astype(F32) + finv[0, part].astype(F32)
                + finv[1, part].astype(F32)
            )

    def out_add(k):
        unit, far_r, far_l = rings[k][:3]
        base = OFF_O + 6 * k
        far_r.wait_recv()
        ref = add_into(unit(xp, 0), oppx[k, 0])
        rings[k].append(remote(base + 4, ref, finx.at[k, 0, 0], x_right, t))
        far_l.wait_recv()
        ref = add_into(unit(xm, 1), oppx[k, 1])
        rings[k].append(remote(base + 5, ref, finx.at[k, 1, 1], x_left, t))

    def out_sum(k):
        unit = rings[k][0]
        for copy in rings[k][3:]:
            copy.wait_recv()
        return [
            unit(x, part)[...].astype(F32) + finx[k, 0, part].astype(F32)
            + finx[k, 1, part].astype(F32)
            for part in range(2)
        ]

    second_ring = {}

    def out_first():
        parts = out_sum(0)
        for part in range(2):
            vsum[0, part] = parts[part].astype(BF16)
        second_ring["far_r"] = remote(ybase, vsum.at[0, 0], oppy.at[0], y_right, t)
        second_ring["far_l"] = remote(ybase + 1, vsum.at[0, 1], oppy.at[1], y_left, t)

    def out_second():
        parts = out_sum(1)
        vsum[1, 1] = parts[1].astype(BF16)
        second_ring["r1"] = remote(ybase + 2, vsum.at[1, 1], finy.at[0, 1], y_right, t)
        second_ring["far_r"].wait_recv()
        vsum[1, 0] = (parts[0] + oppy[0].astype(F32)).astype(BF16)
        second_ring["r0"] = remote(ybase + 3, vsum.at[1, 0], finy.at[0, 0], y_right, t)

    def out_third():
        parts = out_sum(2)
        vsum[2, 0] = parts[0].astype(BF16)
        second_ring["l0"] = remote(ybase + 4, vsum.at[2, 0], finy.at[1, 0], y_left, t)
        second_ring["far_l"].wait_recv()
        vsum[2, 1] = (parts[1] + oppy[1].astype(F32)).astype(BF16)
        second_ring["l1"] = remote(ybase + 5, vsum.at[2, 1], finy.at[1, 1], y_left, t)

    def out_last():
        parts = out_sum(3)
        for name in ("r0", "r1", "l0", "l1"):
            second_ring[name].wait_recv()
        for part in range(2):
            rsum[part * 128:(part + 1) * 128] = (
                parts[part] + finy[0, part].astype(F32) + finy[1, part].astype(F32)
            )

    dims = (((1,), (1,)), ((), ()))

    def gate_piece(k):
        yk = order[k]

        def block(j):
            gate[...] += lax.dot_general(
                ag[j, yk], wg[j, yk], dims, preferred_element_type=F32
            )

        run(0, 4, block)

    piece_pass(1)
    piece_wait(0)
    out_piece(0)
    w_end()
    gate[...] = jnp.zeros_like(gate)
    gate_piece(0)
    piece_forward(3)
    piece_wait(1)
    out_piece(1)
    gate_piece(1)
    out_add(0)
    piece_pass(2)
    along_right()
    piece_wait(2)
    out_piece(2)
    out_add(1)
    gate_piece(2)
    piece_pass(3)
    along_left()
    piece_wait(3)
    gate_piece(3)
    out_first()

    conv_grad = (gate[...] * q_ref[...].astype(F32)).astype(BF16)
    spread(gs, conv_grad)
    run(0, GROUPS, backward_group)
    edge_rows(MODES, 0)
    qbuf[...] = st2[0:MODES].astype(BF16)
    q_pair = pair_copy(1, qbuf, qpeer)
    q_pair.start()

    def gain_scan(grp):
        for part in range(2):
            mode = pl.ds(part * 8, 8)
            decay = a8[mode, :, lane_at(grp)]

            def step(i, carry):
                state, timed, gain_sum, rate_sum = carry
                for u in range(UNROLL):
                    rows = step_rows(i * UNROLL + u)
                    grad = gs[grp, rows][None]
                    decayed = decay * state
                    timed = decay * timed + decayed
                    state = decayed + xs[grp, rows][None]
                    gain_sum = gain_sum + grad * state
                    rate_sum = rate_sum + grad * timed
                return (state, timed, gain_sum, rate_sum)

            zero = jnp.zeros((8, SUB, LANES), F32)
            _, _, gain_sum, rate_sum = lax.fori_loop(
                0, STEPS // UNROLL, step,
                (hfs[mode, :, lane_at(grp)], hft[mode, :, lane_at(grp)], zero, zero),
            )
            scr8[grp, mode] = gain_sum
            scr8[grp, pl.ds(MODES + part * 8, 8)] = rate_sum

    def y_copy(d, index):
        other = (c + d) % NCTX
        return pltpu.make_async_remote_copy(
            src_ref=yz.at[other], dst_ref=yz_in.at[index], send_sem=y_s.at[0],
            recv_sem=y_r.at[0], device_id=(other, t), device_id_type=MESH,
        )

    def o_copy(d, index):
        other = (c + d) % NCTX
        return pltpu.make_async_remote_copy(
            src_ref=yz_all.at[c], dst_ref=yz_all.at[index], send_sem=o_s.at[0],
            recv_sem=o_r.at[0], device_id=(other, t), device_id_type=MESH,
        )

    def incoming_backward(grp):
        ids = lax.broadcasted_iota(jnp.int32, (MODES, SUB, LANES), 1).astype(F32)
        weight = jnp.exp(-rates_at(grp) * (((SUB - 1.0) - ids) * float(STEPS)))
        hbwd[:, :, lane_at(grp)] += weight * hd3[0:MODES, :, lane_at(grp)]

    out_piece(3)
    out_add(2)
    q_pair.wait_recv()
    peer_q = qpeer[...].astype(F32)
    own_q = st2[0:MODES]
    first_q = jnp.where(odd, peer_q, own_q)
    second_q = jnp.where(odd, own_q, peer_q)
    qsend[...] = (first_q + one_decay * second_q).astype(BF16)
    q_copy = exchange(qsend, qall, q_s, q_r)
    run(0, plane, lambda other: q_copy(other, plane).start())

    gq_buf[...] = (gate[...] * cv[...].astype(F32)).astype(BF16)
    stores = [pltpu.make_async_copy(gq_buf, gq_out, io.at[3])]
    stores[0].start()
    out_second()
    along_own()
    run(0, 1, gain_scan)
    out_add(3)
    run(1, 3, gain_scan)
    out_third()
    run(3, GROUPS, gain_scan)
    for grp in range(GROUPS):
        yz[:, grp] = jnp.sum(scr8[grp], axis=1)
    run(1, NCTX, lambda d: y_copy(d, c).start())
    along_add()

    run(plane + 1, PLANE, lambda other: q_copy(other, other).wait_recv())
    tail = lax.fori_loop(
        0, PLANE - 1 - plane,
        lambda j, h: two_decay * h + qall[PLANE - 1 - j].astype(F32),
        zero_rows,
    )
    tail = jnp.where(odd, tail, peer_q + one_decay * tail)
    for m in range(MODES):
        hd3[m] = tail[m:m + 1, :]
    run(0, GROUPS, incoming_backward)
    scan_out(gs, True, hbwd, 0, 2)
    out_last()
    along_last()
    rsend[...] = rsum[:, pl.ds(pl.multiple_of((1 - zl) * 128, 128), 128)].astype(BF16)
    z_copy = remote(OFF_O + 42, rsend, zin, z_peer, t)
    scan_out(gs, True, hbwd, 2, GROUPS)
    wait_bytes(yz_in.at[pl.ds(0, NCTX - 1)], y_r.at[0])
    yz_in[c] = yz[c]
    yz_all[c] = jnp.sum(yz_in[...], axis=0)
    run(1, NCTX, lambda d: o_copy(d, c).start())
    input_grad = gather_back().astype(BF16).astype(F32)
    gk_buf[...] = (input_grad * v_ref[...].astype(F32)).astype(BF16)
    stores.append(pltpu.make_async_copy(gk_buf, gk_out, io.at[4]))
    stores[1].start()
    gv_buf[...] = (input_grad * k_ref[...].astype(F32)).astype(BF16)
    stores.append(pltpu.make_async_copy(gv_buf, gv_out, io.at[5]))
    stores[2].start()

    def flush_sends():
        run(plane + 1, PLANE, lambda other: e_copy(other, plane).wait_send())
        run(0, plane, lambda other: q_copy(other, plane).wait_send())
        wait_bytes(yz.at[pl.ds(0, NCTX - 1)], y_s.at[0])
        e_pair.wait_send()
        q_pair.wait_send()
        for n, (ref, rows) in enumerate(zip((ag, wg, op), SENT_ROWS)):
            wait_bytes(ref.at[:, :, pl.ds(0, rows)], ring_s.at[n])

    flush_sends()
    z_copy.wait_recv()
    ow_buf[...] = (rsum[:, own_lanes] + zin[...].astype(F32)) * NORM
    stores.append(pltpu.make_async_copy(ow_buf, ow_out, io.at[6]))
    stores[3].start()

    wait_bytes(yz_all.at[pl.ds(0, NCTX - 1)], o_r.at[0])
    scale = NORM * jnp.sqrt(2.0 * rate_rows)
    gain_sum = jnp.concatenate([yz_all[0:MODES, grp] for grp in range(GROUPS)], axis=1)
    rate_sum = jnp.concatenate([yz_all[MODES:2 * MODES, grp] for grp in range(GROUPS)], axis=1)
    gain_out[...] = scale * gain_sum
    rate_out[...] = scale * gain2[...] * (0.5 * gain_sum - rate_rows * rate_sum)
    wait_bytes(yz_all.at[pl.ds(0, NCTX - 1)], o_s.at[0])
    for copy in stores:
        copy.wait()


def on_device(query_proj, key_proj, value_proj, filter_gains, log_rates, out_weight, grad_out):
    gain2 = filter_gains.T
    rate2 = log_rates.T
    vmem = pl.BlockSpec(memory_space=pltpu.VMEM)
    hbm = pl.BlockSpec(memory_space=pl.ANY)
    shape = jax.ShapeDtypeStruct
    dma = pltpu.SemaphoreType.DMA
    wide = (MODES, SUB, CH)
    grad_query, grad_key, grad_value, grad_gains, grad_rates, grad_weight = pl.pallas_call(
        kernel,
        out_shape=(
            shape((ROWS, CH), BF16),
            shape((ROWS, CH), BF16),
            shape((ROWS, CH), BF16),
            shape((MODES, CH), F32),
            shape((MODES, CH), F32),
            shape((CH, 128), F32),
        ),
        in_specs=[hbm, hbm, hbm, vmem, vmem, hbm, hbm],
        out_specs=[hbm, hbm, hbm, vmem, vmem, hbm],
        scratch_shapes=[
            pltpu.VMEM((ROWS, CH), BF16),
            pltpu.VMEM((ROWS, CH), BF16),
            pltpu.VMEM((ROWS, CH), BF16),
            pltpu.VMEM((ROWS, CH), BF16),
            pltpu.VMEM((ROWS, CH), BF16),
            pltpu.VMEM((ROWS, CH), BF16),
            pltpu.VMEM((CH, 128), F32),
            pltpu.VMEM((MODES, 1, CH), F32),
            pltpu.VMEM((4, 4, ROWS, 256), BF16),
            pltpu.VMEM((4, 4, CH, 256), BF16),
            pltpu.VMEM((4, 4, CH, 256), BF16),
            pltpu.VMEM((GROUPS, ROWS, LANES), F32),
            pltpu.VMEM((GROUPS, ROWS, LANES), F32),
            pltpu.VMEM((GROUPS, ROWS, LANES), F32),
            pltpu.VMEM((ROWS, ROWS), BF16),
            pltpu.VMEM((ROWS, ROWS), BF16),
            pltpu.VMEM(wide, F32),
            pltpu.VMEM(wide, F32),
            pltpu.VMEM((2 * MODES, CH), BF16),
            pltpu.VMEM((2 * MODES, CH), BF16),
            pltpu.VMEM((2 * MODES, CH), BF16),
            pltpu.VMEM((PLANE, 2 * MODES, CH), BF16),
            pltpu.VMEM((MODES, CH), BF16),
            pltpu.VMEM((MODES, CH), BF16),
            pltpu.VMEM((MODES, CH), BF16),
            pltpu.VMEM((PLANE, MODES, CH), BF16),
            pltpu.VMEM((2 * MODES, 1, CH), F32),
            pltpu.VMEM((2 * MODES, CH), F32),
            pltpu.VMEM((GROUPS, 2 * MODES, SUB, LANES), F32),
            pltpu.VMEM(wide, F32),
            pltpu.VMEM(wide, F32),
            pltpu.VMEM(wide, F32),
            pltpu.VMEM((ROWS, CH), F32),
            pltpu.VMEM((ROWS, CH), BF16),
            pltpu.VMEM((CH, ROWS), BF16),
            pltpu.VMEM((2 * MODES, GROUPS, LANES), F32),
            pltpu.VMEM((NCTX, GROUPS, LANES), F32),
            pltpu.VMEM((NCTX, GROUPS, LANES), F32),
            pltpu.VMEM((4, 2, 128, 256), BF16),
            pltpu.VMEM((4, 2, 2, 128, 256), BF16),
            pltpu.VMEM((3, 2, 128, 256), BF16),
            pltpu.VMEM((2, 128, 256), BF16),
            pltpu.VMEM((2, 2, 128, 256), BF16),
            pltpu.VMEM((2, 4, 128, 256), BF16),
            pltpu.VMEM((2, 2, 4, 128, 256), BF16),
            pltpu.VMEM((4, 256, 256), BF16),
            pltpu.VMEM((2, 128, 256), BF16),
            pltpu.VMEM((2, 2, 128, 256), BF16),
            pltpu.VMEM((CH, 256), F32),
            pltpu.VMEM((CH, 128), BF16),
            pltpu.VMEM((CH, 128), BF16),
            dma((3,)),
            dma((N_RING,)),
            dma((PLANE,)),
            dma((PLANE,)),
            dma((PLANE,)),
            dma((PLANE,)),
            dma((1,)),
            dma((1,)),
            dma((1,)),
            dma((1,)),
            dma((2,)),
            dma((2,)),
            dma((3,)),
            dma((7,)),
        ],
        compiler_params=pltpu.CompilerParams(
            collective_id=0, has_side_effects=True, vmem_limit_bytes=56 * 1024 * 1024
        ),
        cost_estimate=pl.CostEstimate(
            flops=5_000_000_000, bytes_accessed=5_000_000, transcendentals=0
        ),
    )(
        query_proj, key_proj, value_proj, gain2, rate2, out_weight, grad_out,
    )
    return (grad_query, grad_key, grad_value, grad_gains.T, grad_rates.T, grad_weight)


def solution(mesh):
    in_specs = (
        P("context", "tensor"),
        P("context", "tensor"),
        P("context", "tensor"),
        P("tensor", None),
        P("tensor", None),
        P("tensor", "context"),
        P("context", "tensor"),
    )
    out_specs = (
        P("context", "tensor"),
        P("context", "tensor"),
        P("context", "tensor"),
        P("tensor", None),
        P("tensor", None),
        P("tensor", "context"),
    )
    return jax.shard_map(
        on_device, mesh=mesh, in_specs=in_specs, out_specs=out_specs, check_vma=False
    )
```

```python
import math

import jax
import jax.numpy as jnp
from jax import lax
from jax.experimental import pallas as pl
from jax.experimental.pallas import tpu as pltpu
from jax.sharding import PartitionSpec as P

BF16 = jnp.bfloat16
F32 = jnp.float32
MESH = pl.DeviceIdType.MESH

NCTX = 32
ROWS = 512
CH = 512
MODES = 16
SUB = 8
STEPS = ROWS // SUB
LANES = 128
GROUPS = CH // LANES
SEQ = ROWS * NCTX
NORM = 1.0 / math.sqrt(SEQ)

N_A = 36
N_W = 45
N_O = 6 * 4 + 6 + 6 + 6 + 2
OFF_W = N_A
OFF_O = OFF_W + N_W
N_RING = OFF_O + N_O
SENT_ROWS = (448, 496, 496)
W_SPLIT = 256


def shift_sub(val, step):
    rolled = pltpu.roll(val, step % SUB, 1)
    ids = lax.broadcasted_iota(jnp.int32, val.shape, 1)
    keep = ids >= step if step > 0 else ids < SUB + step
    return jnp.where(keep, rolled, 0.0)


def kernel(
    q_in, k_in, v_in, gain_in, rate_in, w_ref, go_ref,
    gq_out, ig_out, yz_out, ow_out,
    q_ref, k_ref, v_ref, gain2, rate2, rate3, tkeep, ag, wg, op, xs, gs, ys, perm, perm_t, a8, amp8,
    ebuf, epeer, esend, erow, eout, ecol, qbuf, qpeer, qsend, qrow, qout, qcol, hd3, st2,
    scr8, hfs, hft, hbwd, gate, cv, gt, yz, yz_in, yz_all,
    oppx, finx, vsum, oppy, finy, oppb, finb, vcol, oppv, finv, rsum, rsend, zin,
    ring_s, ring_r, e_s, e_r, q_s, q_r, y_s, y_r, o_s, o_r, pair_s, pair_r, loc, io,
):
    c = lax.axis_index("context")
    t = lax.axis_index("tensor")
    x = c // 8
    y = (c // 2) % 4
    zl = c % 2
    zh = t // 2
    core = t % 2

    def ctx_of(xx, yy, zz):
        return xx * 8 + yy * 2 + zz

    xm, xp, xo = (x + 3) % 4, (x + 1) % 4, (x + 2) % 4
    ym, yp, yo = (y + 3) % 4, (y + 1) % 4, (y + 2) % 4
    zm, zp, zo = (zh + 3) % 4, (zh + 1) % 4, (zh + 2) % 4
    x_right, x_left = ctx_of(xp, y, zl), ctx_of(xm, y, zl)
    y_right, y_left = ctx_of(x, yp, zl), ctx_of(x, ym, zl)
    z_peer = ctx_of(x, y, 1 - zl)
    partner = zh * 2 + (1 - core)
    t_right, t_left = zp * 2 + core, zm * 2 + core

    def remote(index, src, dst, ctx, ten):
        copy = pltpu.make_async_remote_copy(
            src_ref=src, dst_ref=dst, send_sem=ring_s.at[(index >= OFF_W) + (index >= OFF_O)],
            recv_sem=ring_r.at[index],
            device_id=(ctx, ten), device_id_type=MESH,
        )
        copy.start()
        return copy

    def wait_bytes(ref, sem):
        pltpu.make_async_copy(ref, ref, sem).wait()

    def run(first, last, fun):
        def body(i, carry):
            fun(i)
            return carry

        lax.fori_loop(first, last, body, 0)

    barrier = pltpu.get_barrier_semaphore()

    def greet(d):
        pl.semaphore_signal(barrier, inc=1, device_id=((c + d) % NCTX, t), device_id_type=MESH)

    run(1, NCTX, greet)
    for ten in (partner, t_right, t_left):
        pl.semaphore_signal(barrier, inc=1, device_id=(c, ten), device_id_type=MESH)
    loads = [
        pltpu.make_async_copy(src, dst, io.at[n])
        for n, (src, dst) in enumerate(
            [(k_in, k_ref), (v_in, v_ref), (q_in, q_ref), (gain_in, gain2), (rate_in, rate2)]
        )
    ]
    for copy in reversed(loads):
        copy.start()

    pl.semaphore_wait(barrier, NCTX - 1 + 3)

    lane_half = [pl.ds(0, 256), pl.ds(256, 256)]
    mine, theirs = pl.multiple_of(core * 256, 256), pl.multiple_of((1 - core) * 256, 256)
    a_init = []
    for h in range(2):
        a_init.append(remote(
            h, go_ref.at[pl.ds(theirs, 256), lane_half[h]],
            ag.at[zh, core * 2 + h, pl.ds(theirs, 256)], c, partner,
        ))
    own_lanes = pl.ds(pl.multiple_of(zl * 128, 128), 128)
    wz = remote(OFF_W, w_ref, wg.at[x, y, :, own_lanes], z_peer, t)
    local = [
        pltpu.make_async_copy(
            go_ref.at[:, lane_half[h]], ag.at[zh, core * 2 + h], loc.at[h]
        )
        for h in range(2)
    ]
    local.append(pltpu.make_async_copy(w_ref, wg.at[x, y, :, own_lanes], loc.at[2]))
    for copy in local:
        copy.start()
    for h in range(2):
        a_init.append(remote(
            2 + h, go_ref.at[pl.ds(mine, 256), lane_half[h]],
            ag.at[zh, core * 2 + h, pl.ds(mine, 256)], c, partner,
        ))

    order = [yo, yp, ym, y]
    duty = pl.ds(mine, 256)
    duty_lo = pl.ds(mine, 128)
    duty_hi = pl.ds(pl.multiple_of(core * 256 + 128, 128), 128)
    piece_own, piece_fwd, piece_par = {}, {}, {}

    def piece_start(k):
        src = ag.at[zh, order[k], duty]
        base = 4 + 8 * k
        piece_own[k] = (
            remote(base, src, src, c, t_right), remote(base + 1, src, src, c, t_left)
        )

    def piece_forward(k):
        base = 4 + 8 * k
        from_left, from_right = piece_own[k]
        yk = order[k]
        from_left.wait_recv()
        lo = ag.at[zm, yk, duty_lo]
        f_r = remote(base + 2, lo, lo, c, t_right)
        full = ag.at[zm, yk, duty]
        p_l = remote(base + 4, full, full, c, partner)
        from_right.wait_recv()
        hi = ag.at[zp, yk, duty_hi]
        f_l = remote(base + 3, hi, hi, c, t_left)
        full = ag.at[zp, yk, duty]
        p_r = remote(base + 5, full, full, c, partner)
        piece_fwd[k] = (f_r, f_l)
        piece_par[k] = [p_l, p_r]
        if k + 2 < 4:
            piece_start(k + 2)

    def piece_pass(k):
        base = 4 + 8 * k
        yk = order[k]
        f_r, f_l = piece_fwd[k]
        f_r.wait_recv()
        lo = ag.at[zo, yk, duty_lo]
        p_a = remote(base + 6, lo, lo, c, partner)
        f_l.wait_recv()
        hi = ag.at[zo, yk, duty_hi]
        p_b = remote(base + 7, hi, hi, c, partner)
        piece_par[k] += [p_a, p_b]

    def piece_wait(k):
        for copy in piece_par[k]:
            copy.wait_recv()

    loads[3].wait()
    loads[4].wait()
    rate_rows = jnp.exp(rate2[...])
    decay_rows = jnp.exp(-rate_rows)
    amp_rows = gain2[...] * jnp.sqrt(2.0 * rate_rows)
    for m in range(MODES):
        rate3[m] = rate_rows[m:m + 1, :]
        a8[m] = jnp.broadcast_to(decay_rows[m:m + 1, :], (SUB, CH))
        amp8[m] = jnp.broadcast_to(amp_rows[m:m + 1, :], (SUB, CH))

    def spread(dst, natural):
        mixed = jnp.dot(perm[...], natural, preferred_element_type=F32)
        for grp in range(GROUPS):
            dst[grp] = mixed[:, grp * LANES:(grp + 1) * LANES]

    def gather_back():
        mixed = jnp.concatenate([ys[grp] for grp in range(GROUPS)], axis=1).astype(BF16)
        return jnp.dot(perm_t[...], mixed, preferred_element_type=F32)

    w0, w1 = pl.ds(0, W_SPLIT), pl.ds(W_SPLIT, CH - W_SPLIT)
    half0, half1 = W_SPLIT // 2, (CH - W_SPLIT) // 2
    w0a, w0b = pl.ds(0, half0), pl.ds(half0, half0)
    w1a, w1b = pl.ds(W_SPLIT, half1), pl.ds(W_SPLIT + half1, half1)
    wb = OFF_W + 1
    wc = {}

    def w_send(index, ref, ctx):
        return remote(wb + index, ref, ref, ctx, t)

    def w_row(b, xb):
        wc["yr", b] = w_send(4 + 4 * b, wg.at[xb, y, w0], y_right)
        wc["yl", b] = w_send(5 + 4 * b, wg.at[xb, y, w0], y_left)

    def w_row_forward(b, xb):
        wc["yr", b].wait_recv()
        wc["yfr", b] = w_send(6 + 4 * b, wg.at[xb, ym, w0a], y_right)
        wc["yl", b].wait_recv()
        wc["yfl", b] = w_send(7 + 4 * b, wg.at[xb, yp, w0b], y_left)

    def w_col(b, yb):
        wc["xr", b] = w_send(24 + 4 * b, wg.at[x, yb, w1], x_right)
        wc["xl", b] = w_send(25 + 4 * b, wg.at[x, yb, w1], x_left)

    def w_col_forward(b, yb):
        wc["xr", b].wait_recv()
        wc["xfr", b] = w_send(26 + 4 * b, wg.at[xm, yb, w1a], x_right)
        wc["xl", b].wait_recv()
        wc["xfl", b] = w_send(27 + 4 * b, wg.at[xp, yb, w1b], x_left)

    def w_early():
        for n, (rows, ctx) in enumerate(((w0, x_right), (w0, x_left), (w1, y_right), (w1, y_left))):
            wc["early", n] = remote(
                wb + 40 + n, w_ref.at[rows], wg.at[x, y, rows, own_lanes], ctx, t
            )

    def w_first():
        wz.wait_recv()
        peer_lanes = pl.ds(pl.multiple_of((1 - zl) * 128, 128), 128)
        wc["xr"] = w_send(0, wg.at[x, y, w0, peer_lanes], x_right)
        wc["xl"] = w_send(1, wg.at[x, y, w0, peer_lanes], x_left)
        wc["1r"] = w_send(20, wg.at[x, y, w1, peer_lanes], y_right)
        wc["1l"] = w_send(21, wg.at[x, y, w1, peer_lanes], y_left)
        w_row(0, x)
        w_col(0, y)

    def w_second():
        for n in range(4):
            wc["early", n].wait_recv()
        wc["xr"].wait_recv()
        wc["xfr"] = w_send(2, wg.at[xm, y, w0a], x_right)
        wc["xl"].wait_recv()
        wc["xfl"] = w_send(3, wg.at[xp, y, w0b], x_left)
        wc["1r"].wait_recv()
        wc["1fr"] = w_send(22, wg.at[x, ym, w1a], y_right)
        wc["1l"].wait_recv()
        wc["1fl"] = w_send(23, wg.at[x, yp, w1b], y_left)
        w_row(1, xm)
        w_col(1, ym)
        w_row(2, xp)
        w_col(2, yp)

    def w_third():
        wc["1fr"].wait_recv()
        wc["1fl"].wait_recv()
        wc["xfr"].wait_recv()
        wc["xfl"].wait_recv()
        w_row(3, xo)
        w_col(3, yo)
        w_row_forward(0, x)
        w_col_forward(0, y)

    def w_fourth():
        w_row_forward(1, xm)
        w_col_forward(1, ym)
        w_row_forward(2, xp)
        w_col_forward(2, yp)

    def w_fifth():
        w_row_forward(3, xo)
        w_col_forward(3, yo)

    def w_end():
        for b in range(4):
            for name in ("yfr", "yfl", "xfr", "xfl"):
                wc[name, b].wait_recv()

    w_early()

    def lane_at(grp):
        return pl.ds(pl.multiple_of(grp * LANES, LANES), LANES)

    def step_rows(j):
        return pl.ds(pl.multiple_of(j * SUB, SUB), SUB)

    def rates_at(grp):
        return rate3[:, :, lane_at(grp)]

    UNROLL = 4

    def forward_group(grp):
        decay = a8[:, :, lane_at(grp)]

        def step(i, carry):
            state, timed = carry
            for u in range(UNROLL):
                decayed = decay * state
                timed = decay * timed + decayed
                state = decayed + xs[grp, step_rows(i * UNROLL + u)][None]
            return (state, timed)

        zero = jnp.zeros((MODES, SUB, LANES), F32)
        state, timed = lax.fori_loop(0, STEPS // UNROLL, step, (zero, zero))
        rates = rates_at(grp)
        for power in (1, 2, 4):
            factor = jnp.exp(-rates * float(STEPS * power))
            before = shift_sub(state, power)
            timed = timed + factor * (shift_sub(timed, power) + float(STEPS * power) * before)
            state = state + factor * before
        hfs[:, :, lane_at(grp)] = shift_sub(state, 1)
        hft[:, :, lane_at(grp)] = shift_sub(timed, 1)
        scr8[grp, 0:MODES] = state
        scr8[grp, MODES:2 * MODES] = timed

    def backward_group(grp):
        decay = a8[:, :, lane_at(grp)]

        def step(i, state):
            for u in range(UNROLL):
                j = STEPS - 1 - (i * UNROLL + u)
                state = decay * state + gs[grp, step_rows(j)][None]
            return state

        state = lax.fori_loop(0, STEPS // UNROLL, step, jnp.zeros((MODES, SUB, LANES), F32))
        rates = rates_at(grp)
        for power in (1, 2, 4):
            factor = jnp.exp(-rates * float(STEPS * power))
            state = state + factor * shift_sub(state, -power)
        hbwd[:, :, lane_at(grp)] = shift_sub(state, -1)
        scr8[grp, 0:MODES] = state

    def edge_rows(count, edge):
        for grp in range(GROUPS):
            for m in range(count):
                st2[m:m + 1, grp * LANES:(grp + 1) * LANES] = scr8[grp, m, edge:edge + 1, :]

    def scan_forward(grp):
        decay = a8[:, :, lane_at(grp)]
        amp = amp8[:, :, lane_at(grp)]

        def step(i, carry):
            state, timed = carry
            for u in range(UNROLL):
                j = i * UNROLL + u
                decayed = decay * state
                timed = decay * timed + decayed
                state = decayed + xs[grp, step_rows(j)][None]
                tkeep[grp, j] = timed
                ys[grp, step_rows(j)] = jnp.sum(amp * state, axis=0)
            return (state, timed)

        lax.fori_loop(
            0, STEPS // UNROLL, step, (hfs[:, :, lane_at(grp)], hft[:, :, lane_at(grp)])
        )

    def scan_backward(grp):
        decay = a8[:, :, lane_at(grp)]
        amp = amp8[:, :, lane_at(grp)]

        def step(i, state):
            for u in range(UNROLL):
                j = STEPS - 1 - (i * UNROLL + u)
                state = decay * state + gs[grp, step_rows(j)][None]
                ys[grp, step_rows(j)] = jnp.sum(amp * state, axis=0)
            return state

        lax.fori_loop(0, STEPS // UNROLL, step, hbwd[:, :, lane_at(grp)])

    def level_copy(src, dst, send, recv, ctx):
        return pltpu.make_async_remote_copy(
            src_ref=src, dst_ref=dst, send_sem=send, recv_sem=recv,
            device_id=(ctx, t), device_id_type=MESH,
        )

    def row_copies(src, row, send, recv):
        return [
            level_copy(src, row.at[y], send.at[d], recv.at[y], ctx_of(x, (y + d) % 4, zl))
            for d in range(1, 4)
        ]

    def row_wait(src, row, send, recv):
        for d in range(1, 4):
            other = (y + d) % 4
            level_copy(src, row.at[other], send.at[d], recv.at[other], y_right).wait_recv()

    def col_copy(src, col, send, recv, xx, index):
        return level_copy(
            src, col.at[index], send.at[4 + xx], recv.at[4 + index], ctx_of(xx, y, zl)
        )

    def pair_copy(n, src, dst):
        return pltpu.make_async_remote_copy(
            src_ref=src, dst_ref=dst, send_sem=pair_s.at[n], recv_sem=pair_r.at[n],
            device_id=(z_peer, t), device_id_type=MESH,
        )

    chunk = float(ROWS)
    one_decay = jnp.exp(-rate_rows * chunk)
    two_decay = jnp.exp(-rate_rows * (2.0 * chunk))
    odd = zl == 1
    row_decay = jnp.exp(-rate_rows * (8.0 * chunk))
    zero_rows = jnp.zeros((MODES, CH), F32)

    for copy in local:
        copy.wait()
    for copy in a_init:
        copy.wait_recv()
    piece_start(0)
    row_id = lax.broadcasted_iota(jnp.int32, (ROWS, ROWS), 0)
    col_id = lax.broadcasted_iota(jnp.int32, (ROWS, ROWS), 1)
    perm[...] = jnp.where(col_id == STEPS * (row_id % SUB) + row_id // SUB, 1.0, 0.0).astype(BF16)
    perm_t[...] = jnp.where(row_id == STEPS * (col_id % SUB) + col_id // SUB, 1.0, 0.0).astype(BF16)

    loads[0].wait()
    loads[1].wait()
    signal = (k_ref[...].astype(F32) * v_ref[...].astype(F32)).astype(BF16)
    spread(xs, signal)
    run(0, GROUPS, forward_group)
    edge_rows(2 * MODES, SUB - 1)
    ebuf[...] = st2[...].astype(BF16)
    e_pair = pair_copy(0, ebuf, epeer)
    e_pair.start()
    w_first()
    piece_start(1)
    e_pair.wait_recv()
    peer = epeer[...].astype(F32)
    own = st2[...]
    first = jnp.where(odd, peer, own)
    second = jnp.where(odd, own, peer)
    first_s, first_t = first[:MODES], first[MODES:]
    esend[0:MODES] = (second[:MODES] + one_decay * first_s).astype(BF16)
    esend[MODES:] = (second[MODES:] + one_decay * (first_t + chunk * first_s)).astype(BF16)
    e_row = row_copies(esend, erow, e_s, e_r)
    for copy in e_row:
        copy.start()
    erow[y] = esend[...]
    w_second()
    piece_forward(0)

    row_wait(esend, erow, e_s, e_r)
    head_s, head_t, row_s, row_t = (zero_rows,) * 4
    for yy in range(4):
        rows = erow[yy].astype(F32)
        ahead = yy < y
        head_t = jnp.where(
            ahead, two_decay * (head_t + 2.0 * chunk * head_s) + rows[MODES:], head_t
        )
        head_s = jnp.where(ahead, two_decay * head_s + rows[:MODES], head_s)
        row_t = two_decay * (row_t + 2.0 * chunk * row_s) + rows[MODES:]
        row_s = two_decay * row_s + rows[:MODES]
    eout[0:MODES] = row_s.astype(BF16)
    eout[MODES:] = row_t.astype(BF16)
    run(x + 1, 4, lambda xx: col_copy(eout, ecol, e_s, e_r, xx, x).start())
    piece_forward(1)
    w_third()

    run(0, x, lambda xx: col_copy(eout, ecol, e_s, e_r, xx, xx).wait_recv())

    def join_forward(j, carry):
        far_s, far_t = carry
        rows = ecol[j].astype(F32)
        return (
            row_decay * far_s + rows[:MODES],
            row_decay * (far_t + 8.0 * chunk * far_s) + rows[MODES:],
        )

    far_s, far_t = lax.fori_loop(0, x, join_forward, (zero_rows, zero_rows))
    gap = y.astype(F32) * (2.0 * chunk)
    gap_decay = jnp.exp(-rate_rows * gap)
    head_s = head_s + gap_decay * far_s
    head_t = head_t + gap_decay * (far_t + gap * far_s)
    head_t = jnp.where(odd, peer[MODES:] + one_decay * (head_t + chunk * head_s), head_t)
    head_s = jnp.where(odd, peer[:MODES] + one_decay * head_s, head_s)
    for m in range(MODES):
        hd3[m] = head_s[m:m + 1, :]
        hd3[MODES + m] = head_t[m:m + 1, :]

    def incoming_forward(grp):
        ids = lax.broadcasted_iota(jnp.int32, (MODES, SUB, LANES), 1).astype(F32) * float(STEPS)
        weight = jnp.exp(-rates_at(grp) * ids)
        in_s = hd3[0:MODES, :, lane_at(grp)]
        in_t = hd3[MODES:2 * MODES, :, lane_at(grp)]
        hfs[:, :, lane_at(grp)] += weight * in_s
        hft[:, :, lane_at(grp)] += weight * (in_t + ids * in_s)

    run(0, GROUPS, incoming_forward)
    run(0, GROUPS, scan_forward)
    loads[2].wait()
    cv[...] = gather_back().astype(BF16)
    gated = (q_ref[...].astype(F32) * cv[...].astype(F32)).astype(BF16).astype(F32)
    gt[...] = jnp.transpose(gated).astype(BF16)

    rings = {}

    def add_into(ref, extra):
        ref[...] = (ref[...].astype(F32) + extra.astype(F32)).astype(BF16)
        return ref

    def part_a(part):
        return pl.ds(part * 128, 128)

    def part_b(part):
        return pl.ds(256 + part * 128, 128)

    ybase = OFF_O + 24
    bbase = OFF_O + 30
    vbase = OFF_O + 36
    along = {}

    def out_piece(k):
        yk = order[k]

        def block(j):
            op[j, yk] = jnp.dot(gt[...], ag[j, yk], preferred_element_type=F32).astype(BF16)

        run(0, 4, block)

        def unit(target, part):
            return op.at[target, yk, part_a(part)]

        base = OFF_O + 6 * k
        far_r = remote(base, unit(xo, 0), oppx.at[k, 0], x_right, t)
        far_l = remote(base + 1, unit(xo, 1), oppx.at[k, 1], x_left, t)
        rings[k] = [
            unit, far_r, far_l,
            remote(base + 2, unit(xp, 1), finx.at[k, 0, 1], x_right, t),
            remote(base + 3, unit(xm, 0), finx.at[k, 1, 0], x_left, t),
        ]

        def whole(part):
            return op.at[:, yk, part_b(part)]

        if k == 0:
            along["far_r"] = remote(bbase, whole(0), oppb.at[0], y_right, t)
            along["far_l"] = remote(bbase + 1, whole(1), oppb.at[1], y_left, t)
        elif k == 1:
            along["r1"] = remote(bbase + 2, whole(1), finb.at[0, 1], y_right, t)
        elif k == 2:
            along["l0"] = remote(bbase + 4, whole(0), finb.at[1, 0], y_left, t)

    def along_right():
        along["far_r"].wait_recv()
        ref = add_into(op.at[:, order[1], part_b(0)], oppb[0])
        along["r0"] = remote(bbase + 3, ref, finb.at[0, 0], y_right, t)

    def along_left():
        along["far_l"].wait_recv()
        ref = add_into(op.at[:, order[2], part_b(1)], oppb[1])
        along["l1"] = remote(bbase + 5, ref, finb.at[1, 1], y_left, t)

    def along_own():
        for name in ("r0", "r1", "l0", "l1"):
            along[name].wait_recv()
        for part in range(2):
            rows = slice(part * 128, (part + 1) * 128)
            vcol[:, rows] = (
                op[:, y, part_b(part)].astype(F32) + finb[0, part].astype(F32)
                + finb[1, part].astype(F32)
            ).astype(BF16)

        def unit(target, part):
            return vcol.at[target, part_a(part)]

        along["ring"] = [
            unit,
            remote(vbase, unit(xo, 0), oppv.at[0], x_right, t),
            remote(vbase + 1, unit(xo, 1), oppv.at[1], x_left, t),
            remote(vbase + 2, unit(xp, 1), finv.at[0, 1], x_right, t),
            remote(vbase + 3, unit(xm, 0), finv.at[1, 0], x_left, t),
        ]

    def along_add():
        unit, far_r, far_l = along["ring"][:3]
        far_r.wait_recv()
        ref = add_into(unit(xp, 0), oppv[0])
        along["ring"].append(remote(vbase + 4, ref, finv.at[0, 0], x_right, t))
        far_l.wait_recv()
        ref = add_into(unit(xm, 1), oppv[1])
        along["ring"].append(remote(vbase + 5, ref, finv.at[1, 1], x_left, t))

    def along_last():
        for copy in along["ring"][3:]:
            copy.wait_recv()
        for part in range(2):
            rsum[256 + part * 128:256 + (part + 1) * 128] = (
                vcol[x, part * 128:(part + 1) * 128].astype(F32) + finv[0, part].astype(F32)
                + finv[1, part].astype(F32)
            )

    def out_add(k):
        unit, far_r, far_l = rings[k][:3]
        base = OFF_O + 6 * k
        far_r.wait_recv()
        ref = add_into(unit(xp, 0), oppx[k, 0])
        rings[k].append(remote(base + 4, ref, finx.at[k, 0, 0], x_right, t))
        far_l.wait_recv()
        ref = add_into(unit(xm, 1), oppx[k, 1])
        rings[k].append(remote(base + 5, ref, finx.at[k, 1, 1], x_left, t))

    def out_sum(k):
        unit = rings[k][0]
        for copy in rings[k][3:]:
            copy.wait_recv()
        return [
            unit(x, part)[...].astype(F32) + finx[k, 0, part].astype(F32)
            + finx[k, 1, part].astype(F32)
            for part in range(2)
        ]

    second_ring = {}

    def out_first():
        parts = out_sum(0)
        for part in range(2):
            vsum[0, part] = parts[part].astype(BF16)
        second_ring["far_r"] = remote(ybase, vsum.at[0, 0], oppy.at[0], y_right, t)
        second_ring["far_l"] = remote(ybase + 1, vsum.at[0, 1], oppy.at[1], y_left, t)

    def out_second():
        parts = out_sum(1)
        vsum[1, 1] = parts[1].astype(BF16)
        second_ring["r1"] = remote(ybase + 2, vsum.at[1, 1], finy.at[0, 1], y_right, t)
        second_ring["far_r"].wait_recv()
        vsum[1, 0] = (parts[0] + oppy[0].astype(F32)).astype(BF16)
        second_ring["r0"] = remote(ybase + 3, vsum.at[1, 0], finy.at[0, 0], y_right, t)

    def out_third():
        parts = out_sum(2)
        vsum[2, 0] = parts[0].astype(BF16)
        second_ring["l0"] = remote(ybase + 4, vsum.at[2, 0], finy.at[1, 0], y_left, t)
        second_ring["far_l"].wait_recv()
        vsum[2, 1] = (parts[1] + oppy[1].astype(F32)).astype(BF16)
        second_ring["l1"] = remote(ybase + 5, vsum.at[2, 1], finy.at[1, 1], y_left, t)

    def out_last():
        parts = out_sum(3)
        for name in ("r0", "r1", "l0", "l1"):
            second_ring[name].wait_recv()
        for part in range(2):
            rsum[part * 128:(part + 1) * 128] = (
                parts[part] + finy[0, part].astype(F32) + finy[1, part].astype(F32)
            )

    dims = (((1,), (1,)), ((), ()))

    def gate_piece(k):
        yk = order[k]

        def block(j):
            gate[...] += lax.dot_general(
                ag[j, yk], wg[j, yk], dims, preferred_element_type=F32
            )

        run(0, 4, block)

    w_fourth()
    piece_pass(0)
    w_fifth()
    piece_forward(2)
    piece_wait(0)
    out_piece(0)
    piece_pass(1)
    piece_wait(1)
    out_piece(1)
    w_end()
    gate[...] = jnp.zeros_like(gate)
    gate_piece(0)
    piece_forward(3)
    piece_pass(2)
    gate_piece(1)
    out_add(0)
    piece_wait(2)
    out_piece(2)
    along_right()
    along_left()
    gate_piece(2)
    piece_pass(3)
    out_add(1)
    out_first()
    piece_wait(3)
    gate_piece(3)
    out_add(2)

    conv_grad = (gate[...] * q_ref[...].astype(F32)).astype(BF16)
    spread(gs, conv_grad)
    run(0, GROUPS, backward_group)
    edge_rows(MODES, 0)
    qbuf[...] = st2[0:MODES].astype(BF16)
    q_pair = pair_copy(1, qbuf, qpeer)
    q_pair.start()

    def gain_scan(grp):
        for part in range(2):
            mode = pl.ds(part * 8, 8)
            decay = a8[mode, :, lane_at(grp)]

            def step(i, carry):
                state, gain_sum, rate_sum = carry
                for u in range(UNROLL):
                    j = i * UNROLL + u
                    grad = gs[grp, step_rows(j)][None]
                    state = decay * state + xs[grp, step_rows(j)][None]
                    gain_sum = gain_sum + grad * state
                    rate_sum = rate_sum + grad * tkeep[grp, j, mode]
                return (state, gain_sum, rate_sum)

            zero = jnp.zeros((8, SUB, LANES), F32)
            _, gain_sum, rate_sum = lax.fori_loop(
                0, STEPS // UNROLL, step, (hfs[mode, :, lane_at(grp)], zero, zero)
            )
            scr8[grp, mode] = gain_sum
            scr8[grp, pl.ds(MODES + part * 8, 8)] = rate_sum

    def y_copy(d, index):
        other = (c + d) % NCTX
        return pltpu.make_async_remote_copy(
            src_ref=yz.at[other], dst_ref=yz_in.at[index], send_sem=y_s.at[0],
            recv_sem=y_r.at[0], device_id=(other, t), device_id_type=MESH,
        )

    def o_copy(d, index):
        other = (c + d) % NCTX
        return pltpu.make_async_remote_copy(
            src_ref=yz_all.at[c], dst_ref=yz_all.at[index], send_sem=o_s.at[0],
            recv_sem=o_r.at[0], device_id=(other, t), device_id_type=MESH,
        )

    def incoming_backward(grp):
        ids = lax.broadcasted_iota(jnp.int32, (MODES, SUB, LANES), 1).astype(F32)
        weight = jnp.exp(-rates_at(grp) * (((SUB - 1.0) - ids) * float(STEPS)))
        hbwd[:, :, lane_at(grp)] += weight * hd3[0:MODES, :, lane_at(grp)]

    run(0, 1, gain_scan)
    q_pair.wait_recv()
    peer_q = qpeer[...].astype(F32)
    own_q = st2[0:MODES]
    first_q = jnp.where(odd, peer_q, own_q)
    second_q = jnp.where(odd, own_q, peer_q)
    qsend[...] = (first_q + one_decay * second_q).astype(BF16)
    q_row = row_copies(qsend, qrow, q_s, q_r)
    for copy in q_row:
        copy.start()
    qrow[y] = qsend[...]

    gq_out[...] = (gate[...] * cv[...].astype(F32)).astype(BF16)
    out_piece(3)
    run(1, GROUPS, gain_scan)
    row_wait(qsend, qrow, q_s, q_r)
    tail, row_q = zero_rows, zero_rows
    for yy in range(3, -1, -1):
        rows = qrow[yy].astype(F32)
        tail = jnp.where(yy > y, two_decay * tail + rows, tail)
        row_q = two_decay * row_q + rows
    qout[...] = row_q.astype(BF16)
    run(0, x, lambda xx: col_copy(qout, qcol, q_s, q_r, xx, x).start())
    for grp in range(GROUPS):
        yz[:, grp] = jnp.sum(scr8[grp], axis=1)
    run(1, NCTX, lambda d: y_copy(d, c).start())
    out_second()
    along_own()
    out_add(3)
    out_third()

    run(x + 1, 4, lambda xx: col_copy(qout, qcol, q_s, q_r, xx, xx).wait_recv())
    far_q = lax.fori_loop(
        0, 3 - x, lambda j, h: row_decay * h + qcol[3 - j].astype(F32), zero_rows
    )
    tail = tail + jnp.exp(-rate_rows * ((3 - y).astype(F32) * (2.0 * chunk))) * far_q
    tail = jnp.where(odd, tail, peer_q + one_decay * tail)
    for m in range(MODES):
        hd3[m] = tail[m:m + 1, :]
    run(0, GROUPS, incoming_backward)
    run(0, 2, scan_backward)
    along_add()
    run(2, GROUPS, scan_backward)
    ig_out[...] = gather_back().astype(BF16)
    z_copies = []

    def z_start(half):
        rows = slice(half * 256, (half + 1) * 256)
        rsend[rows] = rsum[
            rows, pl.ds(pl.multiple_of((1 - zl) * 128, 128), 128)
        ].astype(BF16)
        z_copies.append(remote(
            OFF_O + 42 + half, rsend.at[pl.ds(half * 256, 256)],
            zin.at[pl.ds(half * 256, 256)], z_peer, t,
        ))

    wait_bytes(yz_in.at[pl.ds(0, NCTX - 1)], y_r.at[0])
    yz_in[c] = yz[c]
    yz_all[c] = jnp.sum(yz_in[...], axis=0)
    run(1, NCTX, lambda d: o_copy(d, c).start())
    out_last()
    z_start(0)
    along_last()
    z_start(1)

    def flush_sends():
        for copy in e_row + q_row:
            copy.wait_send()
        run(x + 1, 4, lambda xx: col_copy(eout, ecol, e_s, e_r, xx, x).wait_send())
        run(0, x, lambda xx: col_copy(qout, qcol, q_s, q_r, xx, x).wait_send())
        wait_bytes(yz.at[pl.ds(0, NCTX - 1)], y_s.at[0])
        e_pair.wait_send()
        q_pair.wait_send()
        for n, (ref, rows) in enumerate(zip((ag, wg, op), SENT_ROWS)):
            wait_bytes(ref.at[:, :, pl.ds(0, rows)], ring_s.at[n])

    flush_sends()
    for copy in z_copies:
        copy.wait_recv()
    ow_out[...] = (rsum[:, own_lanes] + zin[...].astype(F32)) * NORM

    wait_bytes(yz_all.at[pl.ds(0, NCTX - 1)], o_r.at[0])
    yz_out[...] = yz_all[...]
    wait_bytes(yz_all.at[pl.ds(0, NCTX - 1)], o_s.at[0])


def finish(
    gq_in, ow_in, ig_ref, k_ref, v_ref, sums, gain2, rate2,
    gq_out, gk_out, gv_out, gain_out, rate_out, ow_out,
):
    gq_out[...] = gq_in[...]
    ow_out[...] = ow_in[...]
    input_grad = ig_ref[...].astype(F32)
    gk_out[...] = (input_grad * v_ref[...].astype(F32)).astype(BF16)
    gv_out[...] = (input_grad * k_ref[...].astype(F32)).astype(BF16)
    rate_rows = jnp.exp(rate2[...])
    scale = NORM * jnp.sqrt(2.0 * rate_rows)
    gain_sum = jnp.concatenate([sums[0:MODES, grp] for grp in range(GROUPS)], axis=1)
    rate_sum = jnp.concatenate([sums[MODES:2 * MODES, grp] for grp in range(GROUPS)], axis=1)
    gain_out[...] = scale * gain_sum
    rate_out[...] = scale * gain2[...] * (0.5 * gain_sum - rate_rows * rate_sum)


def on_device(query_proj, key_proj, value_proj, filter_gains, log_rates, out_weight, grad_out):
    gain2 = filter_gains.T
    rate2 = log_rates.T
    vmem = pl.BlockSpec(memory_space=pltpu.VMEM)
    hbm = pl.BlockSpec(memory_space=pl.ANY)
    shape = jax.ShapeDtypeStruct
    dma = pltpu.SemaphoreType.DMA
    wide = (MODES, SUB, CH)
    gq_raw, input_grad, sums, ow_raw = pl.pallas_call(
        kernel,
        out_shape=(
            shape((ROWS, CH), BF16),
            shape((ROWS, CH), BF16),
            shape((2 * MODES, GROUPS, LANES), F32),
            shape((CH, 128), F32),
        ),
        in_specs=[hbm] * 7,
        out_specs=[vmem] * 4,
        scratch_shapes=[
            pltpu.VMEM((ROWS, CH), BF16),
            pltpu.VMEM((ROWS, CH), BF16),
            pltpu.VMEM((ROWS, CH), BF16),
            pltpu.VMEM((MODES, CH), F32),
            pltpu.VMEM((MODES, CH), F32),
            pltpu.VMEM((MODES, 1, CH), F32),
            pltpu.VMEM((GROUPS, STEPS, MODES, SUB, LANES), F32),
            pltpu.VMEM((4, 4, ROWS, 256), BF16),
            pltpu.VMEM((4, 4, CH, 256), BF16),
            pltpu.VMEM((4, 4, CH, 256), BF16),
            pltpu.VMEM((GROUPS, ROWS, LANES), F32),
            pltpu.VMEM((GROUPS, ROWS, LANES), F32),
            pltpu.VMEM((GROUPS, ROWS, LANES), F32),
            pltpu.VMEM((ROWS, ROWS), BF16),
            pltpu.VMEM((ROWS, ROWS), BF16),
            pltpu.VMEM(wide, F32),
            pltpu.VMEM(wide, F32),
            pltpu.VMEM((2 * MODES, CH), BF16),
            pltpu.VMEM((2 * MODES, CH), BF16),
            pltpu.VMEM((2 * MODES, CH), BF16),
            pltpu.VMEM((4, 2 * MODES, CH), BF16),
            pltpu.VMEM((2 * MODES, CH), BF16),
            pltpu.VMEM((4, 2 * MODES, CH), BF16),
            pltpu.VMEM((MODES, CH), BF16),
            pltpu.VMEM((MODES, CH), BF16),
            pltpu.VMEM((MODES, CH), BF16),
            pltpu.VMEM((4, MODES, CH), BF16),
            pltpu.VMEM((MODES, CH), BF16),
            pltpu.VMEM((4, MODES, CH), BF16),
            pltpu.VMEM((2 * MODES, 1, CH), F32),
            pltpu.VMEM((2 * MODES, CH), F32),
            pltpu.VMEM((GROUPS, 2 * MODES, SUB, LANES), F32),
            pltpu.VMEM(wide, F32),
            pltpu.VMEM(wide, F32),
            pltpu.VMEM(wide, F32),
            pltpu.VMEM((ROWS, CH), F32),
            pltpu.VMEM((ROWS, CH), BF16),
            pltpu.VMEM((CH, ROWS), BF16),
            pltpu.VMEM((2 * MODES, GROUPS, LANES), F32),
            pltpu.VMEM((NCTX, GROUPS, LANES), F32),
            pltpu.VMEM((NCTX, GROUPS, LANES), F32),
            pltpu.VMEM((4, 2, 128, 256), BF16),
            pltpu.VMEM((4, 2, 2, 128, 256), BF16),
            pltpu.VMEM((3, 2, 128, 256), BF16),
            pltpu.VMEM((2, 128, 256), BF16),
            pltpu.VMEM((2, 2, 128, 256), BF16),
            pltpu.VMEM((2, 4, 128, 256), BF16),
            pltpu.VMEM((2, 2, 4, 128, 256), BF16),
            pltpu.VMEM((4, 256, 256), BF16),
            pltpu.VMEM((2, 128, 256), BF16),
            pltpu.VMEM((2, 2, 128, 256), BF16),
            pltpu.VMEM((CH, 256), F32),
            pltpu.VMEM((CH, 128), BF16),
            pltpu.VMEM((CH, 128), BF16),
            dma((3,)),
            dma((N_RING,)),
            dma((8,)),
            dma((8,)),
            dma((8,)),
            dma((8,)),
            dma((1,)),
            dma((1,)),
            dma((1,)),
            dma((1,)),
            dma((2,)),
            dma((2,)),
            dma((3,)),
            dma((5,)),
        ],
        compiler_params=pltpu.CompilerParams(
            collective_id=0, has_side_effects=True, vmem_limit_bytes=56 * 1024 * 1024
        ),
        cost_estimate=pl.CostEstimate(
            flops=5_000_000_000, bytes_accessed=5_000_000, transcendentals=0
        ),
    )(
        query_proj, key_proj, value_proj, gain2, rate2, out_weight, grad_out,
    )
    grad_query, grad_key, grad_value, grad_gains, grad_rates, grad_weight = pl.pallas_call(
        finish,
        out_shape=(
            shape((ROWS, CH), BF16),
            shape((ROWS, CH), BF16),
            shape((ROWS, CH), BF16),
            shape((MODES, CH), F32),
            shape((MODES, CH), F32),
            shape((CH, 128), F32),
        ),
        in_specs=[vmem] * 8,
        out_specs=[vmem] * 6,
        compiler_params=pltpu.CompilerParams(vmem_limit_bytes=60 * 1024 * 1024),
    )(gq_raw, ow_raw, input_grad, key_proj, value_proj, sums, gain2, rate2)
    return (grad_query, grad_key, grad_value, grad_gains.T, grad_rates.T, grad_weight)


def solution(mesh):
    in_specs = (
        P("context", "tensor"),
        P("context", "tensor"),
        P("context", "tensor"),
        P("tensor", None),
        P("tensor", None),
        P("tensor", "context"),
        P("context", "tensor"),
    )
    out_specs = (
        P("context", "tensor"),
        P("context", "tensor"),
        P("context", "tensor"),
        P("tensor", None),
        P("tensor", None),
        P("tensor", "context"),
    )
    return jax.shard_map(
        on_device, mesh=mesh, in_specs=in_specs, out_specs=out_specs, check_vma=False
    )
```

```python
import math

import jax
import jax.numpy as jnp
from jax import lax
from jax.experimental import pallas as pl
from jax.experimental.pallas import tpu as pltpu
from jax.sharding import PartitionSpec as P

BF16 = jnp.bfloat16
F32 = jnp.float32
MESH = pl.DeviceIdType.MESH

NCTX = 32
ROWS = 512
CH = 512
MODES = 16
SUB = 8
STEPS = ROWS // SUB
LANES = 128
GROUPS = CH // LANES
SEQ = ROWS * NCTX
NORM = 1.0 / math.sqrt(SEQ)

N_A = 36
N_W = 45
N_O = 6 * 4 + 6 + 6 + 6 + 2
OFF_W = N_A
OFF_O = OFF_W + N_W
N_RING = OFF_O + N_O
SENT_ROWS = (448, 496, 496)
W_SPLIT = 256


def shift_sub(val, step):
    rolled = pltpu.roll(val, step % SUB, 1)
    ids = lax.broadcasted_iota(jnp.int32, val.shape, 1)
    keep = ids >= step if step > 0 else ids < SUB + step
    return jnp.where(keep, rolled, 0.0)


def kernel(
    q_in, k_in, v_in, gain_in, rate_in, w_ref, go_ref,
    gq_out, ig_out, yz_out, ow_out,
    q_ref, k_ref, v_ref, gain2, rate2, rate3, tkeep, ag, wg, op, xs, gs, ys, perm, perm_t, a8, amp8,
    ebuf, epeer, esend, erow, eout, ecol, qbuf, qpeer, qsend, qrow, qout, qcol, hd3, st2,
    scr8, hfs, hft, hbwd, gate, cv, gt, yz, yz_in, yz_all,
    oppx, finx, vsum, oppy, finy, oppb, finb, vcol, oppv, finv, rsum, rsend, zin,
    ring_s, ring_r, e_s, e_r, q_s, q_r, y_s, y_r, o_s, o_r, pair_s, pair_r, loc, io,
):
    c = lax.axis_index("context")
    t = lax.axis_index("tensor")
    x = c // 8
    y = (c // 2) % 4
    zl = c % 2
    zh = t // 2
    core = t % 2

    def ctx_of(xx, yy, zz):
        return xx * 8 + yy * 2 + zz

    xm, xp, xo = (x + 3) % 4, (x + 1) % 4, (x + 2) % 4
    ym, yp, yo = (y + 3) % 4, (y + 1) % 4, (y + 2) % 4
    zm, zp, zo = (zh + 3) % 4, (zh + 1) % 4, (zh + 2) % 4
    x_right, x_left = ctx_of(xp, y, zl), ctx_of(xm, y, zl)
    y_right, y_left = ctx_of(x, yp, zl), ctx_of(x, ym, zl)
    z_peer = ctx_of(x, y, 1 - zl)
    partner = zh * 2 + (1 - core)
    t_right, t_left = zp * 2 + core, zm * 2 + core

    def remote(index, src, dst, ctx, ten):
        copy = pltpu.make_async_remote_copy(
            src_ref=src, dst_ref=dst, send_sem=ring_s.at[(index >= OFF_W) + (index >= OFF_O)],
            recv_sem=ring_r.at[index],
            device_id=(ctx, ten), device_id_type=MESH,
        )
        copy.start()
        return copy

    def wait_bytes(ref, sem):
        pltpu.make_async_copy(ref, ref, sem).wait()

    def run(first, last, fun):
        def body(i, carry):
            fun(i)
            return carry

        lax.fori_loop(first, last, body, 0)

    barrier = pltpu.get_barrier_semaphore()

    def greet(d):
        pl.semaphore_signal(barrier, inc=1, device_id=((c + d) % NCTX, t), device_id_type=MESH)

    run(1, NCTX, greet)
    for ten in (partner, t_right, t_left):
        pl.semaphore_signal(barrier, inc=1, device_id=(c, ten), device_id_type=MESH)
    loads = [
        pltpu.make_async_copy(src, dst, io.at[n])
        for n, (src, dst) in enumerate(
            [(k_in, k_ref), (v_in, v_ref), (q_in, q_ref), (gain_in, gain2), (rate_in, rate2)]
        )
    ]
    for copy in reversed(loads):
        copy.start()

    pl.semaphore_wait(barrier, NCTX - 1 + 3)

    lane_half = [pl.ds(0, 256), pl.ds(256, 256)]
    mine, theirs = pl.multiple_of(core * 256, 256), pl.multiple_of((1 - core) * 256, 256)
    a_init = []
    for h in range(2):
        a_init.append(remote(
            h, go_ref.at[pl.ds(theirs, 256), lane_half[h]],
            ag.at[zh, core * 2 + h, pl.ds(theirs, 256)], c, partner,
        ))
    own_lanes = pl.ds(pl.multiple_of(zl * 128, 128), 128)
    wz = remote(OFF_W, w_ref, wg.at[x, y, :, own_lanes], z_peer, t)
    local = [
        pltpu.make_async_copy(
            go_ref.at[:, lane_half[h]], ag.at[zh, core * 2 + h], loc.at[h]
        )
        for h in range(2)
    ]
    local.append(pltpu.make_async_copy(w_ref, wg.at[x, y, :, own_lanes], loc.at[2]))
    for copy in local:
        copy.start()
    for h in range(2):
        a_init.append(remote(
            2 + h, go_ref.at[pl.ds(mine, 256), lane_half[h]],
            ag.at[zh, core * 2 + h, pl.ds(mine, 256)], c, partner,
        ))

    order = [yo, yp, ym, y]
    duty = pl.ds(mine, 256)
    duty_lo = pl.ds(mine, 128)
    duty_hi = pl.ds(pl.multiple_of(core * 256 + 128, 128), 128)
    piece_own, piece_fwd, piece_par = {}, {}, {}

    def piece_start(k):
        src = ag.at[zh, order[k], duty]
        base = 4 + 8 * k
        piece_own[k] = (
            remote(base, src, src, c, t_right), remote(base + 1, src, src, c, t_left)
        )

    def piece_forward(k):
        base = 4 + 8 * k
        from_left, from_right = piece_own[k]
        yk = order[k]
        from_left.wait_recv()
        lo = ag.at[zm, yk, duty_lo]
        f_r = remote(base + 2, lo, lo, c, t_right)
        full = ag.at[zm, yk, duty]
        p_l = remote(base + 4, full, full, c, partner)
        from_right.wait_recv()
        hi = ag.at[zp, yk, duty_hi]
        f_l = remote(base + 3, hi, hi, c, t_left)
        full = ag.at[zp, yk, duty]
        p_r = remote(base + 5, full, full, c, partner)
        piece_fwd[k] = (f_r, f_l)
        piece_par[k] = [p_l, p_r]
        if k + 2 < 4:
            piece_start(k + 2)

    def piece_pass(k):
        base = 4 + 8 * k
        yk = order[k]
        f_r, f_l = piece_fwd[k]
        f_r.wait_recv()
        lo = ag.at[zo, yk, duty_lo]
        p_a = remote(base + 6, lo, lo, c, partner)
        f_l.wait_recv()
        hi = ag.at[zo, yk, duty_hi]
        p_b = remote(base + 7, hi, hi, c, partner)
        piece_par[k] += [p_a, p_b]

    def piece_wait(k):
        for copy in piece_par[k]:
            copy.wait_recv()

    loads[3].wait()
    loads[4].wait()
    rate_rows = jnp.exp(rate2[...])
    decay_rows = jnp.exp(-rate_rows)
    amp_rows = gain2[...] * jnp.sqrt(2.0 * rate_rows)
    for m in range(MODES):
        rate3[m] = rate_rows[m:m + 1, :]
        a8[m] = jnp.broadcast_to(decay_rows[m:m + 1, :], (SUB, CH))
        amp8[m] = jnp.broadcast_to(amp_rows[m:m + 1, :], (SUB, CH))

    def spread(dst, natural):
        mixed = jnp.dot(perm[...], natural, preferred_element_type=F32)
        for grp in range(GROUPS):
            dst[grp] = mixed[:, grp * LANES:(grp + 1) * LANES]

    def gather_back():
        mixed = jnp.concatenate([ys[grp] for grp in range(GROUPS)], axis=1).astype(BF16)
        return jnp.dot(perm_t[...], mixed, preferred_element_type=F32)

    w0, w1 = pl.ds(0, W_SPLIT), pl.ds(W_SPLIT, CH - W_SPLIT)
    half0, half1 = W_SPLIT // 2, (CH - W_SPLIT) // 2
    w0a, w0b = pl.ds(0, half0), pl.ds(half0, half0)
    w1a, w1b = pl.ds(W_SPLIT, half1), pl.ds(W_SPLIT + half1, half1)
    wb = OFF_W + 1
    wc = {}

    def w_send(index, ref, ctx):
        return remote(wb + index, ref, ref, ctx, t)

    def w_row(b, xb):
        wc["yr", b] = w_send(4 + 4 * b, wg.at[xb, y, w0], y_right)
        wc["yl", b] = w_send(5 + 4 * b, wg.at[xb, y, w0], y_left)

    def w_row_forward(b, xb):
        wc["yr", b].wait_recv()
        wc["yfr", b] = w_send(6 + 4 * b, wg.at[xb, ym, w0a], y_right)
        wc["yl", b].wait_recv()
        wc["yfl", b] = w_send(7 + 4 * b, wg.at[xb, yp, w0b], y_left)

    def w_col(b, yb):
        wc["xr", b] = w_send(24 + 4 * b, wg.at[x, yb, w1], x_right)
        wc["xl", b] = w_send(25 + 4 * b, wg.at[x, yb, w1], x_left)

    def w_col_forward(b, yb):
        wc["xr", b].wait_recv()
        wc["xfr", b] = w_send(26 + 4 * b, wg.at[xm, yb, w1a], x_right)
        wc["xl", b].wait_recv()
        wc["xfl", b] = w_send(27 + 4 * b, wg.at[xp, yb, w1b], x_left)

    def w_early():
        for n, (rows, ctx) in enumerate(((w0, x_right), (w0, x_left), (w1, y_right), (w1, y_left))):
            wc["early", n] = remote(
                wb + 40 + n, w_ref.at[rows], wg.at[x, y, rows, own_lanes], ctx, t
            )

    def w_first():
        wz.wait_recv()
        peer_lanes = pl.ds(pl.multiple_of((1 - zl) * 128, 128), 128)
        wc["xr"] = w_send(0, wg.at[x, y, w0, peer_lanes], x_right)
        wc["xl"] = w_send(1, wg.at[x, y, w0, peer_lanes], x_left)
        wc["1r"] = w_send(20, wg.at[x, y, w1, peer_lanes], y_right)
        wc["1l"] = w_send(21, wg.at[x, y, w1, peer_lanes], y_left)
        w_row(0, x)
        w_col(0, y)

    def w_second():
        for n in range(4):
            wc["early", n].wait_recv()
        wc["xr"].wait_recv()
        wc["xfr"] = w_send(2, wg.at[xm, y, w0a], x_right)
        wc["xl"].wait_recv()
        wc["xfl"] = w_send(3, wg.at[xp, y, w0b], x_left)
        wc["1r"].wait_recv()
        wc["1fr"] = w_send(22, wg.at[x, ym, w1a], y_right)
        wc["1l"].wait_recv()
        wc["1fl"] = w_send(23, wg.at[x, yp, w1b], y_left)
        w_row(1, xm)
        w_col(1, ym)
        w_row(2, xp)
        w_col(2, yp)

    def w_third():
        wc["1fr"].wait_recv()
        wc["1fl"].wait_recv()
        wc["xfr"].wait_recv()
        wc["xfl"].wait_recv()
        w_row(3, xo)
        w_col(3, yo)
        w_row_forward(0, x)
        w_col_forward(0, y)

    def w_fourth():
        w_row_forward(1, xm)
        w_col_forward(1, ym)
        w_row_forward(2, xp)
        w_col_forward(2, yp)

    def w_fifth():
        w_row_forward(3, xo)
        w_col_forward(3, yo)

    def w_end():
        for b in range(4):
            for name in ("yfr", "yfl", "xfr", "xfl"):
                wc[name, b].wait_recv()

    w_early()

    def lane_at(grp):
        return pl.ds(pl.multiple_of(grp * LANES, LANES), LANES)

    def step_rows(j):
        return pl.ds(pl.multiple_of(j * SUB, SUB), SUB)

    def rates_at(grp):
        return rate3[:, :, lane_at(grp)]

    UNROLL = 4

    def forward_group(grp):
        decay = a8[:, :, lane_at(grp)]

        def step(i, carry):
            state, timed = carry
            for u in range(UNROLL):
                decayed = decay * state
                timed = decay * timed + decayed
                state = decayed + xs[grp, step_rows(i * UNROLL + u)][None]
            return (state, timed)

        zero = jnp.zeros((MODES, SUB, LANES), F32)
        state, timed = lax.fori_loop(0, STEPS // UNROLL, step, (zero, zero))
        rates = rates_at(grp)
        for power in (1, 2, 4):
            factor = jnp.exp(-rates * float(STEPS * power))
            before = shift_sub(state, power)
            timed = timed + factor * (shift_sub(timed, power) + float(STEPS * power) * before)
            state = state + factor * before
        hfs[:, :, lane_at(grp)] = shift_sub(state, 1)
        hft[:, :, lane_at(grp)] = shift_sub(timed, 1)
        scr8[grp, 0:MODES] = state
        scr8[grp, MODES:2 * MODES] = timed

    def backward_group(grp):
        decay = a8[:, :, lane_at(grp)]

        def step(i, state):
            for u in range(UNROLL):
                j = STEPS - 1 - (i * UNROLL + u)
                state = decay * state + gs[grp, step_rows(j)][None]
            return state

        state = lax.fori_loop(0, STEPS // UNROLL, step, jnp.zeros((MODES, SUB, LANES), F32))
        rates = rates_at(grp)
        for power in (1, 2, 4):
            factor = jnp.exp(-rates * float(STEPS * power))
            state = state + factor * shift_sub(state, -power)
        hbwd[:, :, lane_at(grp)] = shift_sub(state, -1)
        scr8[grp, 0:MODES] = state

    def edge_rows(count, edge):
        for grp in range(GROUPS):
            for m in range(count):
                st2[m:m + 1, grp * LANES:(grp + 1) * LANES] = scr8[grp, m, edge:edge + 1, :]

    def scan_forward(grp):
        decay = a8[:, :, lane_at(grp)]
        amp = amp8[:, :, lane_at(grp)]

        def step(i, carry):
            state, timed = carry
            for u in range(UNROLL):
                j = i * UNROLL + u
                decayed = decay * state
                timed = decay * timed + decayed
                state = decayed + xs[grp, step_rows(j)][None]
                tkeep[grp, j] = timed
                ys[grp, step_rows(j)] = jnp.sum(amp * state, axis=0)
            return (state, timed)

        lax.fori_loop(
            0, STEPS // UNROLL, step, (hfs[:, :, lane_at(grp)], hft[:, :, lane_at(grp)])
        )

    def scan_backward(grp):
        decay = a8[:, :, lane_at(grp)]
        amp = amp8[:, :, lane_at(grp)]

        def step(i, state):
            for u in range(UNROLL):
                j = STEPS - 1 - (i * UNROLL + u)
                state = decay * state + gs[grp, step_rows(j)][None]
                ys[grp, step_rows(j)] = jnp.sum(amp * state, axis=0)
            return state

        lax.fori_loop(0, STEPS // UNROLL, step, hbwd[:, :, lane_at(grp)])

    def level_copy(src, dst, send, recv, ctx):
        return pltpu.make_async_remote_copy(
            src_ref=src, dst_ref=dst, send_sem=send, recv_sem=recv,
            device_id=(ctx, t), device_id_type=MESH,
        )

    def row_copies(src, row, send, recv):
        return [
            level_copy(src, row.at[y], send.at[d], recv.at[y], ctx_of(x, (y + d) % 4, zl))
            for d in range(1, 4)
        ]

    def row_wait(src, row, send, recv):
        for d in range(1, 4):
            other = (y + d) % 4
            level_copy(src, row.at[other], send.at[d], recv.at[other], y_right).wait_recv()

    def col_copy(src, col, send, recv, xx, index):
        return level_copy(
            src, col.at[index], send.at[4 + xx], recv.at[4 + index], ctx_of(xx, y, zl)
        )

    def pair_copy(n, src, dst):
        return pltpu.make_async_remote_copy(
            src_ref=src, dst_ref=dst, send_sem=pair_s.at[n], recv_sem=pair_r.at[n],
            device_id=(z_peer, t), device_id_type=MESH,
        )

    chunk = float(ROWS)
    one_decay = jnp.exp(-rate_rows * chunk)
    two_decay = jnp.exp(-rate_rows * (2.0 * chunk))
    odd = zl == 1
    row_decay = jnp.exp(-rate_rows * (8.0 * chunk))
    zero_rows = jnp.zeros((MODES, CH), F32)

    for copy in local:
        copy.wait()
    for copy in a_init:
        copy.wait_recv()
    piece_start(0)
    row_id = lax.broadcasted_iota(jnp.int32, (ROWS, ROWS), 0)
    col_id = lax.broadcasted_iota(jnp.int32, (ROWS, ROWS), 1)
    perm[...] = jnp.where(col_id == STEPS * (row_id % SUB) + row_id // SUB, 1.0, 0.0).astype(BF16)
    perm_t[...] = jnp.where(row_id == STEPS * (col_id % SUB) + col_id // SUB, 1.0, 0.0).astype(BF16)

    loads[0].wait()
    loads[1].wait()
    signal = (k_ref[...].astype(F32) * v_ref[...].astype(F32)).astype(BF16)
    spread(xs, signal)
    run(0, GROUPS, forward_group)
    edge_rows(2 * MODES, SUB - 1)
    ebuf[...] = st2[...].astype(BF16)
    e_pair = pair_copy(0, ebuf, epeer)
    e_pair.start()
    w_first()
    piece_start(1)
    e_pair.wait_recv()
    peer = epeer[...].astype(F32)
    own = st2[...]
    first = jnp.where(odd, peer, own)
    second = jnp.where(odd, own, peer)
    first_s, first_t = first[:MODES], first[MODES:]
    esend[0:MODES] = (second[:MODES] + one_decay * first_s).astype(BF16)
    esend[MODES:] = (second[MODES:] + one_decay * (first_t + chunk * first_s)).astype(BF16)
    e_row = row_copies(esend, erow, e_s, e_r)
    for copy in e_row:
        copy.start()
    erow[y] = esend[...]
    w_second()
    piece_forward(0)

    row_wait(esend, erow, e_s, e_r)
    head_s, head_t, row_s, row_t = (zero_rows,) * 4
    for yy in range(4):
        rows = erow[yy].astype(F32)
        ahead = yy < y
        head_t = jnp.where(
            ahead, two_decay * (head_t + 2.0 * chunk * head_s) + rows[MODES:], head_t
        )
        head_s = jnp.where(ahead, two_decay * head_s + rows[:MODES], head_s)
        row_t = two_decay * (row_t + 2.0 * chunk * row_s) + rows[MODES:]
        row_s = two_decay * row_s + rows[:MODES]
    eout[0:MODES] = row_s.astype(BF16)
    eout[MODES:] = row_t.astype(BF16)
    run(x + 1, 4, lambda xx: col_copy(eout, ecol, e_s, e_r, xx, x).start())
    piece_forward(1)
    w_third()

    run(0, x, lambda xx: col_copy(eout, ecol, e_s, e_r, xx, xx).wait_recv())

    def join_forward(j, carry):
        far_s, far_t = carry
        rows = ecol[j].astype(F32)
        return (
            row_decay * far_s + rows[:MODES],
            row_decay * (far_t + 8.0 * chunk * far_s) + rows[MODES:],
        )

    far_s, far_t = lax.fori_loop(0, x, join_forward, (zero_rows, zero_rows))
    gap = y.astype(F32) * (2.0 * chunk)
    gap_decay = jnp.exp(-rate_rows * gap)
    head_s = head_s + gap_decay * far_s
    head_t = head_t + gap_decay * (far_t + gap * far_s)
    head_t = jnp.where(odd, peer[MODES:] + one_decay * (head_t + chunk * head_s), head_t)
    head_s = jnp.where(odd, peer[:MODES] + one_decay * head_s, head_s)
    for m in range(MODES):
        hd3[m] = head_s[m:m + 1, :]
        hd3[MODES + m] = head_t[m:m + 1, :]

    def incoming_forward(grp):
        ids = lax.broadcasted_iota(jnp.int32, (MODES, SUB, LANES), 1).astype(F32) * float(STEPS)
        weight = jnp.exp(-rates_at(grp) * ids)
        in_s = hd3[0:MODES, :, lane_at(grp)]
        in_t = hd3[MODES:2 * MODES, :, lane_at(grp)]
        hfs[:, :, lane_at(grp)] += weight * in_s
        hft[:, :, lane_at(grp)] += weight * (in_t + ids * in_s)

    run(0, GROUPS, incoming_forward)
    run(0, GROUPS, scan_forward)
    loads[2].wait()
    cv[...] = gather_back().astype(BF16)
    gated = (q_ref[...].astype(F32) * cv[...].astype(F32)).astype(BF16).astype(F32)
    gt[...] = jnp.transpose(gated).astype(BF16)

    rings = {}

    def add_into(ref, extra):
        ref[...] = (ref[...].astype(F32) + extra.astype(F32)).astype(BF16)
        return ref

    def part_a(part):
        return pl.ds(part * 128, 128)

    def part_b(part):
        return pl.ds(256 + part * 128, 128)

    ybase = OFF_O + 24
    bbase = OFF_O + 30
    vbase = OFF_O + 36
    along = {}

    def out_piece(k):
        yk = order[k]

        def block(j):
            op[j, yk] = jnp.dot(gt[...], ag[j, yk], preferred_element_type=F32).astype(BF16)

        run(0, 4, block)

        def unit(target, part):
            return op.at[target, yk, part_a(part)]

        base = OFF_O + 6 * k
        far_r = remote(base, unit(xo, 0), oppx.at[k, 0], x_right, t)
        far_l = remote(base + 1, unit(xo, 1), oppx.at[k, 1], x_left, t)
        rings[k] = [
            unit, far_r, far_l,
            remote(base + 2, unit(xp, 1), finx.at[k, 0, 1], x_right, t),
            remote(base + 3, unit(xm, 0), finx.at[k, 1, 0], x_left, t),
        ]

        def whole(part):
            return op.at[:, yk, part_b(part)]

        if k == 0:
            along["far_r"] = remote(bbase, whole(0), oppb.at[0], y_right, t)
            along["far_l"] = remote(bbase + 1, whole(1), oppb.at[1], y_left, t)
        elif k == 1:
            along["r1"] = remote(bbase + 2, whole(1), finb.at[0, 1], y_right, t)
        elif k == 2:
            along["l0"] = remote(bbase + 4, whole(0), finb.at[1, 0], y_left, t)

    def along_right():
        along["far_r"].wait_recv()
        ref = add_into(op.at[:, order[1], part_b(0)], oppb[0])
        along["r0"] = remote(bbase + 3, ref, finb.at[0, 0], y_right, t)

    def along_left():
        along["far_l"].wait_recv()
        ref = add_into(op.at[:, order[2], part_b(1)], oppb[1])
        along["l1"] = remote(bbase + 5, ref, finb.at[1, 1], y_left, t)

    def along_own():
        for name in ("r0", "r1", "l0", "l1"):
            along[name].wait_recv()
        for part in range(2):
            rows = slice(part * 128, (part + 1) * 128)
            vcol[:, rows] = (
                op[:, y, part_b(part)].astype(F32) + finb[0, part].astype(F32)
                + finb[1, part].astype(F32)
            ).astype(BF16)

        def unit(target, part):
            return vcol.at[target, part_a(part)]

        along["ring"] = [
            unit,
            remote(vbase, unit(xo, 0), oppv.at[0], x_right, t),
            remote(vbase + 1, unit(xo, 1), oppv.at[1], x_left, t),
            remote(vbase + 2, unit(xp, 1), finv.at[0, 1], x_right, t),
            remote(vbase + 3, unit(xm, 0), finv.at[1, 0], x_left, t),
        ]

    def along_add():
        unit, far_r, far_l = along["ring"][:3]
        far_r.wait_recv()
        ref = add_into(unit(xp, 0), oppv[0])
        along["ring"].append(remote(vbase + 4, ref, finv.at[0, 0], x_right, t))
        far_l.wait_recv()
        ref = add_into(unit(xm, 1), oppv[1])
        along["ring"].append(remote(vbase + 5, ref, finv.at[1, 1], x_left, t))

    def along_last():
        for copy in along["ring"][3:]:
            copy.wait_recv()
        for part in range(2):
            rsum[256 + part * 128:256 + (part + 1) * 128] = (
                vcol[x, part * 128:(part + 1) * 128].astype(F32) + finv[0, part].astype(F32)
                + finv[1, part].astype(F32)
            )

    def out_add(k):
        unit, far_r, far_l = rings[k][:3]
        base = OFF_O + 6 * k
        far_r.wait_recv()
        ref = add_into(unit(xp, 0), oppx[k, 0])
        rings[k].append(remote(base + 4, ref, finx.at[k, 0, 0], x_right, t))
        far_l.wait_recv()
        ref = add_into(unit(xm, 1), oppx[k, 1])
        rings[k].append(remote(base + 5, ref, finx.at[k, 1, 1], x_left, t))

    def out_sum(k):
        unit = rings[k][0]
        for copy in rings[k][3:]:
            copy.wait_recv()
        return [
            unit(x, part)[...].astype(F32) + finx[k, 0, part].astype(F32)
            + finx[k, 1, part].astype(F32)
            for part in range(2)
        ]

    second_ring = {}

    def out_first():
        parts = out_sum(0)
        for part in range(2):
            vsum[0, part] = parts[part].astype(BF16)
        second_ring["far_r"] = remote(ybase, vsum.at[0, 0], oppy.at[0], y_right, t)
        second_ring["far_l"] = remote(ybase + 1, vsum.at[0, 1], oppy.at[1], y_left, t)

    def out_second():
        parts = out_sum(1)
        vsum[1, 1] = parts[1].astype(BF16)
        second_ring["r1"] = remote(ybase + 2, vsum.at[1, 1], finy.at[0, 1], y_right, t)
        second_ring["far_r"].wait_recv()
        vsum[1, 0] = (parts[0] + oppy[0].astype(F32)).astype(BF16)
        second_ring["r0"] = remote(ybase + 3, vsum.at[1, 0], finy.at[0, 0], y_right, t)

    def out_third():
        parts = out_sum(2)
        vsum[2, 0] = parts[0].astype(BF16)
        second_ring["l0"] = remote(ybase + 4, vsum.at[2, 0], finy.at[1, 0], y_left, t)
        second_ring["far_l"].wait_recv()
        vsum[2, 1] = (parts[1] + oppy[1].astype(F32)).astype(BF16)
        second_ring["l1"] = remote(ybase + 5, vsum.at[2, 1], finy.at[1, 1], y_left, t)

    def out_last():
        parts = out_sum(3)
        for name in ("r0", "r1", "l0", "l1"):
            second_ring[name].wait_recv()
        for part in range(2):
            rsum[part * 128:(part + 1) * 128] = (
                parts[part] + finy[0, part].astype(F32) + finy[1, part].astype(F32)
            )

    dims = (((1,), (1,)), ((), ()))

    def gate_piece(k):
        yk = order[k]

        def block(j):
            gate[...] += lax.dot_general(
                ag[j, yk], wg[j, yk], dims, preferred_element_type=F32
            )

        run(0, 4, block)

    w_fourth()
    piece_pass(0)
    w_fifth()
    piece_forward(2)
    piece_wait(0)
    out_piece(0)
    piece_pass(1)
    piece_wait(1)
    out_piece(1)
    w_end()
    gate[...] = jnp.zeros_like(gate)
    gate_piece(0)
    piece_forward(3)
    piece_pass(2)
    gate_piece(1)
    out_add(0)
    piece_wait(2)
    out_piece(2)
    along_right()
    along_left()
    gate_piece(2)
    piece_pass(3)
    out_add(1)
    out_first()
    piece_wait(3)
    gate_piece(3)
    out_add(2)

    conv_grad = (gate[...] * q_ref[...].astype(F32)).astype(BF16)
    spread(gs, conv_grad)
    run(0, GROUPS, backward_group)
    edge_rows(MODES, 0)
    qbuf[...] = st2[0:MODES].astype(BF16)
    q_pair = pair_copy(1, qbuf, qpeer)
    q_pair.start()

    def gain_scan(grp):
        for part in range(2):
            mode = pl.ds(part * 8, 8)
            decay = a8[mode, :, lane_at(grp)]

            def step(i, carry):
                state, gain_sum, rate_sum = carry
                for u in range(UNROLL):
                    j = i * UNROLL + u
                    grad = gs[grp, step_rows(j)][None]
                    state = decay * state + xs[grp, step_rows(j)][None]
                    gain_sum = gain_sum + grad * state
                    rate_sum = rate_sum + grad * tkeep[grp, j, mode]
                return (state, gain_sum, rate_sum)

            zero = jnp.zeros((8, SUB, LANES), F32)
            _, gain_sum, rate_sum = lax.fori_loop(
                0, STEPS // UNROLL, step, (hfs[mode, :, lane_at(grp)], zero, zero)
            )
            scr8[grp, mode] = gain_sum
            scr8[grp, pl.ds(MODES + part * 8, 8)] = rate_sum

    def y_copy(d, index):
        other = (c + d) % NCTX
        return pltpu.make_async_remote_copy(
            src_ref=yz.at[other], dst_ref=yz_in.at[index], send_sem=y_s.at[0],
            recv_sem=y_r.at[0], device_id=(other, t), device_id_type=MESH,
        )

    def o_copy(d, index):
        other = (c + d) % NCTX
        return pltpu.make_async_remote_copy(
            src_ref=yz_all.at[c], dst_ref=yz_all.at[index], send_sem=o_s.at[0],
            recv_sem=o_r.at[0], device_id=(other, t), device_id_type=MESH,
        )

    def incoming_backward(grp):
        ids = lax.broadcasted_iota(jnp.int32, (MODES, SUB, LANES), 1).astype(F32)
        weight = jnp.exp(-rates_at(grp) * (((SUB - 1.0) - ids) * float(STEPS)))
        hbwd[:, :, lane_at(grp)] += weight * hd3[0:MODES, :, lane_at(grp)]

    run(0, 1, gain_scan)
    q_pair.wait_recv()
    peer_q = qpeer[...].astype(F32)
    own_q = st2[0:MODES]
    first_q = jnp.where(odd, peer_q, own_q)
    second_q = jnp.where(odd, own_q, peer_q)
    qsend[...] = (first_q + one_decay * second_q).astype(BF16)
    q_row = row_copies(qsend, qrow, q_s, q_r)
    for copy in q_row:
        copy.start()
    qrow[y] = qsend[...]

    gq_out[...] = (gate[...] * cv[...].astype(F32)).astype(BF16)
    out_piece(3)
    run(1, 2, gain_scan)
    along_own()
    run(2, GROUPS, gain_scan)
    row_wait(qsend, qrow, q_s, q_r)
    tail, row_q = zero_rows, zero_rows
    for yy in range(3, -1, -1):
        rows = qrow[yy].astype(F32)
        tail = jnp.where(yy > y, two_decay * tail + rows, tail)
        row_q = two_decay * row_q + rows
    qout[...] = row_q.astype(BF16)
    run(0, x, lambda xx: col_copy(qout, qcol, q_s, q_r, xx, x).start())
    for grp in range(GROUPS):
        yz[:, grp] = jnp.sum(scr8[grp], axis=1)
    run(1, NCTX, lambda d: y_copy(d, c).start())
    out_second()
    out_add(3)
    out_third()

    run(x + 1, 4, lambda xx: col_copy(qout, qcol, q_s, q_r, xx, xx).wait_recv())
    far_q = lax.fori_loop(
        0, 3 - x, lambda j, h: row_decay * h + qcol[3 - j].astype(F32), zero_rows
    )
    tail = tail + jnp.exp(-rate_rows * ((3 - y).astype(F32) * (2.0 * chunk))) * far_q
    tail = jnp.where(odd, tail, peer_q + one_decay * tail)
    for m in range(MODES):
        hd3[m] = tail[m:m + 1, :]
    run(0, GROUPS, incoming_backward)
    run(0, 1, scan_backward)
    along_add()
    run(1, 3, scan_backward)
    wait_bytes(yz_in.at[pl.ds(0, NCTX - 1)], y_r.at[0])
    yz_in[c] = yz[c]
    yz_all[c] = jnp.sum(yz_in[...], axis=0)
    run(1, NCTX, lambda d: o_copy(d, c).start())
    run(3, GROUPS, scan_backward)
    z_copies = []

    def z_start(half):
        rows = slice(half * 256, (half + 1) * 256)
        rsend[rows] = rsum[
            rows, pl.ds(pl.multiple_of((1 - zl) * 128, 128), 128)
        ].astype(BF16)
        z_copies.append(remote(
            OFF_O + 42 + half, rsend.at[pl.ds(half * 256, 256)],
            zin.at[pl.ds(half * 256, 256)], z_peer, t,
        ))

    out_last()
    z_start(0)
    along_last()
    z_start(1)
    ig_out[...] = gather_back().astype(BF16)

    def flush_sends():
        for copy in e_row + q_row:
            copy.wait_send()
        run(x + 1, 4, lambda xx: col_copy(eout, ecol, e_s, e_r, xx, x).wait_send())
        run(0, x, lambda xx: col_copy(qout, qcol, q_s, q_r, xx, x).wait_send())
        wait_bytes(yz.at[pl.ds(0, NCTX - 1)], y_s.at[0])
        e_pair.wait_send()
        q_pair.wait_send()
        for n, (ref, rows) in enumerate(zip((ag, wg, op), SENT_ROWS)):
            wait_bytes(ref.at[:, :, pl.ds(0, rows)], ring_s.at[n])

    flush_sends()
    for copy in z_copies:
        copy.wait_recv()
    ow_out[...] = (rsum[:, own_lanes] + zin[...].astype(F32)) * NORM

    wait_bytes(yz_all.at[pl.ds(0, NCTX - 1)], o_r.at[0])
    yz_out[...] = yz_all[...]
    wait_bytes(yz_all.at[pl.ds(0, NCTX - 1)], o_s.at[0])


def finish(
    gq_in, ow_in, ig_ref, k_ref, v_ref, sums, gain2, rate2,
    gq_out, gk_out, gv_out, gain_out, rate_out, ow_out,
):
    gq_out[...] = gq_in[...]
    ow_out[...] = ow_in[...]
    input_grad = ig_ref[...].astype(F32)
    gk_out[...] = (input_grad * v_ref[...].astype(F32)).astype(BF16)
    gv_out[...] = (input_grad * k_ref[...].astype(F32)).astype(BF16)
    rate_rows = jnp.exp(rate2[...])
    scale = NORM * jnp.sqrt(2.0 * rate_rows)
    gain_sum = jnp.concatenate([sums[0:MODES, grp] for grp in range(GROUPS)], axis=1)
    rate_sum = jnp.concatenate([sums[MODES:2 * MODES, grp] for grp in range(GROUPS)], axis=1)
    gain_out[...] = scale * gain_sum
    rate_out[...] = scale * gain2[...] * (0.5 * gain_sum - rate_rows * rate_sum)


def on_device(query_proj, key_proj, value_proj, filter_gains, log_rates, out_weight, grad_out):
    gain2 = filter_gains.T
    rate2 = log_rates.T
    vmem = pl.BlockSpec(memory_space=pltpu.VMEM)
    hbm = pl.BlockSpec(memory_space=pl.ANY)
    shape = jax.ShapeDtypeStruct
    dma = pltpu.SemaphoreType.DMA
    wide = (MODES, SUB, CH)
    gq_raw, input_grad, sums, ow_raw = pl.pallas_call(
        kernel,
        out_shape=(
            shape((ROWS, CH), BF16),
            shape((ROWS, CH), BF16),
            shape((2 * MODES, GROUPS, LANES), F32),
            shape((CH, 128), F32),
        ),
        in_specs=[hbm] * 7,
        out_specs=[vmem] * 4,
        scratch_shapes=[
            pltpu.VMEM((ROWS, CH), BF16),
            pltpu.VMEM((ROWS, CH), BF16),
            pltpu.VMEM((ROWS, CH), BF16),
            pltpu.VMEM((MODES, CH), F32),
            pltpu.VMEM((MODES, CH), F32),
            pltpu.VMEM((MODES, 1, CH), F32),
            pltpu.VMEM((GROUPS, STEPS, MODES, SUB, LANES), F32),
            pltpu.VMEM((4, 4, ROWS, 256), BF16),
            pltpu.VMEM((4, 4, CH, 256), BF16),
            pltpu.VMEM((4, 4, CH, 256), BF16),
            pltpu.VMEM((GROUPS, ROWS, LANES), F32),
            pltpu.VMEM((GROUPS, ROWS, LANES), F32),
            pltpu.VMEM((GROUPS, ROWS, LANES), F32),
            pltpu.VMEM((ROWS, ROWS), BF16),
            pltpu.VMEM((ROWS, ROWS), BF16),
            pltpu.VMEM(wide, F32),
            pltpu.VMEM(wide, F32),
            pltpu.VMEM((2 * MODES, CH), BF16),
            pltpu.VMEM((2 * MODES, CH), BF16),
            pltpu.VMEM((2 * MODES, CH), BF16),
            pltpu.VMEM((4, 2 * MODES, CH), BF16),
            pltpu.VMEM((2 * MODES, CH), BF16),
            pltpu.VMEM((4, 2 * MODES, CH), BF16),
            pltpu.VMEM((MODES, CH), BF16),
            pltpu.VMEM((MODES, CH), BF16),
            pltpu.VMEM((MODES, CH), BF16),
            pltpu.VMEM((4, MODES, CH), BF16),
            pltpu.VMEM((MODES, CH), BF16),
            pltpu.VMEM((4, MODES, CH), BF16),
            pltpu.VMEM((2 * MODES, 1, CH), F32),
            pltpu.VMEM((2 * MODES, CH), F32),
            pltpu.VMEM((GROUPS, 2 * MODES, SUB, LANES), F32),
            pltpu.VMEM(wide, F32),
            pltpu.VMEM(wide, F32),
            pltpu.VMEM(wide, F32),
            pltpu.VMEM((ROWS, CH), F32),
            pltpu.VMEM((ROWS, CH), BF16),
            pltpu.VMEM((CH, ROWS), BF16),
            pltpu.VMEM((2 * MODES, GROUPS, LANES), F32),
            pltpu.VMEM((NCTX, GROUPS, LANES), F32),
            pltpu.VMEM((NCTX, GROUPS, LANES), F32),
            pltpu.VMEM((4, 2, 128, 256), BF16),
            pltpu.VMEM((4, 2, 2, 128, 256), BF16),
            pltpu.VMEM((3, 2, 128, 256), BF16),
            pltpu.VMEM((2, 128, 256), BF16),
            pltpu.VMEM((2, 2, 128, 256), BF16),
            pltpu.VMEM((2, 4, 128, 256), BF16),
            pltpu.VMEM((2, 2, 4, 128, 256), BF16),
            pltpu.VMEM((4, 256, 256), BF16),
            pltpu.VMEM((2, 128, 256), BF16),
            pltpu.VMEM((2, 2, 128, 256), BF16),
            pltpu.VMEM((CH, 256), F32),
            pltpu.VMEM((CH, 128), BF16),
            pltpu.VMEM((CH, 128), BF16),
            dma((3,)),
            dma((N_RING,)),
            dma((8,)),
            dma((8,)),
            dma((8,)),
            dma((8,)),
            dma((1,)),
            dma((1,)),
            dma((1,)),
            dma((1,)),
            dma((2,)),
            dma((2,)),
            dma((3,)),
            dma((5,)),
        ],
        compiler_params=pltpu.CompilerParams(
            collective_id=0, has_side_effects=True, vmem_limit_bytes=56 * 1024 * 1024
        ),
        cost_estimate=pl.CostEstimate(
            flops=5_000_000_000, bytes_accessed=5_000_000, transcendentals=0
        ),
    )(
        query_proj, key_proj, value_proj, gain2, rate2, out_weight, grad_out,
    )
    grad_query, grad_key, grad_value, grad_gains, grad_rates, grad_weight = pl.pallas_call(
        finish,
        out_shape=(
            shape((ROWS, CH), BF16),
            shape((ROWS, CH), BF16),
            shape((ROWS, CH), BF16),
            shape((MODES, CH), F32),
            shape((MODES, CH), F32),
            shape((CH, 128), F32),
        ),
        in_specs=[vmem] * 8,
        out_specs=[vmem] * 6,
        compiler_params=pltpu.CompilerParams(vmem_limit_bytes=60 * 1024 * 1024),
    )(gq_raw, ow_raw, input_grad, key_proj, value_proj, sums, gain2, rate2)
    return (grad_query, grad_key, grad_value, grad_gains.T, grad_rates.T, grad_weight)


def solution(mesh):
    in_specs = (
        P("context", "tensor"),
        P("context", "tensor"),
        P("context", "tensor"),
        P("tensor", None),
        P("tensor", None),
        P("tensor", "context"),
        P("context", "tensor"),
    )
    out_specs = (
        P("context", "tensor"),
        P("context", "tensor"),
        P("context", "tensor"),
        P("tensor", None),
        P("tensor", None),
        P("tensor", "context"),
    )
    return jax.shard_map(
        on_device, mesh=mesh, in_specs=in_specs, out_specs=out_specs, check_vma=False
    )
```

```python
import math

import jax
import jax.numpy as jnp
from jax import lax
from jax.experimental import pallas as pl
from jax.experimental.pallas import tpu as pltpu
from jax.sharding import PartitionSpec as P

BF16 = jnp.bfloat16
F32 = jnp.float32
MESH = pl.DeviceIdType.MESH

NCTX = 32
ROWS = 512
CH = 512
MODES = 16
SUB = 8
STEPS = ROWS // SUB
LANES = 128
GROUPS = CH // LANES
SEQ = ROWS * NCTX
NORM = 1.0 / math.sqrt(SEQ)

N_A = 36
N_W = 45
N_O = 6 * 4 + 6 + 6 + 6 + 2
OFF_W = N_A
OFF_O = OFF_W + N_W
N_RING = OFF_O + N_O
N_RECV = N_RING - 12 - 15 - 12 - 9
SENT_ROWS = (448, 496, 496)
W_SPLIT = 256


def shift_sub(val, step):
    rolled = pltpu.roll(val, step % SUB, 1)
    ids = lax.broadcasted_iota(jnp.int32, val.shape, 1)
    keep = ids >= step if step > 0 else ids < SUB + step
    return jnp.where(keep, rolled, 0.0)


def kernel(
    q_in, k_in, v_in, gain_in, rate_in, w_ref, go_ref,
    gq_out, ig_out, yz_out, ow_out,
    q_ref, k_ref, v_ref, gain2, rate2, gq_buf, ig_buf, ow_buf, rate3, tkeep, ag, wg, op, xs, gs, ys, perm, perm_t, a8, amp8,
    ebuf, epeer, esend, erow, eout, ecol, qbuf, qpeer, qsend, qrow, qout, qcol, hd3, st2,
    scr8, hfs, hft, hbwd, gate, cv, gt, yz, yz_in, yz_all,
    oppx, finx, vsum, oppy, finy, oppb, finb, vcol, oppv, finv, rsum, rsend, zin,
    ring_s, ring_r, e_s, e_r, q_s, q_r, y_s, y_r, o_s, o_r, pair_s, pair_r, loc, io,
):
    c = lax.axis_index("context")
    t = lax.axis_index("tensor")
    x = c // 8
    y = (c // 2) % 4
    zl = c % 2
    zh = t // 2
    core = t % 2

    def ctx_of(xx, yy, zz):
        return xx * 8 + yy * 2 + zz

    xm, xp, xo = (x + 3) % 4, (x + 1) % 4, (x + 2) % 4
    ym, yp, yo = (y + 3) % 4, (y + 1) % 4, (y + 2) % 4
    zm, zp, zo = (zh + 3) % 4, (zh + 1) % 4, (zh + 2) % 4
    x_right, x_left = ctx_of(xp, y, zl), ctx_of(xm, y, zl)
    y_right, y_left = ctx_of(x, yp, zl), ctx_of(x, ym, zl)
    z_peer = ctx_of(x, y, 1 - zl)
    partner = zh * 2 + (1 - core)
    t_right, t_left = zp * 2 + core, zm * 2 + core

    ids = {}

    def recv_sem(key):
        return ring_r.at[ids.setdefault(key, len(ids))]

    def remote(index, src, dst, ctx, ten, share=None):
        copy = pltpu.make_async_remote_copy(
            src_ref=src, dst_ref=dst, send_sem=ring_s.at[(index >= OFF_W) + (index >= OFF_O)],
            recv_sem=recv_sem(index if share is None else share),
            device_id=(ctx, ten), device_id_type=MESH,
        )
        copy.start()
        return copy

    def wait_bytes(ref, sem):
        pltpu.make_async_copy(ref, ref, sem).wait()

    def run(first, last, fun):
        def body(i, carry):
            fun(i)
            return carry

        lax.fori_loop(first, last, body, 0)

    barrier = pltpu.get_barrier_semaphore()

    def greet(d):
        pl.semaphore_signal(barrier, inc=1, device_id=((c + d) % NCTX, t), device_id_type=MESH)

    run(1, NCTX, greet)
    for ten in (partner, t_right, t_left):
        pl.semaphore_signal(barrier, inc=1, device_id=(c, ten), device_id_type=MESH)
    loads = [
        pltpu.make_async_copy(src, dst, io.at[n])
        for n, (src, dst) in enumerate(
            [(k_in, k_ref), (v_in, v_ref), (q_in, q_ref), (gain_in, gain2), (rate_in, rate2)]
        )
    ]
    for copy in reversed(loads):
        copy.start()

    pl.semaphore_wait(barrier, NCTX - 1 + 3)

    lane_half = [pl.ds(0, 256), pl.ds(256, 256)]
    mine, theirs = pl.multiple_of(core * 256, 256), pl.multiple_of((1 - core) * 256, 256)
    a_init = []
    for h in range(2):
        a_init.append(remote(
            h, go_ref.at[pl.ds(theirs, 256), lane_half[h]],
            ag.at[zh, core * 2 + h, pl.ds(theirs, 256)], c, partner,
        ))
    own_lanes = pl.ds(pl.multiple_of(zl * 128, 128), 128)
    wz = remote(OFF_W, w_ref, wg.at[x, y, :, own_lanes], z_peer, t)
    local = [
        pltpu.make_async_copy(
            go_ref.at[:, lane_half[h]], ag.at[zh, core * 2 + h], loc.at[h]
        )
        for h in range(2)
    ]
    local.append(pltpu.make_async_copy(w_ref, wg.at[x, y, :, own_lanes], loc.at[2]))
    for copy in local:
        copy.start()
    for h in range(2):
        a_init.append(remote(
            2 + h, go_ref.at[pl.ds(mine, 256), lane_half[h]],
            ag.at[zh, core * 2 + h, pl.ds(mine, 256)], c, partner,
        ))

    order = [yo, yp, ym, y]
    duty = pl.ds(mine, 256)
    duty_lo = pl.ds(mine, 128)
    duty_hi = pl.ds(pl.multiple_of(core * 256 + 128, 128), 128)
    piece_own, piece_fwd, piece_par = {}, {}, {}

    def piece_start(k):
        src = ag.at[zh, order[k], duty]
        base = 4 + 8 * k
        piece_own[k] = (
            remote(base, src, src, c, t_right), remote(base + 1, src, src, c, t_left)
        )

    def piece_forward(k):
        base = 4 + 8 * k
        from_left, from_right = piece_own[k]
        yk = order[k]
        from_left.wait_recv()
        lo = ag.at[zm, yk, duty_lo]
        f_r = remote(base + 2, lo, lo, c, t_right)
        full = ag.at[zm, yk, duty]
        p_l = remote(base + 4, full, full, c, partner, ('p', k))
        from_right.wait_recv()
        hi = ag.at[zp, yk, duty_hi]
        f_l = remote(base + 3, hi, hi, c, t_left)
        full = ag.at[zp, yk, duty]
        p_r = remote(base + 5, full, full, c, partner, ('p', k))
        piece_fwd[k] = (f_r, f_l)
        piece_par[k] = [p_l, p_r]
        if k + 2 < 4:
            piece_start(k + 2)

    def piece_pass(k):
        base = 4 + 8 * k
        yk = order[k]
        f_r, f_l = piece_fwd[k]
        f_r.wait_recv()
        lo = ag.at[zo, yk, duty_lo]
        p_a = remote(base + 6, lo, lo, c, partner, ('p', k))
        f_l.wait_recv()
        hi = ag.at[zo, yk, duty_hi]
        p_b = remote(base + 7, hi, hi, c, partner, ('p', k))
        piece_par[k] += [p_a, p_b]

    def piece_wait(k):
        wait_bytes(ag.at[0, pl.ds(0, 2), pl.ds(0, 384)], recv_sem(('p', k)))

    loads[3].wait()
    loads[4].wait()
    rate_rows = jnp.exp(rate2[...])
    decay_rows = jnp.exp(-rate_rows)
    amp_rows = gain2[...] * jnp.sqrt(2.0 * rate_rows)
    for m in range(MODES):
        rate3[m] = rate_rows[m:m + 1, :]
        a8[m] = jnp.broadcast_to(decay_rows[m:m + 1, :], (SUB, CH))
        amp8[m] = jnp.broadcast_to(amp_rows[m:m + 1, :], (SUB, CH))

    def spread(dst, natural):
        mixed = jnp.dot(perm[...], natural, preferred_element_type=F32)
        for grp in range(GROUPS):
            dst[grp] = mixed[:, grp * LANES:(grp + 1) * LANES]

    def gather_back():
        mixed = jnp.concatenate([ys[grp] for grp in range(GROUPS)], axis=1).astype(BF16)
        return jnp.dot(perm_t[...], mixed, preferred_element_type=F32)

    w0, w1 = pl.ds(0, W_SPLIT), pl.ds(W_SPLIT, CH - W_SPLIT)
    half0, half1 = W_SPLIT // 2, (CH - W_SPLIT) // 2
    w0a, w0b = pl.ds(0, half0), pl.ds(half0, half0)
    w1a, w1b = pl.ds(W_SPLIT, half1), pl.ds(W_SPLIT + half1, half1)
    wb = OFF_W + 1
    wc = {}

    def w_send(index, ref, ctx, share=None):
        return remote(wb + index, ref, ref, ctx, t, share)

    def w_row(b, xb):
        wc["yr", b] = w_send(4 + 4 * b, wg.at[xb, y, w0], y_right)
        wc["yl", b] = w_send(5 + 4 * b, wg.at[xb, y, w0], y_left)

    def w_row_forward(b, xb):
        wc["yr", b].wait_recv()
        wc["yfr", b] = w_send(6 + 4 * b, wg.at[xb, ym, w0a], y_right, 'w')
        wc["yl", b].wait_recv()
        wc["yfl", b] = w_send(7 + 4 * b, wg.at[xb, yp, w0b], y_left, 'w')

    def w_col(b, yb):
        wc["xr", b] = w_send(24 + 4 * b, wg.at[x, yb, w1], x_right)
        wc["xl", b] = w_send(25 + 4 * b, wg.at[x, yb, w1], x_left)

    def w_col_forward(b, yb):
        wc["xr", b].wait_recv()
        wc["xfr", b] = w_send(26 + 4 * b, wg.at[xm, yb, w1a], x_right, 'w')
        wc["xl", b].wait_recv()
        wc["xfl", b] = w_send(27 + 4 * b, wg.at[xp, yb, w1b], x_left, 'w')

    def w_early():
        for n, (rows, ctx) in enumerate(((w0, x_right), (w0, x_left), (w1, y_right), (w1, y_left))):
            wc["early", n] = remote(
                wb + 40 + n, w_ref.at[rows], wg.at[x, y, rows, own_lanes], ctx, t
            )

    def w_first():
        wz.wait_recv()
        peer_lanes = pl.ds(pl.multiple_of((1 - zl) * 128, 128), 128)
        wc["xr"] = w_send(0, wg.at[x, y, w0, peer_lanes], x_right)
        wc["xl"] = w_send(1, wg.at[x, y, w0, peer_lanes], x_left)
        wc["1r"] = w_send(20, wg.at[x, y, w1, peer_lanes], y_right)
        wc["1l"] = w_send(21, wg.at[x, y, w1, peer_lanes], y_left)
        w_row(0, x)
        w_col(0, y)

    def w_second():
        for n in range(4):
            wc["early", n].wait_recv()
        wc["xr"].wait_recv()
        wc["xfr"] = w_send(2, wg.at[xm, y, w0a], x_right)
        wc["xl"].wait_recv()
        wc["xfl"] = w_send(3, wg.at[xp, y, w0b], x_left)
        wc["1r"].wait_recv()
        wc["1fr"] = w_send(22, wg.at[x, ym, w1a], y_right)
        wc["1l"].wait_recv()
        wc["1fl"] = w_send(23, wg.at[x, yp, w1b], y_left)
        w_row(1, xm)
        w_col(1, ym)
        w_row(2, xp)
        w_col(2, yp)

    def w_third():
        wc["1fr"].wait_recv()
        wc["1fl"].wait_recv()
        wc["xfr"].wait_recv()
        wc["xfl"].wait_recv()
        w_row(3, xo)
        w_col(3, yo)
        w_row_forward(0, x)
        w_col_forward(0, y)

    def w_fourth():
        w_row_forward(1, xm)
        w_col_forward(1, ym)
        w_row_forward(2, xp)
        w_col_forward(2, yp)

    def w_fifth():
        w_row_forward(3, xo)
        w_col_forward(3, yo)

    def w_end():
        wait_bytes(wg.at[0], recv_sem('w'))

    w_early()

    def lane_at(grp):
        return pl.ds(pl.multiple_of(grp * LANES, LANES), LANES)

    def step_rows(j):
        return pl.ds(pl.multiple_of(j * SUB, SUB), SUB)

    def rates_at(grp):
        return rate3[:, :, lane_at(grp)]

    UNROLL = 4

    def forward_group(grp):
        decay = a8[:, :, lane_at(grp)]

        def step(i, carry):
            state, timed = carry
            for u in range(UNROLL):
                decayed = decay * state
                timed = decay * timed + decayed
                state = decayed + xs[grp, step_rows(i * UNROLL + u)][None]
            return (state, timed)

        zero = jnp.zeros((MODES, SUB, LANES), F32)
        state, timed = lax.fori_loop(0, STEPS // UNROLL, step, (zero, zero))
        rates = rates_at(grp)
        for power in (1, 2, 4):
            factor = jnp.exp(-rates * float(STEPS * power))
            before = shift_sub(state, power)
            timed = timed + factor * (shift_sub(timed, power) + float(STEPS * power) * before)
            state = state + factor * before
        hfs[:, :, lane_at(grp)] = shift_sub(state, 1)
        hft[:, :, lane_at(grp)] = shift_sub(timed, 1)
        scr8[grp, 0:MODES] = state
        scr8[grp, MODES:2 * MODES] = timed

    def backward_group(grp):
        decay = a8[:, :, lane_at(grp)]

        def step(i, state):
            for u in range(UNROLL):
                j = STEPS - 1 - (i * UNROLL + u)
                state = decay * state + gs[grp, step_rows(j)][None]
            return state

        state = lax.fori_loop(0, STEPS // UNROLL, step, jnp.zeros((MODES, SUB, LANES), F32))
        rates = rates_at(grp)
        for power in (1, 2, 4):
            factor = jnp.exp(-rates * float(STEPS * power))
            state = state + factor * shift_sub(state, -power)
        hbwd[:, :, lane_at(grp)] = shift_sub(state, -1)
        scr8[grp, 0:MODES] = state

    def edge_rows(count, edge):
        for grp in range(GROUPS):
            for m in range(count):
                st2[m:m + 1, grp * LANES:(grp + 1) * LANES] = scr8[grp, m, edge:edge + 1, :]

    def scan_forward(grp):
        decay = a8[:, :, lane_at(grp)]
        amp = amp8[:, :, lane_at(grp)]

        def step(i, carry):
            state, timed = carry
            for u in range(UNROLL):
                j = i * UNROLL + u
                decayed = decay * state
                timed = decay * timed + decayed
                state = decayed + xs[grp, step_rows(j)][None]
                tkeep[grp, j] = timed
                ys[grp, step_rows(j)] = jnp.sum(amp * state, axis=0)
            return (state, timed)

        lax.fori_loop(
            0, STEPS // UNROLL, step, (hfs[:, :, lane_at(grp)], hft[:, :, lane_at(grp)])
        )

    def scan_backward(grp):
        decay = a8[:, :, lane_at(grp)]
        amp = amp8[:, :, lane_at(grp)]

        def step(i, state):
            for u in range(UNROLL):
                j = STEPS - 1 - (i * UNROLL + u)
                state = decay * state + gs[grp, step_rows(j)][None]
                ys[grp, step_rows(j)] = jnp.sum(amp * state, axis=0)
            return state

        lax.fori_loop(0, STEPS // UNROLL, step, hbwd[:, :, lane_at(grp)])

    def level_copy(src, dst, send, recv, ctx):
        return pltpu.make_async_remote_copy(
            src_ref=src, dst_ref=dst, send_sem=send, recv_sem=recv,
            device_id=(ctx, t), device_id_type=MESH,
        )

    def row_copies(src, row, send, recv):
        return [
            level_copy(src, row.at[y], send.at[d], recv.at[y], ctx_of(x, (y + d) % 4, zl))
            for d in range(1, 4)
        ]

    def row_wait(src, row, send, recv):
        for d in range(1, 4):
            other = (y + d) % 4
            level_copy(src, row.at[other], send.at[d], recv.at[other], y_right).wait_recv()

    def col_copy(src, col, send, recv, xx, index):
        return level_copy(
            src, col.at[index], send.at[4 + xx], recv.at[4 + index], ctx_of(xx, y, zl)
        )

    def pair_copy(n, src, dst):
        return pltpu.make_async_remote_copy(
            src_ref=src, dst_ref=dst, send_sem=pair_s.at[n], recv_sem=pair_r.at[n],
            device_id=(z_peer, t), device_id_type=MESH,
        )

    chunk = float(ROWS)
    one_decay = jnp.exp(-rate_rows * chunk)
    two_decay = jnp.exp(-rate_rows * (2.0 * chunk))
    odd = zl == 1
    row_decay = jnp.exp(-rate_rows * (8.0 * chunk))
    zero_rows = jnp.zeros((MODES, CH), F32)

    for copy in local:
        copy.wait()
    for copy in a_init:
        copy.wait_recv()
    piece_start(0)
    row_id = lax.broadcasted_iota(jnp.int32, (ROWS, ROWS), 0)
    col_id = lax.broadcasted_iota(jnp.int32, (ROWS, ROWS), 1)
    perm[...] = jnp.where(col_id == STEPS * (row_id % SUB) + row_id // SUB, 1.0, 0.0).astype(BF16)
    perm_t[...] = jnp.where(row_id == STEPS * (col_id % SUB) + col_id // SUB, 1.0, 0.0).astype(BF16)

    loads[0].wait()
    loads[1].wait()
    signal = (k_ref[...].astype(F32) * v_ref[...].astype(F32)).astype(BF16)
    spread(xs, signal)
    run(0, GROUPS, forward_group)
    edge_rows(2 * MODES, SUB - 1)
    ebuf[...] = st2[...].astype(BF16)
    e_pair = pair_copy(0, ebuf, epeer)
    e_pair.start()
    w_first()
    piece_start(1)
    e_pair.wait_recv()
    peer = epeer[...].astype(F32)
    own = st2[...]
    first = jnp.where(odd, peer, own)
    second = jnp.where(odd, own, peer)
    first_s, first_t = first[:MODES], first[MODES:]
    esend[0:MODES] = (second[:MODES] + one_decay * first_s).astype(BF16)
    esend[MODES:] = (second[MODES:] + one_decay * (first_t + chunk * first_s)).astype(BF16)
    e_row = row_copies(esend, erow, e_s, e_r)
    for copy in e_row:
        copy.start()
    erow[y] = esend[...]
    w_second()
    piece_forward(0)

    row_wait(esend, erow, e_s, e_r)
    head_s, head_t, row_s, row_t = (zero_rows,) * 4
    for yy in range(4):
        rows = erow[yy].astype(F32)
        ahead = yy < y
        head_t = jnp.where(
            ahead, two_decay * (head_t + 2.0 * chunk * head_s) + rows[MODES:], head_t
        )
        head_s = jnp.where(ahead, two_decay * head_s + rows[:MODES], head_s)
        row_t = two_decay * (row_t + 2.0 * chunk * row_s) + rows[MODES:]
        row_s = two_decay * row_s + rows[:MODES]
    eout[0:MODES] = row_s.astype(BF16)
    eout[MODES:] = row_t.astype(BF16)
    run(x + 1, 4, lambda xx: col_copy(eout, ecol, e_s, e_r, xx, x).start())
    piece_forward(1)
    w_third()

    run(0, x, lambda xx: col_copy(eout, ecol, e_s, e_r, xx, xx).wait_recv())

    def join_forward(j, carry):
        far_s, far_t = carry
        rows = ecol[j].astype(F32)
        return (
            row_decay * far_s + rows[:MODES],
            row_decay * (far_t + 8.0 * chunk * far_s) + rows[MODES:],
        )

    far_s, far_t = lax.fori_loop(0, x, join_forward, (zero_rows, zero_rows))
    gap = y.astype(F32) * (2.0 * chunk)
    gap_decay = jnp.exp(-rate_rows * gap)
    head_s = head_s + gap_decay * far_s
    head_t = head_t + gap_decay * (far_t + gap * far_s)
    head_t = jnp.where(odd, peer[MODES:] + one_decay * (head_t + chunk * head_s), head_t)
    head_s = jnp.where(odd, peer[:MODES] + one_decay * head_s, head_s)
    for m in range(MODES):
        hd3[m] = head_s[m:m + 1, :]
        hd3[MODES + m] = head_t[m:m + 1, :]

    def incoming_forward(grp):
        ids = lax.broadcasted_iota(jnp.int32, (MODES, SUB, LANES), 1).astype(F32) * float(STEPS)
        weight = jnp.exp(-rates_at(grp) * ids)
        in_s = hd3[0:MODES, :, lane_at(grp)]
        in_t = hd3[MODES:2 * MODES, :, lane_at(grp)]
        hfs[:, :, lane_at(grp)] += weight * in_s
        hft[:, :, lane_at(grp)] += weight * (in_t + ids * in_s)

    run(0, GROUPS, incoming_forward)
    run(0, GROUPS, scan_forward)
    loads[2].wait()
    cv[...] = gather_back().astype(BF16)
    gated = (q_ref[...].astype(F32) * cv[...].astype(F32)).astype(BF16).astype(F32)
    gt[...] = jnp.transpose(gated).astype(BF16)

    rings = {}

    def add_into(ref, extra):
        ref[...] = (ref[...].astype(F32) + extra.astype(F32)).astype(BF16)
        return ref

    def part_a(part):
        return pl.ds(part * 128, 128)

    def part_b(part):
        return pl.ds(256 + part * 128, 128)

    ybase = OFF_O + 24
    bbase = OFF_O + 30
    vbase = OFF_O + 36
    along = {}

    def out_piece(k):
        yk = order[k]

        def block(j):
            op[j, yk] = jnp.dot(gt[...], ag[j, yk], preferred_element_type=F32).astype(BF16)

        run(0, 4, block)

        def unit(target, part):
            return op.at[target, yk, part_a(part)]

        base = OFF_O + 6 * k
        far_r = remote(base, unit(xo, 0), oppx.at[k, 0], x_right, t)
        far_l = remote(base + 1, unit(xo, 1), oppx.at[k, 1], x_left, t)
        rings[k] = [
            unit, far_r, far_l,
            remote(base + 2, unit(xp, 1), finx.at[k, 0, 1], x_right, t, ('x', k)),
            remote(base + 3, unit(xm, 0), finx.at[k, 1, 0], x_left, t, ('x', k)),
        ]

        def whole(part):
            return op.at[:, yk, part_b(part)]

        if k == 0:
            along["far_r"] = remote(bbase, whole(0), oppb.at[0], y_right, t)
            along["far_l"] = remote(bbase + 1, whole(1), oppb.at[1], y_left, t)
        elif k == 1:
            along["r1"] = remote(bbase + 2, whole(1), finb.at[0, 1], y_right, t, 'b')
        elif k == 2:
            along["l0"] = remote(bbase + 4, whole(0), finb.at[1, 0], y_left, t, 'b')

    def along_right():
        along["far_r"].wait_recv()
        ref = add_into(op.at[:, order[1], part_b(0)], oppb[0])
        along["r0"] = remote(bbase + 3, ref, finb.at[0, 0], y_right, t, 'b')

    def along_left():
        along["far_l"].wait_recv()
        ref = add_into(op.at[:, order[2], part_b(1)], oppb[1])
        along["l1"] = remote(bbase + 5, ref, finb.at[1, 1], y_left, t, 'b')

    def along_own():
        wait_bytes(finb, recv_sem('b'))
        for part in range(2):
            rows = slice(part * 128, (part + 1) * 128)
            vcol[:, rows] = (
                op[:, y, part_b(part)].astype(F32) + finb[0, part].astype(F32)
                + finb[1, part].astype(F32)
            ).astype(BF16)

        def unit(target, part):
            return vcol.at[target, part_a(part)]

        along["ring"] = [
            unit,
            remote(vbase, unit(xo, 0), oppv.at[0], x_right, t),
            remote(vbase + 1, unit(xo, 1), oppv.at[1], x_left, t),
            remote(vbase + 2, unit(xp, 1), finv.at[0, 1], x_right, t, 'v'),
            remote(vbase + 3, unit(xm, 0), finv.at[1, 0], x_left, t, 'v'),
        ]

    def along_add():
        unit, far_r, far_l = along["ring"][:3]
        far_r.wait_recv()
        ref = add_into(unit(xp, 0), oppv[0])
        along["ring"].append(remote(vbase + 4, ref, finv.at[0, 0], x_right, t, 'v'))
        far_l.wait_recv()
        ref = add_into(unit(xm, 1), oppv[1])
        along["ring"].append(remote(vbase + 5, ref, finv.at[1, 1], x_left, t, 'v'))

    def along_last():
        wait_bytes(finv, recv_sem('v'))
        for part in range(2):
            rsum[256 + part * 128:256 + (part + 1) * 128] = (
                vcol[x, part * 128:(part + 1) * 128].astype(F32) + finv[0, part].astype(F32)
                + finv[1, part].astype(F32)
            )

    def out_add(k):
        unit, far_r, far_l = rings[k][:3]
        base = OFF_O + 6 * k
        far_r.wait_recv()
        ref = add_into(unit(xp, 0), oppx[k, 0])
        rings[k].append(remote(base + 4, ref, finx.at[k, 0, 0], x_right, t, ('x', k)))
        far_l.wait_recv()
        ref = add_into(unit(xm, 1), oppx[k, 1])
        rings[k].append(remote(base + 5, ref, finx.at[k, 1, 1], x_left, t, ('x', k)))

    def out_sum(k):
        unit = rings[k][0]
        wait_bytes(finx.at[k], recv_sem(('x', k)))
        return [
            unit(x, part)[...].astype(F32) + finx[k, 0, part].astype(F32)
            + finx[k, 1, part].astype(F32)
            for part in range(2)
        ]

    second_ring = {}

    def out_first():
        parts = out_sum(0)
        for part in range(2):
            vsum[0, part] = parts[part].astype(BF16)
        second_ring["far_r"] = remote(ybase, vsum.at[0, 0], oppy.at[0], y_right, t)
        second_ring["far_l"] = remote(ybase + 1, vsum.at[0, 1], oppy.at[1], y_left, t)

    def out_second():
        parts = out_sum(1)
        vsum[1, 1] = parts[1].astype(BF16)
        second_ring["r1"] = remote(ybase + 2, vsum.at[1, 1], finy.at[0, 1], y_right, t, 'y')
        second_ring["far_r"].wait_recv()
        vsum[1, 0] = (parts[0] + oppy[0].astype(F32)).astype(BF16)
        second_ring["r0"] = remote(ybase + 3, vsum.at[1, 0], finy.at[0, 0], y_right, t, 'y')

    def out_third():
        parts = out_sum(2)
        vsum[2, 0] = parts[0].astype(BF16)
        second_ring["l0"] = remote(ybase + 4, vsum.at[2, 0], finy.at[1, 0], y_left, t, 'y')
        second_ring["far_l"].wait_recv()
        vsum[2, 1] = (parts[1] + oppy[1].astype(F32)).astype(BF16)
        second_ring["l1"] = remote(ybase + 5, vsum.at[2, 1], finy.at[1, 1], y_left, t, 'y')

    def out_last():
        parts = out_sum(3)
        wait_bytes(finy, recv_sem('y'))
        for part in range(2):
            rsum[part * 128:(part + 1) * 128] = (
                parts[part] + finy[0, part].astype(F32) + finy[1, part].astype(F32)
            )

    dims = (((1,), (1,)), ((), ()))

    def gate_piece(k):
        yk = order[k]

        def block(j):
            gate[...] += lax.dot_general(
                ag[j, yk], wg[j, yk], dims, preferred_element_type=F32
            )

        run(0, 4, block)

    w_fourth()
    piece_pass(0)
    w_fifth()
    piece_forward(2)
    piece_wait(0)
    out_piece(0)
    piece_pass(1)
    piece_wait(1)
    out_piece(1)
    w_end()
    gate[...] = jnp.zeros_like(gate)
    gate_piece(0)
    piece_forward(3)
    piece_pass(2)
    gate_piece(1)
    out_add(0)
    piece_wait(2)
    out_piece(2)
    along_right()
    along_left()
    gate_piece(2)
    piece_pass(3)
    out_add(1)
    out_first()
    piece_wait(3)
    gate_piece(3)
    out_add(2)

    conv_grad = (gate[...] * q_ref[...].astype(F32)).astype(BF16)
    spread(gs, conv_grad)
    run(0, GROUPS, backward_group)
    edge_rows(MODES, 0)
    qbuf[...] = st2[0:MODES].astype(BF16)
    q_pair = pair_copy(1, qbuf, qpeer)
    q_pair.start()

    def gain_scan(grp):
        for part in range(2):
            mode = pl.ds(part * 8, 8)
            decay = a8[mode, :, lane_at(grp)]

            def step(i, carry):
                state, gain_sum, rate_sum = carry
                for u in range(UNROLL):
                    j = i * UNROLL + u
                    grad = gs[grp, step_rows(j)][None]
                    state = decay * state + xs[grp, step_rows(j)][None]
                    gain_sum = gain_sum + grad * state
                    rate_sum = rate_sum + grad * tkeep[grp, j, mode]
                return (state, gain_sum, rate_sum)

            zero = jnp.zeros((8, SUB, LANES), F32)
            _, gain_sum, rate_sum = lax.fori_loop(
                0, STEPS // UNROLL, step, (hfs[mode, :, lane_at(grp)], zero, zero)
            )
            scr8[grp, mode] = gain_sum
            scr8[grp, pl.ds(MODES + part * 8, 8)] = rate_sum

    def y_copy(d, index):
        other = (c + d) % NCTX
        return pltpu.make_async_remote_copy(
            src_ref=yz.at[other], dst_ref=yz_in.at[index], send_sem=y_s.at[0],
            recv_sem=y_r.at[0], device_id=(other, t), device_id_type=MESH,
        )

    def o_copy(d, index):
        other = (c + d) % NCTX
        return pltpu.make_async_remote_copy(
            src_ref=yz_all.at[c], dst_ref=yz_all.at[index], send_sem=o_s.at[0],
            recv_sem=o_r.at[0], device_id=(other, t), device_id_type=MESH,
        )

    def incoming_backward(grp):
        ids = lax.broadcasted_iota(jnp.int32, (MODES, SUB, LANES), 1).astype(F32)
        weight = jnp.exp(-rates_at(grp) * (((SUB - 1.0) - ids) * float(STEPS)))
        hbwd[:, :, lane_at(grp)] += weight * hd3[0:MODES, :, lane_at(grp)]

    run(0, 1, gain_scan)
    q_pair.wait_recv()
    peer_q = qpeer[...].astype(F32)
    own_q = st2[0:MODES]
    first_q = jnp.where(odd, peer_q, own_q)
    second_q = jnp.where(odd, own_q, peer_q)
    qsend[...] = (first_q + one_decay * second_q).astype(BF16)
    q_row = row_copies(qsend, qrow, q_s, q_r)
    for copy in q_row:
        copy.start()
    qrow[y] = qsend[...]

    gq_buf[...] = (gate[...] * cv[...].astype(F32)).astype(BF16)
    stores = [pltpu.make_async_copy(gq_buf, gq_out, io.at[5])]
    stores[0].start()
    out_piece(3)
    run(1, GROUPS, gain_scan)
    row_wait(qsend, qrow, q_s, q_r)
    tail, row_q = zero_rows, zero_rows
    for yy in range(3, -1, -1):
        rows = qrow[yy].astype(F32)
        tail = jnp.where(yy > y, two_decay * tail + rows, tail)
        row_q = two_decay * row_q + rows
    qout[...] = row_q.astype(BF16)
    run(0, x, lambda xx: col_copy(qout, qcol, q_s, q_r, xx, x).start())
    for grp in range(GROUPS):
        yz[:, grp] = jnp.sum(scr8[grp], axis=1)
    run(1, NCTX, lambda d: y_copy(d, c).start())
    out_second()
    along_own()
    out_add(3)
    out_third()

    run(x + 1, 4, lambda xx: col_copy(qout, qcol, q_s, q_r, xx, xx).wait_recv())
    far_q = lax.fori_loop(
        0, 3 - x, lambda j, h: row_decay * h + qcol[3 - j].astype(F32), zero_rows
    )
    tail = tail + jnp.exp(-rate_rows * ((3 - y).astype(F32) * (2.0 * chunk))) * far_q
    tail = jnp.where(odd, tail, peer_q + one_decay * tail)
    for m in range(MODES):
        hd3[m] = tail[m:m + 1, :]
    run(0, GROUPS, incoming_backward)
    run(0, 2, scan_backward)
    along_add()
    run(2, GROUPS, scan_backward)
    ig_buf[...] = gather_back().astype(BF16)
    stores.append(pltpu.make_async_copy(ig_buf, ig_out, io.at[6]))
    stores[1].start()
    z_copies = []

    def z_start(half):
        rows = slice(half * 256, (half + 1) * 256)
        rsend[rows] = rsum[
            rows, pl.ds(pl.multiple_of((1 - zl) * 128, 128), 128)
        ].astype(BF16)
        z_copies.append(remote(
            OFF_O + 42 + half, rsend.at[pl.ds(half * 256, 256)],
            zin.at[pl.ds(half * 256, 256)], z_peer, t,
        ))

    wait_bytes(yz_in.at[pl.ds(0, NCTX - 1)], y_r.at[0])
    yz_in[c] = yz[c]
    yz_all[c] = jnp.sum(yz_in[...], axis=0)
    run(1, NCTX, lambda d: o_copy(d, c).start())
    out_last()
    z_start(0)
    along_last()
    z_start(1)

    def flush_sends():
        for copy in e_row + q_row:
            copy.wait_send()
        run(x + 1, 4, lambda xx: col_copy(eout, ecol, e_s, e_r, xx, x).wait_send())
        run(0, x, lambda xx: col_copy(qout, qcol, q_s, q_r, xx, x).wait_send())
        wait_bytes(yz.at[pl.ds(0, NCTX - 1)], y_s.at[0])
        e_pair.wait_send()
        q_pair.wait_send()
        for n, (ref, rows) in enumerate(zip((ag, wg, op), SENT_ROWS)):
            wait_bytes(ref.at[:, :, pl.ds(0, rows)], ring_s.at[n])

    flush_sends()
    assert len(ids) == N_RECV
    for copy in z_copies:
        copy.wait_recv()
    ow_buf[...] = (rsum[:, own_lanes] + zin[...].astype(F32)) * NORM
    stores.append(pltpu.make_async_copy(ow_buf, ow_out, io.at[7]))
    stores[2].start()

    wait_bytes(yz_all.at[pl.ds(0, NCTX - 1)], o_r.at[0])
    yz_out[...] = yz_all[...]
    wait_bytes(yz_all.at[pl.ds(0, NCTX - 1)], o_s.at[0])
    for copy in stores:
        copy.wait()


def finish(
    gq_in, ow_in, ig_ref, k_ref, v_ref, sums, gain2, rate2,
    gq_out, gk_out, gv_out, gain_out, rate_out, ow_out,
):
    gq_out[...] = gq_in[...]
    ow_out[...] = ow_in[...]
    input_grad = ig_ref[...].astype(F32)
    gk_out[...] = (input_grad * v_ref[...].astype(F32)).astype(BF16)
    gv_out[...] = (input_grad * k_ref[...].astype(F32)).astype(BF16)
    rate_rows = jnp.exp(rate2[...])
    scale = NORM * jnp.sqrt(2.0 * rate_rows)
    gain_sum = jnp.concatenate([sums[0:MODES, grp] for grp in range(GROUPS)], axis=1)
    rate_sum = jnp.concatenate([sums[MODES:2 * MODES, grp] for grp in range(GROUPS)], axis=1)
    gain_out[...] = scale * gain_sum
    rate_out[...] = scale * gain2[...] * (0.5 * gain_sum - rate_rows * rate_sum)


def on_device(query_proj, key_proj, value_proj, filter_gains, log_rates, out_weight, grad_out):
    gain2 = filter_gains.T
    rate2 = log_rates.T
    vmem = pl.BlockSpec(memory_space=pltpu.VMEM)
    hbm = pl.BlockSpec(memory_space=pl.ANY)
    shape = jax.ShapeDtypeStruct
    dma = pltpu.SemaphoreType.DMA
    wide = (MODES, SUB, CH)
    gq_raw, input_grad, sums, ow_raw = pl.pallas_call(
        kernel,
        out_shape=(
            shape((ROWS, CH), BF16),
            shape((ROWS, CH), BF16),
            shape((2 * MODES, GROUPS, LANES), F32),
            shape((CH, 128), F32),
        ),
        in_specs=[hbm] * 7,
        out_specs=[hbm, hbm, vmem, hbm],
        scratch_shapes=[
            pltpu.VMEM((ROWS, CH), BF16),
            pltpu.VMEM((ROWS, CH), BF16),
            pltpu.VMEM((ROWS, CH), BF16),
            pltpu.VMEM((MODES, CH), F32),
            pltpu.VMEM((MODES, CH), F32),
            pltpu.VMEM((ROWS, CH), BF16),
            pltpu.VMEM((ROWS, CH), BF16),
            pltpu.VMEM((CH, 128), F32),
            pltpu.VMEM((MODES, 1, CH), F32),
            pltpu.VMEM((GROUPS, STEPS, MODES, SUB, LANES), F32),
            pltpu.VMEM((4, 4, ROWS, 256), BF16),
            pltpu.VMEM((4, 4, CH, 256), BF16),
            pltpu.VMEM((4, 4, CH, 256), BF16),
            pltpu.VMEM((GROUPS, ROWS, LANES), F32),
            pltpu.VMEM((GROUPS, ROWS, LANES), F32),
            pltpu.VMEM((GROUPS, ROWS, LANES), F32),
            pltpu.VMEM((ROWS, ROWS), BF16),
            pltpu.VMEM((ROWS, ROWS), BF16),
            pltpu.VMEM(wide, F32),
            pltpu.VMEM(wide, F32),
            pltpu.VMEM((2 * MODES, CH), BF16),
            pltpu.VMEM((2 * MODES, CH), BF16),
            pltpu.VMEM((2 * MODES, CH), BF16),
            pltpu.VMEM((4, 2 * MODES, CH), BF16),
            pltpu.VMEM((2 * MODES, CH), BF16),
            pltpu.VMEM((4, 2 * MODES, CH), BF16),
            pltpu.VMEM((MODES, CH), BF16),
            pltpu.VMEM((MODES, CH), BF16),
            pltpu.VMEM((MODES, CH), BF16),
            pltpu.VMEM((4, MODES, CH), BF16),
            pltpu.VMEM((MODES, CH), BF16),
            pltpu.VMEM((4, MODES, CH), BF16),
            pltpu.VMEM((2 * MODES, 1, CH), F32),
            pltpu.VMEM((2 * MODES, CH), F32),
            pltpu.VMEM((GROUPS, 2 * MODES, SUB, LANES), F32),
            pltpu.VMEM(wide, F32),
            pltpu.VMEM(wide, F32),
            pltpu.VMEM(wide, F32),
            pltpu.VMEM((ROWS, CH), F32),
            pltpu.VMEM((ROWS, CH), BF16),
            pltpu.VMEM((CH, ROWS), BF16),
            pltpu.VMEM((2 * MODES, GROUPS, LANES), F32),
            pltpu.VMEM((NCTX, GROUPS, LANES), F32),
            pltpu.VMEM((NCTX, GROUPS, LANES), F32),
            pltpu.VMEM((4, 2, 128, 256), BF16),
            pltpu.VMEM((4, 2, 2, 128, 256), BF16),
            pltpu.VMEM((3, 2, 128, 256), BF16),
            pltpu.VMEM((2, 128, 256), BF16),
            pltpu.VMEM((2, 2, 128, 256), BF16),
            pltpu.VMEM((2, 4, 128, 256), BF16),
            pltpu.VMEM((2, 2, 4, 128, 256), BF16),
            pltpu.VMEM((4, 256, 256), BF16),
            pltpu.VMEM((2, 128, 256), BF16),
            pltpu.VMEM((2, 2, 128, 256), BF16),
            pltpu.VMEM((CH, 256), F32),
            pltpu.VMEM((CH, 128), BF16),
            pltpu.VMEM((CH, 128), BF16),
            dma((3,)),
            dma((N_RECV,)),
            dma((8,)),
            dma((8,)),
            dma((8,)),
            dma((8,)),
            dma((1,)),
            dma((1,)),
            dma((1,)),
            dma((1,)),
            dma((2,)),
            dma((2,)),
            dma((3,)),
            dma((8,)),
        ],
        compiler_params=pltpu.CompilerParams(
            collective_id=0, has_side_effects=True, vmem_limit_bytes=56 * 1024 * 1024
        ),
        cost_estimate=pl.CostEstimate(
            flops=5_000_000_000, bytes_accessed=5_000_000, transcendentals=0
        ),
    )(
        query_proj, key_proj, value_proj, gain2, rate2, out_weight, grad_out,
    )
    grad_query, grad_key, grad_value, grad_gains, grad_rates, grad_weight = pl.pallas_call(
        finish,
        out_shape=(
            shape((ROWS, CH), BF16),
            shape((ROWS, CH), BF16),
            shape((ROWS, CH), BF16),
            shape((MODES, CH), F32),
            shape((MODES, CH), F32),
            shape((CH, 128), F32),
        ),
        in_specs=[vmem] * 8,
        out_specs=[vmem] * 6,
        compiler_params=pltpu.CompilerParams(vmem_limit_bytes=60 * 1024 * 1024),
    )(gq_raw, ow_raw, input_grad, key_proj, value_proj, sums, gain2, rate2)
    return (grad_query, grad_key, grad_value, grad_gains.T, grad_rates.T, grad_weight)


def solution(mesh):
    in_specs = (
        P("context", "tensor"),
        P("context", "tensor"),
        P("context", "tensor"),
        P("tensor", None),
        P("tensor", None),
        P("tensor", "context"),
        P("context", "tensor"),
    )
    out_specs = (
        P("context", "tensor"),
        P("context", "tensor"),
        P("context", "tensor"),
        P("tensor", None),
        P("tensor", None),
        P("tensor", "context"),
    )
    return jax.shard_map(
        on_device, mesh=mesh, in_specs=in_specs, out_specs=out_specs, check_vma=False
    )
```
